32 devices in a mesh: dp: 16 (over z, y, x), mp: 2 (over core).
Axes of the slice: x: 2, y: 2, z: 4, core: 2. Of those that a mesh axis runs over, the one named last changes fastest.
Arguments:
- embeddings: bfloat16 [49152, 1024], P('dp', 'mp'), may hold values from -24 to 24
- first_level: int32 [49152], P('dp'), may hold values from 0 to 1023, as said below
- second_level: int32 [1024, 1], P('dp'), may hold values from 0 to 1023
Outputs:
- first_centroids: bfloat16 [1024, 1024], P('dp', 'mp')
- second_centroids: bfloat16 [1024, 1024], P('dp', 'mp')
- scores: float32 [1024, 1024], P('dp', 'mp')
The draws below stay inside these ranges and needn't reach their ends.
Inputs may be any that keep to these rules, and one draw needn't show every extreme that they name: `first_level`: the rows i * 3072 to (i + 1) * 3072 - 1 are assigned only to level-one centroids numbered from ((i + j) mod 16) * 64, that is to the centroids (i + j) * 64 to (i + j + 1) * 64 - 1 taken modulo 1024, for j from 0 to 7; every level-one centroid has at least one row. `second_level`: every level-two centroid is named by at least one level-one centroid.
All inputs are finite; a program needn't handle non-finite values.
Results may differ from the reference program's by a relative error of at most 0.012.
Values may be sent and summed in bfloat16 or wider, within the bound.
No kernel may reach another device: no remote copies, remote signals or barrier semaphores. Data moves between devices by JAX's collectives and lax.ppermute only.
A program may use at most 64 MiB of HBM per device.

```python
import jax
import jax.numpy as jnp
from jax import lax

D = 1024
CENT_DEV = 64
BAND = 8
K2 = 1024
R_DEV = 3072
K1 = 1024
ROWS = 49152
N_DP = 16


def draw_first_level(key, part):
    devices = ROWS // R_DEV
    key_offset, key_local, key_order = jax.random.split(jax.random.fold_in(key, 11), 3)
    offsets = jax.random.randint(key_offset, (devices, R_DEV), 0, BAND)
    locals_drawn = jax.random.randint(key_local, (devices, R_DEV), 0, CENT_DEV)
    positions = jnp.arange(R_DEV, dtype=jnp.int32)[None, :]
    covering = positions < CENT_DEV
    offsets = jnp.where(covering, positions % BAND, offsets)
    locals_drawn = jnp.where(covering, positions % CENT_DEV, locals_drawn)
    orders = jax.vmap(lambda single: jax.random.permutation(single, R_DEV))(jax.random.split(key_order, devices))
    offsets = jnp.take_along_axis(offsets, orders, axis=1)
    locals_drawn = jnp.take_along_axis(locals_drawn, orders, axis=1)
    owners = (jnp.arange(devices, dtype=jnp.int32)[:, None] + offsets) % devices
    return (owners * CENT_DEV + locals_drawn).reshape(ROWS).astype(jnp.int32)


def block_scale(key, dims, cuts, least, high):
    factor_of = 1.0
    for dim, parts in cuts:
        heights = jax.random.uniform(jax.random.fold_in(jax.random.fold_in(key, 6), dim), (parts,), jnp.float32, least / len(cuts), high / len(cuts))
        factor_of = factor_of * jnp.repeat(jnp.exp(heights), dims[dim] // parts).reshape((-1,) + (1,) * (len(dims) - 1 - dim))
    return factor_of


def picks_of(key, rows, count, top, lift):
    order = jax.random.permutation(jax.random.fold_in(key, 1), count)
    boost = order
    for power in range(3):
        boost = boost * boost // count
    boost = boost * lift // count
    chance = jax.random.randint(jax.random.fold_in(key, 2), (rows, count), 0, 4096) + boost
    holders = jax.random.permutation(jax.random.fold_in(key, 3), rows)[jnp.arange(count) % rows]
    chance = jnp.where(jnp.arange(rows)[:, None] == holders[None, :], 1 << 14, chance)
    score = chance * count + jnp.arange(count)
    return lax.top_k(score.astype(jnp.int32), top)[1].astype(jnp.int32)


def bell_draw(stream_key, extent, deviation, limit, pieces=(), kind=jnp.bfloat16):
    values = deviation * jax.random.normal(stream_key, extent, jnp.float32)
    if pieces:
        values = values * block_scale(stream_key, extent, pieces, -0.22, 0.18)
    return jnp.clip(values, -limit, limit).astype(kind)


def setup_inputs(seed: int = 0) -> dict:
    key_of = jax.random.split(jax.random.key(seed), 4)
    embeddings = bell_draw(key_of[0], (ROWS, D), 4.0, 24.0, ((0, 16), (1, 2)))
    first_level = draw_first_level(jax.random.fold_in(key_of[3], 71), 0)
    second_level = picks_of(key_of[2], K1, K2, 1, 8)
    return {"embeddings": embeddings, "first_level": first_level, "second_level": second_level}


def reference(embeddings, first_level, second_level):
    clusters = CENT_DEV * N_DP
    width = embeddings.shape[1]

    def accumulate(running, pair):
        rows_block, ids_block = pair
        totals = running[0] + jax.ops.segment_sum(rows_block.astype(jnp.float32), ids_block, num_segments=clusters)
        tallies = running[1] + jax.ops.segment_sum(jnp.ones(ids_block.shape, jnp.float32), ids_block, num_segments=clusters)
        return (totals, tallies), None

    start_state = (jnp.zeros((clusters, width), jnp.float32), jnp.zeros((clusters,), jnp.float32))
    (first_sums, first_counts), unused = lax.scan(
        accumulate, start_state,
        (embeddings.reshape(N_DP, R_DEV, width), first_level.reshape(N_DP, R_DEV)))
    first_centroids = (first_sums / first_counts[:, None]).astype(jnp.bfloat16)
    group_ids = second_level[:, 0]
    second_sums = jax.ops.segment_sum(first_centroids.astype(jnp.float32), group_ids, num_segments=K2)
    second_counts = jax.ops.segment_sum(jnp.ones(group_ids.shape, jnp.float32), group_ids, num_segments=K2)
    second_centroids = (second_sums / second_counts[:, None]).astype(jnp.bfloat16)
    values = second_centroids.astype(jnp.float32)
    products = jnp.dot(first_centroids, second_centroids.T, preferred_element_type=jnp.float32)
    scores = products - 0.5 * jnp.sum(values * values, axis=1)[None, :]
    return first_centroids, second_centroids, scores
```

```python
import functools

import jax
import jax.numpy as jnp
from jax import lax
from jax.experimental import pallas as pl
from jax.experimental.pallas import tpu as pltpu
from jax.sharding import PartitionSpec as P

BAND = 8
K2 = 1024
GROUP = 4
META = 16
BASE = 256
LANES = 128
BF16 = jnp.bfloat16
F32 = jnp.float32


def whole():
    return pl.BlockSpec(memory_space=pltpu.VMEM)


def exchanged(value, pairs):
    return lax.ppermute(value, ("dp", "mp"), pairs)


def iota(shape, dim):
    return lax.broadcasted_iota(jnp.int32, shape, dim)


def split_digits(row):
    high = jnp.floor(row * (1.0 / BASE))
    return high, row - high * BASE


def as_column(row, cent):
    hit = iota((cent, LANES), 0) == iota((cent, LANES), 1)
    return jnp.sum(jnp.where(hit, row, 0.0), axis=1, keepdims=True)


def as_row(column):
    rows = column.shape[0]
    hit = iota((rows, LANES), 0) == iota((rows, LANES), 1)
    return jnp.sum(jnp.where(hit, column, 0.0), axis=0, keepdims=True)


def sum_kernel(devices, cent, ids_ref, rows_ref, group_ref, own_ref, own_meta_ref, *rest):
    sends, (totals, tallies) = rest[:-2], rest[-2:]
    step = pl.program_id(0)
    block = ids_ref.shape[-1]
    position = lax.axis_index("dp")
    mate = position % GROUP
    offset = ids_ref[0] - position * cent
    offset = jnp.where(offset < 0, offset + devices * cent, offset)
    ahead = offset // cent + mate
    partner = (ahead % GROUP) ^ mate
    slot = jnp.where(ahead // GROUP == 1, 1, 0)
    label = partner * (2 * cent) + slot * cent + offset % cent
    labels = 2 * GROUP * cent
    hit = iota((labels, block), 0) == label
    one_hot = jnp.where(hit, 1.0, 0.0).astype(BF16)
    part = lax.dot_general(
        one_hot, rows_ref[...], (((1,), (0,)), ((), ())), preferred_element_type=F32
    )
    count = one_hot[:, :LANES]
    for start in range(LANES, block, LANES):
        count = count + one_hot[:, start : start + LANES]

    @pl.when(step == 0)
    def _():
        totals[...] = part
        tallies[...] = count.astype(F32)

    @pl.when(step > 0)
    def _():
        totals[...] += part
        tallies[...] += count.astype(F32)

    @pl.when(step == pl.num_programs(0) - 1)
    def _():
        ids = as_row(group_ref[...].astype(F32))
        id_high, id_low = split_digits(ids)
        ones = jnp.ones((8, LANES), F32)
        counts = lax.dot_general(
            ones.astype(BF16),
            tallies[...].astype(BF16),
            (((1,), (1,)), ((), ())),
            preferred_element_type=F32,
        )
        pair = 2 * cent
        own_ref[...] = totals[:pair]
        for index in range(GROUP):
            count_row = counts[:1, index * pair : (index + 1) * pair]
            high, low = split_digits(count_row)
            meta = jnp.concatenate(
                [high, low, id_high, id_low, jnp.zeros((META - 4, LANES), F32)], axis=0
            )
            if index == 0:
                own_meta_ref[...] = meta
            else:
                sends[index - 1][:pair] = totals[index * pair : (index + 1) * pair].astype(BF16)
                sends[index - 1][pair:, :LANES] = meta.astype(BF16)
                sends[index - 1][pair:, LANES:] = jnp.zeros(
                    (META, sends[index - 1].shape[1] - LANES), BF16
                )


def band_sums(devices, cent, ids, rows, group):
    count, width = rows.shape
    block = min(1024, count)
    steps = count // block
    pair = 2 * cent
    send = jax.ShapeDtypeStruct((pair + META, width), BF16)
    fixed = lambda step: (0, 0)
    return pl.pallas_call(
        functools.partial(sum_kernel, devices, cent),
        grid=(steps,),
        in_specs=[
            pl.BlockSpec((1, 1, block), lambda step: (step, 0, 0)),
            pl.BlockSpec((block, width), lambda step: (step, 0)),
            pl.BlockSpec(group.shape, fixed),
        ],
        out_specs=[
            pl.BlockSpec((pair, width), fixed),
            pl.BlockSpec((META, LANES), fixed),
        ]
        + [pl.BlockSpec((pair + META, width), fixed)] * (GROUP - 1),
        out_shape=[
            jax.ShapeDtypeStruct((pair, width), F32),
            jax.ShapeDtypeStruct((META, LANES), F32),
        ]
        + [send] * (GROUP - 1),
        scratch_shapes=[
            pltpu.VMEM((GROUP * pair, width), F32),
            pltpu.VMEM((GROUP * pair, LANES), F32),
        ],
        compiler_params=pltpu.CompilerParams(vmem_limit_bytes=32 * 2**20),
    )(ids.reshape(steps, 1, block), rows, group)


def group_kernel(cent, own, own_meta, one, two, three, base_ref, base_meta_ref, next_ref, far_ref):
    mate = lax.axis_index("dp") % GROUP
    pair = 2 * cent
    lane = iota((1, LANES), 1)
    near = own[:cent]
    middle = own[cent:]
    far = jnp.zeros_like(near)
    counts = own_meta[0:1] * BASE + own_meta[1:2]
    far_counts = jnp.zeros_like(counts)
    for index, got in ((1, one), (2, two), (3, three)):
        before = (mate ^ index) < mate
        first = got[:cent].astype(F32)
        near = near + jnp.where(before, first, 0.0)
        far = far + jnp.where(before, 0.0, first)
        middle = middle + got[cent:pair].astype(F32)
        meta = got[pair:, :LANES].astype(F32)
        row = meta[0:1] * BASE + meta[1:2]
        mask = (lane >= cent) | before
        counts = counts + jnp.where(mask, row, 0.0)
        far_counts = far_counts + jnp.where(mask, 0.0, row)
        base_meta_ref[2 + 2 * index : 4 + 2 * index] = meta[2:4]
    base_ref[...] = near
    base_meta_ref[0:1] = counts
    base_meta_ref[1:2] = jnp.zeros_like(counts)
    base_meta_ref[2:4] = own_meta[2:4]
    base_meta_ref[10:] = jnp.zeros((META - 10, LANES), F32)
    for send, sums, row in ((next_ref, middle, counts), (far_ref, far, far_counts)):
        high, low = split_digits(row)
        meta = jnp.concatenate([high, low, jnp.zeros((META - 2, LANES), F32)], axis=0)
        send[:cent] = sums.astype(BF16)
        send[cent:, :LANES] = meta.astype(BF16)
        send[cent:, LANES:] = jnp.zeros((META, send.shape[1] - LANES), BF16)


def group_sums(cent, own, own_meta, got):
    width = own.shape[1]
    send = jax.ShapeDtypeStruct((cent + META, width), BF16)
    return pl.pallas_call(
        functools.partial(group_kernel, cent),
        in_specs=[whole()] * 5,
        out_specs=[whole()] * 4,
        out_shape=[
            jax.ShapeDtypeStruct((cent, width), F32),
            jax.ShapeDtypeStruct((META, LANES), F32),
            send,
            send,
        ],
    )(own, own_meta, *got)


def mean_kernel(cent, base, base_meta, one, two, mean_ref, send_ref):
    sums = base[...] + one[:cent].astype(F32) + two[:cent].astype(F32)
    first = one[cent:, :LANES].astype(F32)
    second = two[cent:, :LANES].astype(F32)
    middle = first[0:1] * BASE + first[1:2]
    row = base_meta[0:1] + pltpu.roll(middle, LANES - cent, 1) + second[0:1] * BASE + second[1:2]
    mean = (sums / as_column(row, cent)).astype(BF16)
    mean_ref[...] = mean
    send_ref[:cent] = mean
    send_ref[cent:, :LANES] = base_meta[...].astype(BF16)
    send_ref[cent:, LANES:] = jnp.zeros((META, mean.shape[1] - LANES), BF16)


def means(cent, base, base_meta, got):
    width = base.shape[1]
    return pl.pallas_call(
        functools.partial(mean_kernel, cent),
        in_specs=[whole()] * 4,
        out_specs=[whole()] * 2,
        out_shape=[
            jax.ShapeDtypeStruct((cent, width), BF16),
            jax.ShapeDtypeStruct((cent + META, width), BF16),
        ],
    )(base, base_meta, *got)


def line_kernel(cent, *refs):
    blocks, (line_ref, ids_ref) = refs[:-2], refs[-2:]
    lane = iota((1, LANES), 1)
    for index, block in enumerate(blocks):
        line_ref[index * cent : (index + 1) * cent] = block[:cent]
    metas = [block[cent:, :LANES].astype(F32) for block in blocks]
    for index in range(GROUP):
        at = 2 + 2 * index
        rows = [meta[at : at + 1] * BASE + meta[at + 1 : at + 2] for meta in metas]
        joined = []
        for left, right in zip(rows[0::2], rows[1::2]):
            joined.append(jnp.where(lane < cent, left, pltpu.roll(right, cent, 1)))
        ids_ref[index : index + 1] = jnp.concatenate(joined, axis=1).astype(jnp.int32)


def line(cent, blocks):
    width = blocks[0].shape[1]
    return pl.pallas_call(
        functools.partial(line_kernel, cent),
        in_specs=[whole()] * len(blocks),
        out_specs=[whole()] * 2,
        out_shape=[
            jax.ShapeDtypeStruct((len(blocks) * cent, width), BF16),
            jax.ShapeDtypeStruct((8, len(blocks) * cent), jnp.int32),
        ],
    )(*blocks)


def score_kernel(owned, ids, mean, *refs):
    blocks, (second_ref, keep_ref, send_ref, sums) = refs[:-4], refs[-4:]
    count = jnp.zeros((K2, 1), F32)
    for index, block in enumerate(blocks):
        hit = iota((K2, block.shape[0]), 0) == ids[index : index + 1]
        one_hot = jnp.where(hit, 1.0, 0.0)
        count = count + jnp.sum(one_hot, axis=1, keepdims=True)
        part = jnp.dot(one_hot.astype(BF16), block[...], preferred_element_type=F32)
        if index == 0:
            sums[...] = part
        else:
            sums[...] += part
    second = (sums[...] / count).astype(BF16)
    values = second.astype(F32)
    sums[...] = values
    start = pl.multiple_of(lax.axis_index("dp") * owned, owned)
    second_ref[...] = sums[pl.ds(start, owned)].astype(BF16)
    norms = 0.5 * jnp.sum(values * values, axis=1, keepdims=True)
    row = jnp.concatenate(
        [as_row(norms[at : at + LANES]) for at in range(0, K2, LANES)], axis=1
    )
    products = lax.dot_general(
        mean[...], second, (((1,), (1,)), ((), ())), preferred_element_type=F32
    )
    scores = products - row
    half = K2 // 2
    low = lax.axis_index("mp") == 0
    keep_ref[...] = jnp.where(low, scores[:, :half], scores[:, half:])
    send_ref[...] = jnp.where(low, scores[:, half:], scores[:, :half]).astype(BF16)


def second_level_scores(owned, ids, mean, blocks):
    cent, width = mean.shape
    return pl.pallas_call(
        functools.partial(score_kernel, owned),
        in_specs=[whole()] * (2 + len(blocks)),
        out_specs=[whole()] * 3,
        out_shape=[
            jax.ShapeDtypeStruct((owned, width), BF16),
            jax.ShapeDtypeStruct((cent, K2 // 2), F32),
            jax.ShapeDtypeStruct((cent, K2 // 2), BF16),
        ],
        scratch_shapes=[pltpu.VMEM((K2, width), F32)],
        compiler_params=pltpu.CompilerParams(vmem_limit_bytes=32 * 2**20),
    )(ids, mean, *blocks)


def summed_scores(devices, second_level, first_centroids):
    second_ids = jnp.arange(K2, dtype=jnp.int32)
    group_hot = (second_level == second_ids[None, :]).astype(BF16)
    group_totals = jnp.einsum("ck,cd->kd", group_hot, first_centroids, preferred_element_type=F32)
    group_counts = jnp.sum(group_hot.astype(F32), axis=0)
    total, total_counts = lax.psum((group_totals, group_counts), "dp")
    every = (total / total_counts[:, None]).astype(BF16)
    owned = K2 // devices
    second = lax.dynamic_slice_in_dim(every, lax.axis_index("dp") * owned, owned, 0)
    values = every.astype(F32)
    products = jnp.einsum("cd,kd->ck", first_centroids, every, preferred_element_type=F32)
    partial_value = products - 0.5 * jnp.sum(values * values, axis=1)[None, :]
    scores = lax.psum_scatter(
        partial_value.astype(BF16), "mp", scatter_dimension=1, tiled=True
    ).astype(F32)
    return second, scores


def shards(embeddings, first_level, second_level):
    devices = lax.axis_size("dp")
    cores = lax.axis_size("mp")
    cent = second_level.shape[0]
    everyone = [(d, c) for d in range(devices) for c in range(cores)]

    def partner(value, index):
        return exchanged(value, [(d * cores + c, (d ^ index) * cores + c) for d, c in everyone])

    def ahead(value, steps):
        return exchanged(
            value, [(d * cores + c, (d + steps) % devices * cores + c) for d, c in everyone]
        )

    own, own_meta, *sends = band_sums(devices, cent, first_level, embeddings, second_level)
    got = [partner(send, index + 1) for index, send in enumerate(sends)]
    base, base_meta, following, far = group_sums(cent, own, own_meta, got)
    got = [ahead(following, GROUP), ahead(far, 2 * GROUP)]
    mean, send = means(cent, base, base_meta, got)
    if devices * cent > K2 or cores != 2:
        return (mean, *summed_scores(devices, second_level, mean))
    blocks = [send] + [ahead(send, steps) for steps in range(GROUP, devices, GROUP)]
    row, ids = line(cent, blocks)
    rows = [row] + [partner(row, index) for index in range(1, GROUP)]
    second, keep, send = second_level_scores(K2 // devices, ids, mean, rows)
    got = exchanged(send, [(d * cores + c, d * cores + (c ^ 1)) for d, c in everyone])
    return mean, second, keep + got.astype(F32)


def solution(mesh):
    placed = (P("dp", "mp"), P("dp"), P("dp", None))
    return jax.shard_map(
        shards,
        mesh=mesh,
        in_specs=placed,
        out_specs=(P("dp", "mp"), P("dp", "mp"), P("dp", "mp")),
        check_vma=False,
    )
```

```python
import functools

import jax
import jax.numpy as jnp
from jax import lax
from jax.experimental import pallas as pl
from jax.experimental.pallas import tpu as pltpu
from jax.sharding import PartitionSpec as P

BAND = 8
K2 = 1024
GROUP = 4
META = 16
BASE = 256
LANES = 128
BF16 = jnp.bfloat16
F32 = jnp.float32


def small():
    return pltpu.CompilerParams(vmem_limit_bytes=16 * 2**20)


def whole():
    return pl.BlockSpec(memory_space=pltpu.VMEM)


def exchanged(value, pairs):
    return lax.ppermute(value, ("dp", "mp"), pairs)


def iota(shape, dim):
    return lax.broadcasted_iota(jnp.int32, shape, dim)


def split_digits(row):
    high = jnp.floor(row * (1.0 / BASE))
    return high, row - high * BASE


def as_column(row, cent):
    hit = iota((cent, LANES), 0) == iota((cent, LANES), 1)
    return jnp.sum(jnp.where(hit, row, 0.0), axis=1, keepdims=True)


def as_row(column):
    rows = column.shape[0]
    hit = iota((rows, LANES), 0) == iota((rows, LANES), 1)
    return jnp.sum(jnp.where(hit, column, 0.0), axis=0, keepdims=True)


def one_hot_of(rows, label):
    hit = lax.broadcasted_iota(jnp.int16, (rows, label.shape[1]), 0) == label.astype(jnp.int16)
    return jnp.where(hit, jnp.ones((), BF16), jnp.zeros((), BF16))


def sum_kernel(devices, cent, ids_hbm, rows_hbm, group_ref, own_ref, own_meta_ref, *rest):
    sends, (ids_ref, rows_ref, totals, arrived) = rest[:-4], rest[-4:]
    steps, block = rows_ref.shape[:2]
    ids_copy = pltpu.make_async_copy(ids_hbm, ids_ref, arrived.at[steps])
    ids_copy.start()
    copies = [
        pltpu.make_async_copy(
            rows_hbm.at[step * block : (step + 1) * block], rows_ref.at[step], arrived.at[step]
        )
        for step in range(steps)
    ]
    for copy in copies:
        copy.start()
    position = lax.axis_index("dp")
    mate = position % GROUP
    labels = 2 * GROUP * cent
    ids_copy.wait()
    tallies = jnp.zeros((labels, LANES), BF16)
    for step in range(steps):
        offset = ids_ref[:, step * block : (step + 1) * block] - position * cent
        offset = jnp.where(offset < 0, offset + devices * cent, offset)
        ahead = offset // cent + mate
        partner = (ahead % GROUP) ^ mate
        slot = jnp.where(ahead // GROUP == 1, 1, 0)
        label = partner * (2 * cent) + slot * cent + offset % cent
        one_hot = one_hot_of(labels, label)
        for start in range(0, block, LANES):
            tallies = tallies + one_hot[:, start : start + LANES]
        copies[step].wait()
        part = jnp.dot(one_hot, rows_ref[step], preferred_element_type=F32)
        if step == 0:
            totals[...] = part
        else:
            totals[...] += part
    id_high, id_low = split_digits(group_ref[...].astype(F32))
    id_digits = jnp.concatenate([id_high, id_low], axis=0)
    counts = lax.dot_general(
        jnp.ones((8, LANES), BF16), tallies, (((1,), (1,)), ((), ())), preferred_element_type=F32
    )
    pair = 2 * cent
    own_ref[...] = totals[:pair]
    for index in range(GROUP):
        high, low = split_digits(counts[:1, index * pair : (index + 1) * pair])
        meta = jnp.concatenate([high, low, jnp.zeros((META - 2, LANES), F32)], axis=0)
        if index == 0:
            own_meta_ref[...] = meta
            own_meta_ref[2:4, :cent] = id_digits
        else:
            send = sends[index - 1]
            send[:pair] = totals[index * pair : (index + 1) * pair].astype(BF16)
            send[pair:, :LANES] = meta.astype(BF16)
            send[pair:, LANES:] = jnp.zeros((META, send.shape[1] - LANES), BF16)
            send[pair + 2 : pair + 4, :cent] = id_digits.astype(BF16)


def band_sums(devices, cent, ids, rows, group):
    count, width = rows.shape
    steps = 4
    block = count // steps
    pair = 2 * cent
    send = jax.ShapeDtypeStruct((pair + META, width), BF16)
    return pl.pallas_call(
        functools.partial(sum_kernel, devices, cent),
        in_specs=[pl.BlockSpec(memory_space=pltpu.HBM)] * 2 + [whole()],
        out_specs=[whole()] * (GROUP + 1),
        out_shape=[
            jax.ShapeDtypeStruct((pair, width), F32),
            jax.ShapeDtypeStruct((META, LANES), F32),
        ]
        + [send] * (GROUP - 1),
        scratch_shapes=[
            pltpu.VMEM((1, count), jnp.int32),
            pltpu.VMEM((steps, block, width), BF16),
            pltpu.VMEM((GROUP * pair, width), F32),
            pltpu.SemaphoreType.DMA((steps + 1,)),
        ],
        compiler_params=small(),
    )(
        pltpu.with_memory_space_constraint(ids.reshape(1, count), pltpu.HBM),
        pltpu.with_memory_space_constraint(rows, pltpu.HBM),
        group.reshape(1, cent),
    )


def group_kernel(cent, own, own_meta, one, two, three, base_ref, base_meta_ref, next_ref, far_ref):
    mate = lax.axis_index("dp") % GROUP
    pair = 2 * cent
    lane = iota((1, LANES), 1)
    near = own[:cent]
    middle = own[cent:]
    far = jnp.zeros_like(near)
    counts = own_meta[0:1] * BASE + own_meta[1:2]
    far_counts = jnp.zeros_like(counts)
    id_digits = [own_meta[2:4]]
    for index, got in ((1, one), (2, two), (3, three)):
        before = (mate ^ index) < mate
        first = got[:cent].astype(F32)
        near = near + jnp.where(before, first, 0.0)
        far = far + jnp.where(before, 0.0, first)
        middle = middle + got[cent:pair].astype(F32)
        meta = got[pair:, :LANES].astype(F32)
        row = meta[0:1] * BASE + meta[1:2]
        mask = (lane >= cent) | before
        counts = counts + jnp.where(mask, row, 0.0)
        far_counts = far_counts + jnp.where(mask, 0.0, row)
        id_digits.append(meta[2:4])
    id_digits = jnp.concatenate(id_digits, axis=0)
    padding = jnp.zeros((META - 2 - 2 * GROUP, LANES), F32)

    def meta_of(row):
        high, low = split_digits(row)
        return jnp.concatenate([high, low, id_digits, padding], axis=0)

    base_ref[...] = near
    base_meta_ref[...] = meta_of(counts)
    for send, sums, row in ((next_ref, middle, counts), (far_ref, far, far_counts)):
        send[:cent] = sums.astype(BF16)
        send[cent:, :LANES] = meta_of(row).astype(BF16)
        send[cent:, LANES:] = jnp.zeros((META, send.shape[1] - LANES), BF16)


def group_sums(cent, own, own_meta, got):
    width = own.shape[1]
    send = jax.ShapeDtypeStruct((cent + META, width), BF16)
    return pl.pallas_call(
        functools.partial(group_kernel, cent),
        in_specs=[whole()] * 5,
        out_specs=[whole()] * 4,
        out_shape=[
            jax.ShapeDtypeStruct((cent, width), F32),
            jax.ShapeDtypeStruct((META, LANES), F32),
            send,
            send,
        ],
        compiler_params=small(),
    )(own, own_meta, *got)


def mean_kernel(cent, base, base_meta, one, two, mean_ref, plain_ref, send_ref):
    sums = base[...] + one[:cent].astype(F32) + two[:cent].astype(F32)
    metas = [base_meta[...], one[cent:, :LANES].astype(F32), two[cent:, :LANES].astype(F32)]
    rows = [meta[0:1] * BASE + meta[1:2] for meta in metas]
    row = rows[0] + pltpu.roll(rows[1], LANES - cent, 1) + rows[2]
    mean = (sums / as_column(row, cent)).astype(BF16)
    mean_ref[...] = mean
    plain_ref[...] = mean
    send_ref[:cent] = mean
    for index, meta in enumerate(metas):
        send_ref[cent:, index * LANES : (index + 1) * LANES] = meta.astype(BF16)
    known = len(metas) * LANES
    send_ref[cent:, known:] = jnp.zeros((META, mean.shape[1] - known), BF16)


def means(cent, base, base_meta, got):
    width = base.shape[1]
    mean = jax.ShapeDtypeStruct((cent, width), BF16)
    return pl.pallas_call(
        functools.partial(mean_kernel, cent),
        in_specs=[whole()] * 4,
        out_specs=[whole()] * 3,
        out_shape=[mean, mean, jax.ShapeDtypeStruct((cent + META, width), BF16)],
        compiler_params=small(),
    )(base, base_meta, *got)


def near_kernel(cent, own, got, near_ref, ids_ref):
    near_ref[:cent] = own[:cent]
    near_ref[cent:] = got[:cent]
    odd = lax.axis_index("dp") // GROUP % 2 == 1
    lane = iota((1, LANES), 1)

    def ids_of(block, steps, index):
        meta = block[cent:, steps * LANES : (steps + 1) * LANES].astype(F32)
        at = 2 + 2 * index
        return meta[at : at + 1] * BASE + meta[at + 1 : at + 2]

    near_rows, far_rows = [], []
    for index in range(GROUP):
        near_rows.append((ids_of(own, 0, index), ids_of(got, 0, index)))
        last = jnp.where(odd, ids_of(got, 2, index), ids_of(own, 1, index))
        far_rows.append((ids_of(own, 2, index), last))
    rows = [
        jnp.where(lane < cent, left, pltpu.roll(right, cent, 1))
        for left, right in near_rows + far_rows
    ]
    ids_ref[...] = jnp.concatenate(rows, axis=0).astype(jnp.int32)


def near_rows(cent, own, got):
    width = own.shape[1]
    return pl.pallas_call(
        functools.partial(near_kernel, cent),
        in_specs=[whole()] * 2,
        out_specs=[whole()] * 2,
        out_shape=[
            jax.ShapeDtypeStruct((2 * cent, width), BF16),
            jax.ShapeDtypeStruct((2 * GROUP, LANES), jnp.int32),
        ],
        compiler_params=small(),
    )(own, got)


def far_kernel(first, second, far_ref):
    rows = first.shape[0]
    far_ref[:rows] = first[...]
    far_ref[rows:] = second[...]


def far_rows(first, second):
    rows, width = first.shape
    return pl.pallas_call(
        far_kernel,
        in_specs=[whole()] * 2,
        out_specs=whole(),
        out_shape=jax.ShapeDtypeStruct((2 * rows, width), BF16),
        compiler_params=small(),
    )(first, second)


def ids_row(ids, base, order):
    low = lax.axis_index("mp") == 0
    first = ids[base + order : base + order + 1]
    if order in (0, GROUP - 1):
        return first
    other = ids[base + GROUP - 1 - order : base + GROUP - order]
    return jnp.where(low, first, other)


def gather_kernel(ids, *refs):
    blocks, (sums_ref, tally_ref) = refs[:-2], refs[-2:]
    tally = jnp.zeros((K2, LANES), BF16)
    labels = [ids_row(ids, 0, order) for order in range(GROUP)]
    labels += [ids_row(ids, GROUP, order) for order in range(GROUP - 1)]
    total = None
    for label, block in zip(labels, blocks):
        one_hot = one_hot_of(K2, label)
        tally = tally + one_hot
        part = jnp.dot(one_hot, block[...], preferred_element_type=F32)
        total = part if total is None else total + part
    sums_ref[...] = total
    tally_ref[...] = tally


def gathered_sums(ids, blocks):
    width = blocks[0].shape[1]
    return pl.pallas_call(
        gather_kernel,
        in_specs=[whole()] * (1 + len(blocks)),
        out_specs=[whole()] * 2,
        out_shape=[
            jax.ShapeDtypeStruct((K2, width), F32),
            jax.ShapeDtypeStruct((K2, LANES), BF16),
        ],
        compiler_params=small(),
    )(ids, *blocks)


def score_kernel(owned, ids, mean, sums, tally, block, second_ref, keep_ref, send_ref, values_ref):
    one_hot = one_hot_of(K2, ids_row(ids, GROUP, GROUP - 1))
    count = jnp.sum((tally[...] + one_hot).astype(F32), axis=1, keepdims=True)
    total = sums[...] + jnp.dot(one_hot, block[...], preferred_element_type=F32)
    second = (total * (1.0 / count)).astype(BF16)
    values = second.astype(F32)
    values_ref[...] = values
    start = pl.multiple_of(lax.axis_index("dp") * owned, owned)
    second_ref[...] = values_ref[pl.ds(start, owned)].astype(BF16)
    norms = 0.5 * jnp.sum(values * values, axis=1, keepdims=True)
    row = jnp.concatenate(
        [as_row(norms[at : at + LANES]) for at in range(0, K2, LANES)], axis=1
    )
    products = lax.dot_general(
        mean[...], second, (((1,), (1,)), ((), ())), preferred_element_type=F32
    )
    scores = products - row
    half = K2 // 2
    low = lax.axis_index("mp") == 0
    keep_ref[...] = jnp.where(low, scores[:, :half], scores[:, half:])
    send_ref[...] = jnp.where(low, scores[:, half:], scores[:, :half]).astype(BF16)


def second_level_scores(owned, ids, mean, sums, tally, block):
    cent, width = mean.shape
    return pl.pallas_call(
        functools.partial(score_kernel, owned),
        in_specs=[whole()] * 5,
        out_specs=[whole()] * 3,
        out_shape=[
            jax.ShapeDtypeStruct((owned, width), BF16),
            jax.ShapeDtypeStruct((cent, K2 // 2), F32),
            jax.ShapeDtypeStruct((cent, K2 // 2), BF16),
        ],
        scratch_shapes=[pltpu.VMEM((K2, width), F32)],
        compiler_params=small(),
    )(ids, mean, sums, tally, block)


def summed_scores(devices, second_level, first_centroids):
    second_ids = jnp.arange(K2, dtype=jnp.int32)
    group_hot = (second_level == second_ids[None, :]).astype(BF16)
    group_totals = jnp.einsum("ck,cd->kd", group_hot, first_centroids, preferred_element_type=F32)
    group_counts = jnp.sum(group_hot.astype(F32), axis=0)
    total, total_counts = lax.psum((group_totals, group_counts), "dp")
    every = (total / total_counts[:, None]).astype(BF16)
    owned = K2 // devices
    second = lax.dynamic_slice_in_dim(every, lax.axis_index("dp") * owned, owned, 0)
    values = every.astype(F32)
    products = jnp.einsum("cd,kd->ck", first_centroids, every, preferred_element_type=F32)
    partial_value = products - 0.5 * jnp.sum(values * values, axis=1)[None, :]
    scores = lax.psum_scatter(
        partial_value.astype(BF16), "mp", scatter_dimension=1, tiled=True
    ).astype(F32)
    return second, scores


def shards(embeddings, first_level, second_level):
    devices = lax.axis_size("dp")
    cores = lax.axis_size("mp")
    cent = second_level.shape[0]
    everyone = [(d, c) for d in range(devices) for c in range(cores)]

    def partner(value, index):
        return exchanged(value, [(d * cores + c, (d ^ index) * cores + c) for d, c in everyone])

    def ahead(value, steps):
        return exchanged(
            value, [(d * cores + c, (d + steps) % devices * cores + c) for d, c in everyone]
        )

    own, own_meta, *sends = band_sums(devices, cent, first_level, embeddings, second_level)
    got = [partner(send, index + 1) for index, send in enumerate(sends)]
    base, base_meta, following, far = group_sums(cent, own, own_meta, got)
    got = [ahead(following, GROUP), ahead(far, 2 * GROUP)]
    mean, plain, send = means(cent, base, base_meta, got)
    if devices != GROUP * GROUP or cores != 2 or devices * cent > K2:
        return (mean, *summed_scores(devices, second_level, mean))

    def sideways(value, steps):
        return exchanged(
            value, [(d * cores + c, (d ^ steps[c]) * cores + c) for d, c in everyone]
        )

    def plane_rows(value):
        first = sideways(value, (1, 2))
        second = sideways(value, (2, 1))
        return [value, first, second, sideways(first, (2, 1))]

    near, ids = near_rows(cent, send, partner(send, GROUP))
    far = far_rows(partner(plain, 2 * GROUP), partner(plain, 3 * GROUP))
    *blocks, last = plane_rows(near) + plane_rows(far)
    sums, tally = gathered_sums(ids, blocks)
    second, keep, send = second_level_scores(K2 // devices, ids, plain, sums, tally, last)
    got = exchanged(send, [(d * cores + c, d * cores + (c ^ 1)) for d, c in everyone])
    return mean, second, keep + got.astype(F32)


def solution(mesh):
    placed = (P("dp", "mp"), P("dp"), P("dp", None))
    return jax.shard_map(
        shards,
        mesh=mesh,
        in_specs=placed,
        out_specs=(P("dp", "mp"), P("dp", "mp"), P("dp", "mp")),
        check_vma=False,
    )
```

```python
import functools

import jax
import jax.numpy as jnp
from jax import lax
from jax.experimental import pallas as pl
from jax.experimental.pallas import tpu as pltpu
from jax.sharding import PartitionSpec as P

BAND = 8
K2 = 1024
GROUP = 4
META = 8
BASE = 256
LANES = 128
BF16 = jnp.bfloat16
F32 = jnp.float32


def small():
    return pltpu.CompilerParams(vmem_limit_bytes=16 * 2**20)


def whole():
    return pl.BlockSpec(memory_space=pltpu.VMEM)


def exchanged(value, pairs):
    return lax.ppermute(value, ("dp", "mp"), pairs)


def iota(shape, dim):
    return lax.broadcasted_iota(jnp.int32, shape, dim)


def split_digits(row):
    high = jnp.floor(row * (1.0 / BASE))
    return high, row - high * BASE


def as_column(row, cent):
    hit = iota((cent, LANES), 0) == iota((cent, LANES), 1)
    return jnp.sum(jnp.where(hit, row, 0.0), axis=1, keepdims=True)


def as_row(column):
    rows = column.shape[0]
    hit = iota((rows, LANES), 0) == iota((rows, LANES), 1)
    return jnp.sum(jnp.where(hit, column, 0.0), axis=0, keepdims=True)


def one_hot_of(rows, label):
    hit = lax.broadcasted_iota(jnp.int16, (rows, label.shape[1]), 0) == label.astype(jnp.int16)
    return jnp.where(hit, jnp.ones((), BF16), jnp.zeros((), BF16))


def sum_kernel(devices, cent, ids_hbm, rows_hbm, group_hbm, own_ref, own_meta_ref, *rest):
    sends, (ids_ref, rows_ref, group_ref, totals, arrived) = rest[:-5], rest[-5:]
    steps, block = rows_ref.shape[:2]
    ids_copy = pltpu.make_async_copy(ids_hbm, ids_ref, arrived.at[steps])
    ids_copy.start()
    group_copy = pltpu.make_async_copy(group_hbm, group_ref, arrived.at[steps + 1])
    copies = [
        pltpu.make_async_copy(
            rows_hbm.at[step * block : (step + 1) * block], rows_ref.at[step], arrived.at[step]
        )
        for step in range(steps)
    ]
    for copy in copies:
        copy.start()
    group_copy.start()
    position = lax.axis_index("dp")
    mate = position % GROUP
    labels = 2 * GROUP * cent
    ids_copy.wait()
    tallies = jnp.zeros((labels, LANES), BF16)
    for step in range(steps):
        offset = ids_ref[:, step * block : (step + 1) * block] - position * cent
        offset = jnp.where(offset < 0, offset + devices * cent, offset)
        ahead = offset // cent + mate
        partner = (ahead % GROUP) ^ mate
        slot = jnp.where(ahead // GROUP == 1, 1, 0)
        label = partner * (2 * cent) + slot * cent + offset % cent
        one_hot = one_hot_of(labels, label)
        for start in range(0, block, LANES):
            tallies = tallies + one_hot[:, start : start + LANES]
        copies[step].wait()
        part = jnp.dot(one_hot, rows_ref[step], preferred_element_type=F32)
        if step == 0:
            totals[...] = part
        else:
            totals[...] += part
    group_copy.wait()
    id_high, id_low = split_digits(group_ref[...].astype(F32))
    id_digits = jnp.concatenate([id_high, id_low], axis=0)
    counts = lax.dot_general(
        jnp.ones((8, LANES), BF16), tallies, (((1,), (1,)), ((), ())), preferred_element_type=F32
    )
    pair = 2 * cent
    own_ref[...] = totals[:pair]
    for index in range(GROUP):
        high, low = split_digits(counts[:1, index * pair : (index + 1) * pair])
        meta = jnp.concatenate([high, low, jnp.zeros((META - 2, LANES), F32)], axis=0)
        if index == 0:
            own_meta_ref[:, :LANES] = meta
            own_meta_ref[:, LANES:] = jnp.zeros((META, LANES), F32)
            own_meta_ref[:2, LANES : LANES + cent] = id_digits
        else:
            send = sends[index - 1]
            send[:pair] = totals[index * pair : (index + 1) * pair].astype(BF16)
            send[pair:, :LANES] = meta.astype(BF16)
            send[pair:, LANES:] = jnp.zeros((META, send.shape[1] - LANES), BF16)
            send[pair : pair + 2, LANES : LANES + cent] = id_digits.astype(BF16)


def band_sums(devices, cent, ids, rows, group):
    count, width = rows.shape
    steps = 4
    block = count // steps
    pair = 2 * cent
    send = jax.ShapeDtypeStruct((pair + META, width), BF16)
    return pl.pallas_call(
        functools.partial(sum_kernel, devices, cent),
        in_specs=[pl.BlockSpec(memory_space=pltpu.HBM)] * 3,
        out_specs=[whole()] * (GROUP + 1),
        out_shape=[
            jax.ShapeDtypeStruct((pair, width), F32),
            jax.ShapeDtypeStruct((META, 2 * LANES), F32),
        ]
        + [send] * (GROUP - 1),
        scratch_shapes=[
            pltpu.VMEM((1, count), jnp.int32),
            pltpu.VMEM((steps, block, width), BF16),
            pltpu.VMEM((1, cent), jnp.int32),
            pltpu.VMEM((GROUP * pair, width), F32),
            pltpu.SemaphoreType.DMA((steps + 2,)),
        ],
        compiler_params=small(),
    )(
        pltpu.with_memory_space_constraint(ids.reshape(1, count), pltpu.HBM),
        pltpu.with_memory_space_constraint(rows, pltpu.HBM),
        pltpu.with_memory_space_constraint(group.reshape(1, cent), pltpu.HBM),
    )


def group_kernel(cent, own, own_meta, one, two, three, base_ref, base_meta_ref, next_ref, far_ref):
    mate = lax.axis_index("dp") % GROUP
    pair = 2 * cent
    lane = iota((1, LANES), 1)
    near = own[:cent]
    middle = own[cent:]
    far = jnp.zeros_like(near)
    counts = own_meta[0:1, :LANES] * BASE + own_meta[1:2, :LANES]
    far_counts = jnp.zeros_like(counts)
    id_digits = [own_meta[0:2, LANES:]]
    for index, got in ((1, one), (2, two), (3, three)):
        before = (mate ^ index) < mate
        first = got[:cent].astype(F32)
        near = near + jnp.where(before, first, 0.0)
        far = far + jnp.where(before, 0.0, first)
        middle = middle + got[cent:pair].astype(F32)
        meta = got[pair:, : 2 * LANES].astype(F32)
        row = meta[0:1, :LANES] * BASE + meta[1:2, :LANES]
        mask = (lane >= cent) | before
        counts = counts + jnp.where(mask, row, 0.0)
        far_counts = far_counts + jnp.where(mask, 0.0, row)
        id_digits.append(meta[0:2, LANES:])
    id_digits = jnp.concatenate(id_digits, axis=0)

    def meta_of(row):
        high, low = split_digits(row)
        digits = jnp.concatenate([high, low, jnp.zeros((META - 2, LANES), F32)], axis=0)
        return jnp.concatenate([digits, id_digits], axis=1)

    base_ref[...] = near
    base_meta_ref[...] = meta_of(counts)
    for send, sums, row in ((next_ref, middle, counts), (far_ref, far, far_counts)):
        send[:cent] = sums.astype(BF16)
        send[cent:, : 2 * LANES] = meta_of(row).astype(BF16)
        send[cent:, 2 * LANES :] = jnp.zeros((META, send.shape[1] - 2 * LANES), BF16)


def group_sums(cent, own, own_meta, got):
    width = own.shape[1]
    send = jax.ShapeDtypeStruct((cent + META, width), BF16)
    return pl.pallas_call(
        functools.partial(group_kernel, cent),
        in_specs=[whole()] * 5,
        out_specs=[whole()] * 4,
        out_shape=[
            jax.ShapeDtypeStruct((cent, width), F32),
            jax.ShapeDtypeStruct((META, 2 * LANES), F32),
            send,
            send,
        ],
        compiler_params=small(),
    )(own, own_meta, *got)


def mean_kernel(cent, base, base_meta, one, two, mean_ref, send_ref):
    sums = base[...] + one[:cent].astype(F32) + two[:cent].astype(F32)
    metas = [meta[...].astype(F32) for meta in (base_meta, one.at[cent:], two.at[cent:])]
    rows = [meta[0:1, :LANES] * BASE + meta[1:2, :LANES] for meta in metas]
    row = rows[0] + pltpu.roll(rows[1], LANES - cent, 1) + rows[2]
    mean = (sums / as_column(row, cent)).astype(BF16)
    mean_ref[...] = mean
    send_ref[:cent] = mean
    for index, meta in enumerate(metas):
        ids = meta[:, LANES : 2 * LANES].astype(BF16)
        send_ref[cent:, index * LANES : (index + 1) * LANES] = ids
    known = len(metas) * LANES
    send_ref[cent:, known:] = jnp.zeros((META, mean.shape[1] - known), BF16)


def means(cent, base, base_meta, got):
    width = base.shape[1]
    mean = jax.ShapeDtypeStruct((cent, width), BF16)
    return pl.pallas_call(
        functools.partial(mean_kernel, cent),
        in_specs=[whole()] * 4,
        out_specs=[whole()] * 2,
        out_shape=[mean, jax.ShapeDtypeStruct((cent + META, width), BF16)],
        compiler_params=small(),
    )(base, base_meta, *got)


def near_kernel(cent, own, got, near_ref, ids_ref):
    near_ref[:cent] = own[:cent]
    near_ref[cent:] = got[:cent]
    odd = lax.axis_index("dp") // GROUP % 2 == 1
    lane = iota((1, LANES), 1)

    def ids_of(block, steps, index):
        meta = block[cent:, steps * LANES : (steps + 1) * LANES].astype(F32)
        at = 2 * index
        return meta[at : at + 1] * BASE + meta[at + 1 : at + 2]

    near_rows, far_rows = [], []
    for index in range(GROUP):
        near_rows.append((ids_of(own, 0, index), ids_of(got, 0, index)))
        last = jnp.where(odd, ids_of(got, 2, index), ids_of(own, 1, index))
        far_rows.append((ids_of(own, 2, index), last))
    rows = [
        jnp.where(lane < cent, left, pltpu.roll(right, cent, 1))
        for left, right in near_rows + far_rows
    ]
    ids_ref[...] = jnp.concatenate(rows, axis=0).astype(jnp.int32)


def near_rows(cent, own, got):
    width = own.shape[1]
    return pl.pallas_call(
        functools.partial(near_kernel, cent),
        in_specs=[whole()] * 2,
        out_specs=[whole()] * 2,
        out_shape=[
            jax.ShapeDtypeStruct((2 * cent, width), BF16),
            jax.ShapeDtypeStruct((2 * GROUP, LANES), jnp.int32),
        ],
        compiler_params=small(),
    )(own, got)


def join_kernel(first, second, out_ref):
    rows = first.shape[0]
    out_ref[:rows] = first[...]
    out_ref[rows:] = second[...]


def joined(first, second):
    rows, width = first.shape
    return pl.pallas_call(
        join_kernel,
        in_specs=[whole()] * 2,
        out_specs=whole(),
        out_shape=jax.ShapeDtypeStruct((2 * rows, width), BF16),
        cost_estimate=pl.CostEstimate(flops=100000000000, bytes_accessed=300000000, transcendentals=0),
        compiler_params=small(),
    )(first, second)


def ids_row(ids, base, order):
    low = lax.axis_index("mp") == 0
    first = ids[base + order : base + order + 1]
    if order in (0, GROUP - 1):
        return first
    other = ids[base + GROUP - 1 - order : base + GROUP - order]
    return jnp.where(low, first, other)


def gathered(ids, base, blocks):
    one_hots = [one_hot_of(K2, ids_row(ids, base, order)) for order in range(GROUP)]
    rows = [block[...] for block in blocks]
    if len(rows) == GROUP:
        rows[2:] = [jnp.concatenate(rows[2:], axis=0)]
    rows[:2] = [jnp.concatenate(rows[:2], axis=0)]
    total = None
    for index, row in enumerate(rows):
        one_hot = jnp.concatenate(one_hots[2 * index : 2 * index + 2], axis=1)
        part = jnp.dot(one_hot, row, preferred_element_type=F32)
        total = part if total is None else total + part
    return total, sum(one_hots[1:], one_hots[0])


def gather_kernel(ids, *refs):
    blocks, (sums_ref, tally_ref) = refs[:-2], refs[-2:]
    sums_ref[...], tally_ref[...] = gathered(ids, 0, blocks)


def gathered_sums(ids, blocks):
    width = blocks[0].shape[1]
    return pl.pallas_call(
        gather_kernel,
        in_specs=[whole()] * (1 + len(blocks)),
        out_specs=[whole()] * 2,
        out_shape=[
            jax.ShapeDtypeStruct((K2, width), F32),
            jax.ShapeDtypeStruct((K2, LANES), BF16),
        ],
        compiler_params=small(),
    )(ids, *blocks)


def score_kernel(owned, ids, mean, sums, tally, *refs):
    blocks, refs = refs[:-7], refs[-7:]
    mean_hbm, second_hbm, keep_ref, send_ref, values_ref, second_ref, sent = refs
    mean_copy = pltpu.make_async_copy(mean, mean_hbm, sent.at[0])
    mean_copy.start()
    total, tally_here = gathered(ids, GROUP, blocks)
    count = jnp.sum((tally[...] + tally_here).astype(F32), axis=1, keepdims=True)
    second = ((sums[...] + total) * (1.0 / count)).astype(BF16)
    values = second.astype(F32)
    values_ref[...] = values
    start = pl.multiple_of(lax.axis_index("dp") * owned, owned)
    second_ref[...] = values_ref[pl.ds(start, owned)].astype(BF16)
    second_copy = pltpu.make_async_copy(second_ref, second_hbm, sent.at[1])
    second_copy.start()
    norms = 0.5 * jnp.sum(values * values, axis=1, keepdims=True)
    row = jnp.concatenate(
        [as_row(norms[at : at + LANES]) for at in range(0, K2, LANES)], axis=1
    )
    products = lax.dot_general(
        mean[...], second, (((1,), (1,)), ((), ())), preferred_element_type=F32
    )
    scores = products - row
    half = K2 // 2
    low = lax.axis_index("mp") == 0
    keep_ref[...] = jnp.where(low, scores[:, :half], scores[:, half:])
    send_ref[...] = jnp.where(low, scores[:, half:], scores[:, :half]).astype(BF16)
    mean_copy.wait()
    second_copy.wait()


def second_level_scores(owned, ids, mean, sums, tally, blocks):
    cent, width = mean.shape
    hbm = pl.BlockSpec(memory_space=pltpu.HBM)
    return pl.pallas_call(
        functools.partial(score_kernel, owned),
        in_specs=[whole()] * (4 + len(blocks)),
        out_specs=[hbm, hbm, whole(), whole()],
        out_shape=[
            jax.ShapeDtypeStruct((cent, width), BF16),
            jax.ShapeDtypeStruct((owned, width), BF16),
            jax.ShapeDtypeStruct((cent, K2 // 2), F32),
            jax.ShapeDtypeStruct((cent, K2 // 2), BF16),
        ],
        scratch_shapes=[
            pltpu.VMEM((K2, width), F32),
            pltpu.VMEM((owned, width), BF16),
            pltpu.SemaphoreType.DMA((2,)),
        ],
        compiler_params=small(),
    )(ids, mean, sums, tally, *blocks)


def summed_scores(devices, second_level, first_centroids):
    second_ids = jnp.arange(K2, dtype=jnp.int32)
    group_hot = (second_level == second_ids[None, :]).astype(BF16)
    group_totals = jnp.einsum("ck,cd->kd", group_hot, first_centroids, preferred_element_type=F32)
    group_counts = jnp.sum(group_hot.astype(F32), axis=0)
    total, total_counts = lax.psum((group_totals, group_counts), "dp")
    every = (total / total_counts[:, None]).astype(BF16)
    owned = K2 // devices
    second = lax.dynamic_slice_in_dim(every, lax.axis_index("dp") * owned, owned, 0)
    values = every.astype(F32)
    products = jnp.einsum("cd,kd->ck", first_centroids, every, preferred_element_type=F32)
    partial_value = products - 0.5 * jnp.sum(values * values, axis=1)[None, :]
    scores = lax.psum_scatter(
        partial_value.astype(BF16), "mp", scatter_dimension=1, tiled=True
    ).astype(F32)
    return second, scores


def shards(embeddings, first_level, second_level):
    devices = lax.axis_size("dp")
    cores = lax.axis_size("mp")
    cent = second_level.shape[0]
    everyone = [(d, c) for d in range(devices) for c in range(cores)]

    def partner(value, index):
        return exchanged(value, [(d * cores + c, (d ^ index) * cores + c) for d, c in everyone])

    def ahead(value, steps):
        return exchanged(
            value, [(d * cores + c, (d + steps) % devices * cores + c) for d, c in everyone]
        )

    own, own_meta, *sends = band_sums(devices, cent, first_level, embeddings, second_level)
    got = [partner(send, index + 1) for index, send in enumerate(sends)]
    base, base_meta, following, far = group_sums(cent, own, own_meta, got)
    got = [ahead(following, GROUP), ahead(far, 2 * GROUP)]
    mean, send = means(cent, base, base_meta, got)
    if devices != GROUP * GROUP or cores != 2 or devices * cent > K2:
        return (mean, *summed_scores(devices, second_level, mean))

    def sideways(value, steps):
        return exchanged(
            value, [(d * cores + c, (d ^ steps[c]) * cores + c) for d, c in everyone]
        )

    def plane_rows(value):
        return [value, sideways(value, (1, 2)), sideways(value, (2, 1)), partner(value, 3)]

    def relayed_rows(value):
        first = sideways(value, (1, 2))
        return [value, first, sideways(joined(value, first), (2, 1))]

    near, ids = near_rows(cent, send, partner(send, GROUP))
    far = joined(partner(mean, 2 * GROUP), partner(mean, 3 * GROUP))
    sums, tally = gathered_sums(ids, plane_rows(near))
    mean, second, keep, send = second_level_scores(
        K2 // devices, ids, mean, sums, tally, plane_rows(far)
    )
    got = exchanged(send, [(d * cores + c, d * cores + (c ^ 1)) for d, c in everyone])
    return mean, second, keep + got.astype(F32)


def solution(mesh):
    placed = (P("dp", "mp"), P("dp"), P("dp", None))
    return jax.shard_map(
        shards,
        mesh=mesh,
        in_specs=placed,
        out_specs=(P("dp", "mp"), P("dp", "mp"), P("dp", "mp")),
        check_vma=False,
    )
```

```python
import functools

import jax
import jax.numpy as jnp
from jax import lax
from jax.experimental import pallas as pl
from jax.experimental.pallas import tpu as pltpu
from jax.sharding import PartitionSpec as P

BAND = 8
K2 = 1024
GROUP = 4
META = 8
BASE = 256
LANES = 128
BF16 = jnp.bfloat16
F32 = jnp.float32


def small():
    return pltpu.CompilerParams(vmem_limit_bytes=16 * 2**20)


def whole():
    return pl.BlockSpec(memory_space=pltpu.VMEM)


def exchanged(value, pairs):
    return lax.ppermute(value, ("dp", "mp"), pairs)


def iota(shape, dim):
    return lax.broadcasted_iota(jnp.int32, shape, dim)


def even_line():
    return lax.axis_index("dp") // GROUP % 2 == 0


def split_digits(row):
    high = jnp.floor(row * (1.0 / BASE))
    return high, row - high * BASE


def as_column(row, cent):
    hit = iota((cent, LANES), 0) == iota((cent, LANES), 1)
    return jnp.sum(jnp.where(hit, row, 0.0), axis=1, keepdims=True)


def as_row(column):
    rows = column.shape[0]
    hit = iota((rows, LANES), 0) == iota((rows, LANES), 1)
    return jnp.sum(jnp.where(hit, column, 0.0), axis=0, keepdims=True)


def one_hot_of(rows, label):
    hit = lax.broadcasted_iota(jnp.int16, (rows, label.shape[1]), 0) == label.astype(jnp.int16)
    return jnp.where(hit, jnp.ones((), BF16), jnp.zeros((), BF16))


def sum_kernel(devices, cent, ids_hbm, rows_hbm, group_hbm, own_ref, own_meta_ref, *rest):
    sends, (ids_ref, rows_ref, group_ref, totals, arrived) = rest[:-5], rest[-5:]
    steps, block = rows_ref.shape[:2]
    ids_copy = pltpu.make_async_copy(ids_hbm, ids_ref, arrived.at[steps])
    ids_copy.start()
    group_copy = pltpu.make_async_copy(group_hbm, group_ref, arrived.at[steps + 1])
    copies = [
        pltpu.make_async_copy(
            rows_hbm.at[step * block : (step + 1) * block], rows_ref.at[step], arrived.at[step]
        )
        for step in range(steps)
    ]
    for copy in copies:
        copy.start()
    group_copy.start()
    position = lax.axis_index("dp")
    mate = position % GROUP
    labels = 2 * GROUP * cent
    ids_copy.wait()
    tallies = jnp.zeros((labels, LANES), BF16)
    for step in range(steps):
        offset = ids_ref[:, step * block : (step + 1) * block] - position * cent
        offset = jnp.where(offset < 0, offset + devices * cent, offset)
        ahead = offset // cent + mate
        partner = (ahead % GROUP) ^ mate
        slot = jnp.where(ahead // GROUP == 1, 1, 0)
        label = partner * (2 * cent) + slot * cent + offset % cent
        one_hot = one_hot_of(labels, label)
        for start in range(0, block, LANES):
            tallies = tallies + one_hot[:, start : start + LANES]
        copies[step].wait()
        part = jnp.dot(one_hot, rows_ref[step], preferred_element_type=F32)
        if step == 0:
            totals[...] = part
        else:
            totals[...] += part
    group_copy.wait()
    id_high, id_low = split_digits(group_ref[...].astype(F32))
    id_digits = jnp.concatenate([id_high, id_low], axis=0)
    counts = lax.dot_general(
        jnp.ones((8, LANES), BF16), tallies, (((1,), (1,)), ((), ())), preferred_element_type=F32
    )
    pair = 2 * cent
    own_ref[...] = totals[:pair]
    for index in range(GROUP):
        high, low = split_digits(counts[:1, index * pair : (index + 1) * pair])
        meta = jnp.concatenate([high, low, jnp.zeros((META - 2, LANES), F32)], axis=0)
        if index == 0:
            own_meta_ref[:, :LANES] = meta
            own_meta_ref[:, LANES:] = jnp.zeros((META, LANES), F32)
            own_meta_ref[:2, LANES : LANES + cent] = id_digits
        else:
            send = sends[index - 1]
            send[:pair] = totals[index * pair : (index + 1) * pair].astype(BF16)
            send[pair:, :LANES] = meta.astype(BF16)
            send[pair:, LANES:] = jnp.zeros((META, send.shape[1] - LANES), BF16)
            send[pair : pair + 2, LANES : LANES + cent] = id_digits.astype(BF16)


def band_sums(devices, cent, ids, rows, group):
    count, width = rows.shape
    steps = 4
    block = count // steps
    pair = 2 * cent
    send = jax.ShapeDtypeStruct((pair + META, width), BF16)
    return pl.pallas_call(
        functools.partial(sum_kernel, devices, cent),
        in_specs=[pl.BlockSpec(memory_space=pltpu.HBM)] * 3,
        out_specs=[whole()] * (GROUP + 1),
        out_shape=[
            jax.ShapeDtypeStruct((pair, width), F32),
            jax.ShapeDtypeStruct((META, 2 * LANES), F32),
        ]
        + [send] * (GROUP - 1),
        scratch_shapes=[
            pltpu.VMEM((1, count), jnp.int32),
            pltpu.VMEM((steps, block, width), BF16),
            pltpu.VMEM((1, cent), jnp.int32),
            pltpu.VMEM((GROUP * pair, width), F32),
            pltpu.SemaphoreType.DMA((steps + 2,)),
        ],
        compiler_params=small(),
    )(
        pltpu.with_memory_space_constraint(ids.reshape(1, count), pltpu.HBM),
        pltpu.with_memory_space_constraint(rows, pltpu.HBM),
        pltpu.with_memory_space_constraint(group.reshape(1, cent), pltpu.HBM),
    )


def group_kernel(cent, four, own, own_meta, one, two, three, base_ref, base_meta_ref, next_ref, far_ref):
    mate = lax.axis_index("dp") % GROUP
    pair = 2 * cent
    lane = iota((1, LANES), 1)
    near = own[:cent]
    middle = own[cent:]
    far = jnp.zeros_like(near)
    counts = own_meta[0:1, :LANES] * BASE + own_meta[1:2, :LANES]
    far_counts = jnp.zeros_like(counts)
    id_digits = [own_meta[0:2, LANES:]]
    for index, got in ((1, one), (2, two), (3, three)):
        before = (mate ^ index) < mate
        first = got[:cent].astype(F32)
        near = near + jnp.where(before, first, 0.0)
        far = far + jnp.where(before, 0.0, first)
        middle = middle + got[cent:pair].astype(F32)
        meta = got[pair:, : 2 * LANES].astype(F32)
        row = meta[0:1, :LANES] * BASE + meta[1:2, :LANES]
        mask = (lane >= cent) | before
        counts = counts + jnp.where(mask, row, 0.0)
        far_counts = far_counts + jnp.where(mask, 0.0, row)
        id_digits.append(meta[0:2, LANES:])
    id_digits = jnp.concatenate(id_digits, axis=0)

    def meta_of(row):
        high, low = split_digits(row)
        digits = jnp.concatenate([high, low, jnp.zeros((META - 2, LANES), F32)], axis=0)
        return jnp.concatenate([digits, id_digits], axis=1)

    if four:
        even = even_line()
        near, far = jnp.where(even, far, near), jnp.where(even, near, far)
        counts, far_counts = (
            jnp.where(even & (lane < cent), far_counts, counts),
            jnp.where(even, counts, far_counts),
        )
    base_ref[...] = near
    base_meta_ref[...] = meta_of(counts)
    for send, sums, row in ((next_ref, middle, counts), (far_ref, far, far_counts)):
        send[:cent] = sums.astype(BF16)
        send[cent:, : 2 * LANES] = meta_of(row).astype(BF16)
        send[cent:, 2 * LANES :] = jnp.zeros((META, send.shape[1] - 2 * LANES), BF16)


def group_sums(cent, four, own, own_meta, got):
    width = own.shape[1]
    send = jax.ShapeDtypeStruct((cent + META, width), BF16)
    return pl.pallas_call(
        functools.partial(group_kernel, cent, four),
        in_specs=[whole()] * 5,
        out_specs=[whole()] * 4,
        out_shape=[
            jax.ShapeDtypeStruct((cent, width), F32),
            jax.ShapeDtypeStruct((META, 2 * LANES), F32),
            send,
            send,
        ],
        compiler_params=small(),
    )(own, own_meta, *got)


def mean_kernel(cent, base, base_meta, one, two, mean_ref, send_ref):
    sums = base[...] + one[:cent].astype(F32) + two[:cent].astype(F32)
    metas = [meta[...].astype(F32) for meta in (base_meta, one.at[cent:], two.at[cent:])]
    rows = [meta[0:1, :LANES] * BASE + meta[1:2, :LANES] for meta in metas]
    row = rows[0] + pltpu.roll(rows[1], LANES - cent, 1) + rows[2]
    mean = (sums / as_column(row, cent)).astype(BF16)
    mean_ref[...] = mean
    send_ref[:cent] = mean
    for index, meta in enumerate(metas):
        ids = meta[:, LANES : 2 * LANES].astype(BF16)
        send_ref[cent:, index * LANES : (index + 1) * LANES] = ids
    known = len(metas) * LANES
    send_ref[cent:, known:] = jnp.zeros((META, mean.shape[1] - known), BF16)


def means(cent, base, base_meta, got):
    width = base.shape[1]
    mean = jax.ShapeDtypeStruct((cent, width), BF16)
    return pl.pallas_call(
        functools.partial(mean_kernel, cent),
        in_specs=[whole()] * 4,
        out_specs=[whole()] * 2,
        out_shape=[mean, jax.ShapeDtypeStruct((cent + META, width), BF16)],
        compiler_params=small(),
    )(base, base_meta, *got)


def near_kernel(cent, own, got, near_ref, ids_ref):
    near_ref[:cent] = own[:cent]
    near_ref[cent:] = got[:cent]
    even = even_line()
    lane = iota((1, LANES), 1)

    def ids_of(block, steps, index):
        meta = block[cent:, steps * LANES : (steps + 1) * LANES].astype(F32)
        at = 2 * index
        return meta[at : at + 1] * BASE + meta[at + 1 : at + 2]

    near_rows, far_rows = [], []
    for index in range(GROUP):
        here, one, two = (ids_of(own, steps, index) for steps in range(3))
        three = ids_of(got, 2, index)
        near_rows.append((jnp.where(even, two, here), jnp.where(even, one, three)))
        far_rows.append((jnp.where(even, here, two), jnp.where(even, three, one)))
    rows = [
        jnp.where(lane < cent, left, pltpu.roll(right, cent, 1))
        for left, right in near_rows + far_rows
    ]
    ids_ref[...] = jnp.concatenate(rows, axis=0).astype(jnp.int32)


def near_rows(cent, own, got):
    width = own.shape[1]
    return pl.pallas_call(
        functools.partial(near_kernel, cent),
        in_specs=[whole()] * 2,
        out_specs=[whole()] * 2,
        out_shape=[
            jax.ShapeDtypeStruct((2 * cent, width), BF16),
            jax.ShapeDtypeStruct((2 * GROUP, LANES), jnp.int32),
        ],
        compiler_params=small(),
    )(own, got)


def join_kernel(first, second, out_ref):
    rows = first.shape[0]
    out_ref[:rows] = first[...]
    out_ref[rows:] = second[...]


def joined(first, second):
    rows, width = first.shape
    return pl.pallas_call(
        join_kernel,
        in_specs=[whole()] * 2,
        out_specs=whole(),
        out_shape=jax.ShapeDtypeStruct((2 * rows, width), BF16),
        cost_estimate=pl.CostEstimate(flops=100000000000, bytes_accessed=300000000, transcendentals=0),
        compiler_params=small(),
    )(first, second)


def ids_row(ids, base, order):
    low = lax.axis_index("mp") == 0
    first = ids[base + order : base + order + 1]
    if order in (0, GROUP - 1):
        return first
    other = ids[base + GROUP - 1 - order : base + GROUP - order]
    return jnp.where(low, first, other)


def gathered(ids, base, blocks):
    one_hots = [one_hot_of(K2, ids_row(ids, base, order)) for order in range(GROUP)]
    rows = [block[...] for block in blocks]
    if len(rows) == GROUP:
        rows[2:] = [jnp.concatenate(rows[2:], axis=0)]
    rows[:2] = [jnp.concatenate(rows[:2], axis=0)]
    total = None
    for index, row in enumerate(rows):
        one_hot = jnp.concatenate(one_hots[2 * index : 2 * index + 2], axis=1)
        part = jnp.dot(one_hot, row, preferred_element_type=F32)
        total = part if total is None else total + part
    return total, sum(one_hots[1:], one_hots[0])


def gather_kernel(ids, *refs):
    blocks, (sums_ref, tally_ref) = refs[:-2], refs[-2:]
    sums_ref[...], tally_ref[...] = gathered(ids, 0, blocks)


def gathered_sums(ids, blocks):
    width = blocks[0].shape[1]
    return pl.pallas_call(
        gather_kernel,
        in_specs=[whole()] * (1 + len(blocks)),
        out_specs=[whole()] * 2,
        out_shape=[
            jax.ShapeDtypeStruct((K2, width), F32),
            jax.ShapeDtypeStruct((K2, LANES), BF16),
        ],
        compiler_params=small(),
    )(ids, *blocks)


def score_kernel(owned, ids, mean, sums, tally, *refs):
    blocks, refs = refs[:-8], refs[-8:]
    mean_hbm, second_hbm, keep_ref, send_ref, values_ref, mean_ref, second_ref, sent = refs
    cent = mean.shape[0]
    first = jnp.where(even_line(), blocks[0][:cent], mean[...])
    mean_ref[...] = first
    mean_copy = pltpu.make_async_copy(mean_ref, mean_hbm, sent.at[0])
    mean_copy.start()
    total, tally_here = gathered(ids, GROUP, blocks)
    count = jnp.sum((tally[...] + tally_here).astype(F32), axis=1, keepdims=True)
    second = ((sums[...] + total) * (1.0 / count)).astype(BF16)
    values = second.astype(F32)
    values_ref[...] = values
    start = pl.multiple_of(lax.axis_index("dp") * owned, owned)
    second_ref[...] = values_ref[pl.ds(start, owned)].astype(BF16)
    second_copy = pltpu.make_async_copy(second_ref, second_hbm, sent.at[1])
    second_copy.start()
    norms = 0.5 * jnp.sum(values * values, axis=1, keepdims=True)
    row = jnp.concatenate(
        [as_row(norms[at : at + LANES]) for at in range(0, K2, LANES)], axis=1
    )
    products = lax.dot_general(
        first, second, (((1,), (1,)), ((), ())), preferred_element_type=F32
    )
    scores = products - row
    half = K2 // 2
    low = lax.axis_index("mp") == 0
    keep_ref[...] = jnp.where(low, scores[:, :half], scores[:, half:])
    send_ref[...] = jnp.where(low, scores[:, half:], scores[:, :half]).astype(BF16)
    mean_copy.wait()
    second_copy.wait()


def second_level_scores(owned, ids, mean, sums, tally, blocks):
    cent, width = mean.shape
    hbm = pl.BlockSpec(memory_space=pltpu.HBM)
    return pl.pallas_call(
        functools.partial(score_kernel, owned),
        in_specs=[whole()] * (4 + len(blocks)),
        out_specs=[hbm, hbm, whole(), whole()],
        out_shape=[
            jax.ShapeDtypeStruct((cent, width), BF16),
            jax.ShapeDtypeStruct((owned, width), BF16),
            jax.ShapeDtypeStruct((cent, K2 // 2), F32),
            jax.ShapeDtypeStruct((cent, K2 // 2), BF16),
        ],
        scratch_shapes=[
            pltpu.VMEM((K2, width), F32),
            pltpu.VMEM((cent, width), BF16),
            pltpu.VMEM((owned, width), BF16),
            pltpu.SemaphoreType.DMA((2,)),
        ],
        compiler_params=small(),
    )(ids, mean, sums, tally, *blocks)


def summed_scores(devices, second_level, first_centroids):
    second_ids = jnp.arange(K2, dtype=jnp.int32)
    group_hot = (second_level == second_ids[None, :]).astype(BF16)
    group_totals = jnp.einsum("ck,cd->kd", group_hot, first_centroids, preferred_element_type=F32)
    group_counts = jnp.sum(group_hot.astype(F32), axis=0)
    total, total_counts = lax.psum((group_totals, group_counts), "dp")
    every = (total / total_counts[:, None]).astype(BF16)
    owned = K2 // devices
    second = lax.dynamic_slice_in_dim(every, lax.axis_index("dp") * owned, owned, 0)
    values = every.astype(F32)
    products = jnp.einsum("cd,kd->ck", first_centroids, every, preferred_element_type=F32)
    partial_value = products - 0.5 * jnp.sum(values * values, axis=1)[None, :]
    scores = lax.psum_scatter(
        partial_value.astype(BF16), "mp", scatter_dimension=1, tiled=True
    ).astype(F32)
    return second, scores


def shards(embeddings, first_level, second_level):
    devices = lax.axis_size("dp")
    cores = lax.axis_size("mp")
    cent = second_level.shape[0]
    everyone = [(d, c) for d in range(devices) for c in range(cores)]

    def partner(value, index):
        return exchanged(value, [(d * cores + c, (d ^ index) * cores + c) for d, c in everyone])

    def ahead(value, steps):
        return exchanged(
            value, [(d * cores + c, (d + steps) % devices * cores + c) for d, c in everyone]
        )

    own, own_meta, *sends = band_sums(devices, cent, first_level, embeddings, second_level)
    got = [partner(send, index + 1) for index, send in enumerate(sends)]
    four = devices == GROUP * GROUP and cores == 2 and devices * cent <= K2
    base, base_meta, following, far = group_sums(cent, four, own, own_meta, got)
    if four:
        got = [partner(following, GROUP), partner(far, 2 * GROUP)]
    else:
        got = [ahead(following, GROUP), ahead(far, 2 * GROUP)]
    mean, send = means(cent, base, base_meta, got)
    if not four:
        return (mean, *summed_scores(devices, second_level, mean))

    def sideways(value, steps):
        return exchanged(
            value, [(d * cores + c, (d ^ steps[c]) * cores + c) for d, c in everyone]
        )

    def plane_rows(value):
        return [value, sideways(value, (1, 2)), sideways(value, (2, 1)), partner(value, 3)]

    def relayed_rows(value):
        first = sideways(value, (1, 2))
        return [value, first, sideways(joined(value, first), (2, 1))]

    near, ids = near_rows(cent, send, partner(send, GROUP))
    far = joined(partner(mean, 2 * GROUP), partner(mean, 3 * GROUP))
    sums, tally = gathered_sums(ids, plane_rows(near))
    mean, second, keep, send = second_level_scores(
        K2 // devices, ids, mean, sums, tally, plane_rows(far)
    )
    got = exchanged(send, [(d * cores + c, d * cores + (c ^ 1)) for d, c in everyone])
    return mean, second, keep + got.astype(F32)


def solution(mesh):
    placed = (P("dp", "mp"), P("dp"), P("dp", None))
    return jax.shard_map(
        shards,
        mesh=mesh,
        in_specs=placed,
        out_specs=(P("dp", "mp"), P("dp", "mp"), P("dp", "mp")),
        check_vma=False,
    )
```

```python
import functools

import jax
import jax.numpy as jnp
from jax import lax
from jax.experimental import pallas as pl
from jax.experimental.pallas import tpu as pltpu
from jax.sharding import PartitionSpec as P

BAND = 8
K2 = 1024
GROUP = 4
META = 8
BASE = 256
LANES = 128
BF16 = jnp.bfloat16
F32 = jnp.float32


def small():
    return pltpu.CompilerParams(vmem_limit_bytes=16 * 2**20)


def whole():
    return pl.BlockSpec(memory_space=pltpu.VMEM)


def exchanged(value, pairs):
    return lax.ppermute(value, ("dp", "mp"), pairs)


def iota(shape, dim):
    return lax.broadcasted_iota(jnp.int32, shape, dim)


def even_line():
    return lax.axis_index("dp") // GROUP % 2 == 0


def split_digits(row):
    high = jnp.floor(row * (1.0 / BASE))
    return high, row - high * BASE


def as_column(row, cent):
    hit = iota((cent, LANES), 0) == iota((cent, LANES), 1)
    return jnp.sum(jnp.where(hit, row, 0.0), axis=1, keepdims=True)


def as_row(column):
    rows = column.shape[0]
    hit = iota((rows, LANES), 0) == iota((rows, LANES), 1)
    return jnp.sum(jnp.where(hit, column, 0.0), axis=0, keepdims=True)


def one_hot_of(rows, label):
    hit = lax.broadcasted_iota(jnp.int16, (rows, label.shape[1]), 0) == label.astype(jnp.int16)
    return jnp.where(hit, jnp.ones((), BF16), jnp.zeros((), BF16))


ORDER = (3, 1, 2, 0)


def labelled_sums(start, labels, chunks, label_ref, rows_ref, totals, copies=None):
    tallies = jnp.zeros((labels, LANES), BF16)
    for step, (low, high) in enumerate(chunks):
        one_hot = one_hot_of(labels, label_ref[:, low:high] - start)
        for at in range(0, high - low, LANES):
            tallies = tallies + one_hot[:, at : at + LANES]
        if copies:
            copies[step].wait()
        part = jnp.dot(one_hot, rows_ref[low:high], preferred_element_type=F32)
        if step == 0:
            totals[...] = part
        else:
            totals[...] += part
    counts = lax.dot_general(
        jnp.ones((8, LANES), BF16), tallies, (((1,), (1,)), ((), ())), preferred_element_type=F32
    )
    return counts[:1]


def fill_send(send, sums, counts, id_digits):
    pair = sums.shape[0]
    cent = id_digits.shape[1]
    high, low = split_digits(counts)
    meta = jnp.concatenate([high, low, jnp.zeros((META - 2, LANES), F32)], axis=0)
    send[:pair] = sums.astype(BF16)
    send[pair:, :LANES] = meta.astype(BF16)
    send[pair:, LANES:] = jnp.zeros((META, send.shape[1] - LANES), BF16)
    send[pair : pair + 2, LANES : LANES + cent] = id_digits.astype(BF16)


def first_kernel(devices, cent, chunks, ids_hbm, rows_hbm, group_hbm, *refs):
    sends, (rows_ref, label_ref, digits_ref, ids_ref, group_ref, totals, arrived) = refs[:2], refs[2:]
    steps = len(chunks)
    ids_copy = pltpu.make_async_copy(ids_hbm, ids_ref, arrived.at[steps])
    group_copy = pltpu.make_async_copy(group_hbm, group_ref, arrived.at[steps + 1])
    copies = [
        pltpu.make_async_copy(rows_hbm.at[low:high], rows_ref.at[low:high], arrived.at[step])
        for step, (low, high) in enumerate(chunks)
    ]
    ids_copy.start()
    for copy in copies:
        copy.start()
    group_copy.start()
    position = lax.axis_index("dp")
    mate = position % GROUP
    pair = 2 * cent
    ids_copy.wait()
    offset = ids_ref[...] - position * cent
    offset = jnp.where(offset < 0, offset + devices * cent, offset)
    ahead = offset // cent + mate
    partner = (ahead % GROUP) ^ mate
    place = jnp.zeros_like(partner)
    for index, who in enumerate(ORDER):
        place = jnp.where(partner == who, index, place)
    slot = jnp.where(ahead // GROUP == 1, 1, 0)
    label_ref[...] = place * pair + slot * cent + offset % cent
    counts = labelled_sums(0, 2 * pair, chunks, label_ref, rows_ref, totals, copies)
    group_copy.wait()
    digits = jnp.concatenate(split_digits(group_ref[...].astype(F32)), axis=0)
    digits_ref[...] = digits
    for index, send in enumerate(sends):
        at = index * pair
        fill_send(send, totals[at : at + pair], counts[:, at : at + pair], digits)


def second_kernel(cent, chunks, label_ref, rows_ref, digits_ref, send, own_ref, own_meta_ref, totals):
    pair = 2 * cent
    counts = labelled_sums(2 * pair, 2 * pair, chunks, label_ref, rows_ref, totals)
    digits = digits_ref[...]
    fill_send(send, totals[:pair], counts[:, :pair], digits)
    own_ref[...] = totals[pair:]
    high, low = split_digits(counts[:, pair:])
    meta = jnp.concatenate([high, low, jnp.zeros((META - 2, LANES), F32)], axis=0)
    own_meta_ref[:, :LANES] = meta
    own_meta_ref[:, LANES:] = jnp.zeros((META, LANES), F32)
    own_meta_ref[:2, LANES : LANES + cent] = digits


def band_sums(devices, cent, ids, rows, group):
    count, width = rows.shape
    pair = 2 * cent
    send = jax.ShapeDtypeStruct((pair + META, width), BF16)
    edges = [count * part // 12 for part in (0, 3, 6, 9, 12)]
    chunks = list(zip(edges[:-1], edges[1:]))
    half = count // 2
    hbm = pl.BlockSpec(memory_space=pltpu.HBM)
    one, two, rows, label, digits = pl.pallas_call(
        functools.partial(first_kernel, devices, cent, chunks),
        in_specs=[hbm] * 3,
        out_specs=[whole()] * 5,
        out_shape=[
            send,
            send,
            jax.ShapeDtypeStruct((count, width), BF16),
            jax.ShapeDtypeStruct((1, count), jnp.int32),
            jax.ShapeDtypeStruct((2, cent), F32),
        ],
        scratch_shapes=[
            pltpu.VMEM((1, count), jnp.int32),
            pltpu.VMEM((1, cent), jnp.int32),
            pltpu.VMEM((2 * pair, width), F32),
            pltpu.SemaphoreType.DMA((len(chunks) + 2,)),
        ],
        compiler_params=small(),
    )(
        pltpu.with_memory_space_constraint(ids.reshape(1, count), pltpu.HBM),
        pltpu.with_memory_space_constraint(rows, pltpu.HBM),
        pltpu.with_memory_space_constraint(group.reshape(1, cent), pltpu.HBM),
    )
    three, own, own_meta = pl.pallas_call(
        functools.partial(second_kernel, cent, [(0, half), (half, count)]),
        in_specs=[whole()] * 3,
        out_specs=[whole()] * 3,
        out_shape=[
            send,
            jax.ShapeDtypeStruct((pair, width), F32),
            jax.ShapeDtypeStruct((META, 2 * LANES), F32),
        ],
        cost_estimate=pl.CostEstimate(flops=100000000000, bytes_accessed=300000000, transcendentals=0),
        scratch_shapes=[pltpu.VMEM((2 * pair, width), F32)],
        compiler_params=small(),
    )(label, rows, digits)
    sends = [None] * GROUP
    for index, send in zip(ORDER, (one, two, three)):
        sends[index] = send
    return own, own_meta, *sends[1:]


def group_kernel(cent, four, three, one, two, own, own_meta, base_ref, base_meta_ref, next_ref, far_ref):
    mate = lax.axis_index("dp") % GROUP
    pair = 2 * cent
    lane = iota((1, LANES), 1)
    near = own[:cent]
    middle = own[cent:]
    far = jnp.zeros_like(near)
    counts = own_meta[0:1, :LANES] * BASE + own_meta[1:2, :LANES]
    far_counts = jnp.zeros_like(counts)
    id_digits = [own_meta[0:2, LANES:]]
    for index, got in ((1, one), (2, two), (3, three)):
        before = (mate ^ index) < mate
        first = got[:cent].astype(F32)
        near = near + jnp.where(before, first, 0.0)
        far = far + jnp.where(before, 0.0, first)
        middle = middle + got[cent:pair].astype(F32)
        meta = got[pair:, : 2 * LANES].astype(F32)
        row = meta[0:1, :LANES] * BASE + meta[1:2, :LANES]
        mask = (lane >= cent) | before
        counts = counts + jnp.where(mask, row, 0.0)
        far_counts = far_counts + jnp.where(mask, 0.0, row)
        id_digits.append(meta[0:2, LANES:])
    id_digits = jnp.concatenate(id_digits, axis=0)

    def meta_of(row):
        high, low = split_digits(row)
        digits = jnp.concatenate([high, low, jnp.zeros((META - 2, LANES), F32)], axis=0)
        return jnp.concatenate([digits, id_digits], axis=1)

    if four:
        even = even_line()
        near, far = jnp.where(even, far, near), jnp.where(even, near, far)
        counts, far_counts = (
            jnp.where(even & (lane < cent), far_counts, counts),
            jnp.where(even, counts, far_counts),
        )
    base_ref[...] = near
    base_meta_ref[...] = meta_of(counts)
    for send, sums, row in ((next_ref, middle, counts), (far_ref, far, far_counts)):
        send[:cent] = sums.astype(BF16)
        send[cent:, : 2 * LANES] = meta_of(row).astype(BF16)
        send[cent:, 2 * LANES :] = jnp.zeros((META, send.shape[1] - 2 * LANES), BF16)


def group_sums(cent, four, own, own_meta, got):
    width = own.shape[1]
    send = jax.ShapeDtypeStruct((cent + META, width), BF16)
    return pl.pallas_call(
        functools.partial(group_kernel, cent, four),
        in_specs=[whole()] * 5,
        out_specs=[whole()] * 4,
        out_shape=[
            jax.ShapeDtypeStruct((cent, width), F32),
            jax.ShapeDtypeStruct((META, 2 * LANES), F32),
            send,
            send,
        ],
        compiler_params=small(),
    )(got[2], got[0], got[1], own, own_meta)


def mean_kernel(cent, two, one, base, base_meta, mean_ref, send_ref):
    sums = base[...] + one[:cent].astype(F32) + two[:cent].astype(F32)
    metas = [meta[...].astype(F32) for meta in (base_meta, one.at[cent:], two.at[cent:])]
    rows = [meta[0:1, :LANES] * BASE + meta[1:2, :LANES] for meta in metas]
    row = rows[0] + pltpu.roll(rows[1], LANES - cent, 1) + rows[2]
    mean = (sums / as_column(row, cent)).astype(BF16)
    mean_ref[...] = mean
    send_ref[:cent] = mean
    for index, meta in enumerate(metas):
        ids = meta[:, LANES : 2 * LANES].astype(BF16)
        send_ref[cent:, index * LANES : (index + 1) * LANES] = ids
    known = len(metas) * LANES
    send_ref[cent:, known:] = jnp.zeros((META, mean.shape[1] - known), BF16)


def means(cent, base, base_meta, got):
    width = base.shape[1]
    mean = jax.ShapeDtypeStruct((cent, width), BF16)
    return pl.pallas_call(
        functools.partial(mean_kernel, cent),
        in_specs=[whole()] * 4,
        out_specs=[whole()] * 2,
        out_shape=[mean, jax.ShapeDtypeStruct((cent + META, width), BF16)],
        compiler_params=small(),
    )(got[1], got[0], base, base_meta)


def near_kernel(cent, own, got, near_ref, ids_ref):
    near_ref[:cent] = own[:cent]
    near_ref[cent:] = got[:cent]
    even = even_line()
    lane = iota((1, LANES), 1)

    def ids_of(block, steps, index):
        meta = block[cent:, steps * LANES : (steps + 1) * LANES].astype(F32)
        at = 2 * index
        return meta[at : at + 1] * BASE + meta[at + 1 : at + 2]

    near_rows, far_rows = [], []
    for index in range(GROUP):
        here, one, two = (ids_of(own, steps, index) for steps in range(3))
        three = ids_of(got, 2, index)
        near_rows.append((jnp.where(even, two, here), jnp.where(even, one, three)))
        far_rows.append((jnp.where(even, here, two), jnp.where(even, three, one)))
    rows = [
        jnp.where(lane < cent, left, pltpu.roll(right, cent, 1))
        for left, right in near_rows + far_rows
    ]
    ids_ref[...] = jnp.concatenate(rows, axis=0).astype(jnp.int32)


def near_rows(cent, own, got):
    width = own.shape[1]
    return pl.pallas_call(
        functools.partial(near_kernel, cent),
        in_specs=[whole()] * 2,
        out_specs=[whole()] * 2,
        out_shape=[
            jax.ShapeDtypeStruct((2 * cent, width), BF16),
            jax.ShapeDtypeStruct((2 * GROUP, LANES), jnp.int32),
        ],
        compiler_params=small(),
    )(own, got)


def join_kernel(second, first, out_ref):
    rows = first.shape[0]
    out_ref[:rows] = first[...]
    out_ref[rows:] = second[...]


def joined(first, second):
    rows, width = first.shape
    return pl.pallas_call(
        join_kernel,
        in_specs=[whole()] * 2,
        out_specs=whole(),
        out_shape=jax.ShapeDtypeStruct((2 * rows, width), BF16),
        cost_estimate=pl.CostEstimate(flops=100000000000, bytes_accessed=300000000, transcendentals=0),
        compiler_params=small(),
    )(second, first)


def ids_row(ids, base, order):
    low = lax.axis_index("mp") == 0
    first = ids[base + order : base + order + 1]
    if order in (0, GROUP - 1):
        return first
    other = ids[base + GROUP - 1 - order : base + GROUP - order]
    return jnp.where(low, first, other)


def gathered(ids, base, blocks):
    one_hots = [one_hot_of(K2, ids_row(ids, base, order)) for order in range(GROUP)]
    rows = [block[...] for block in blocks]
    if len(rows) == GROUP:
        rows[2:] = [jnp.concatenate(rows[2:], axis=0)]
    rows[:2] = [jnp.concatenate(rows[:2], axis=0)]
    total = None
    for index, row in enumerate(rows):
        one_hot = jnp.concatenate(one_hots[2 * index : 2 * index + 2], axis=1)
        part = jnp.dot(one_hot, row, preferred_element_type=F32)
        total = part if total is None else total + part
    return total, sum(one_hots[1:], one_hots[0])


def gather_kernel(ids, *refs):
    blocks, (sums_ref, tally_ref) = refs[:-2], refs[-2:]
    sums_ref[...], tally_ref[...] = gathered(ids, 0, blocks)


def gathered_sums(ids, blocks):
    width = blocks[0].shape[1]
    return pl.pallas_call(
        gather_kernel,
        in_specs=[whole()] * (1 + len(blocks)),
        out_specs=[whole()] * 2,
        out_shape=[
            jax.ShapeDtypeStruct((K2, width), F32),
            jax.ShapeDtypeStruct((K2, LANES), BF16),
        ],
        compiler_params=small(),
    )(ids, *blocks)


def score_kernel(owned, ids, mean, sums, tally, *refs):
    blocks, refs = refs[:-8], refs[-8:]
    mean_hbm, second_hbm, keep_ref, send_ref, values_ref, mean_ref, second_ref, sent = refs
    cent = mean.shape[0]
    first = jnp.where(even_line(), blocks[0][:cent], mean[...])
    mean_ref[...] = first
    mean_copy = pltpu.make_async_copy(mean_ref, mean_hbm, sent.at[0])
    mean_copy.start()
    total, tally_here = gathered(ids, GROUP, blocks)
    count = jnp.sum((tally[...] + tally_here).astype(F32), axis=1, keepdims=True)
    second = ((sums[...] + total) * (1.0 / count)).astype(BF16)
    values = second.astype(F32)
    values_ref[...] = values
    start = pl.multiple_of(lax.axis_index("dp") * owned, owned)
    second_ref[...] = values_ref[pl.ds(start, owned)].astype(BF16)
    second_copy = pltpu.make_async_copy(second_ref, second_hbm, sent.at[1])
    second_copy.start()
    norms = 0.5 * jnp.sum(values * values, axis=1, keepdims=True)
    row = jnp.concatenate(
        [as_row(norms[at : at + LANES]) for at in range(0, K2, LANES)], axis=1
    )
    products = lax.dot_general(
        first, second, (((1,), (1,)), ((), ())), preferred_element_type=F32
    )
    scores = products - row
    half = K2 // 2
    low = lax.axis_index("mp") == 0
    keep_ref[...] = jnp.where(low, scores[:, :half], scores[:, half:])
    send_ref[...] = jnp.where(low, scores[:, half:], scores[:, :half]).astype(BF16)
    mean_copy.wait()
    second_copy.wait()


def second_level_scores(owned, ids, mean, sums, tally, blocks):
    cent, width = mean.shape
    hbm = pl.BlockSpec(memory_space=pltpu.HBM)
    return pl.pallas_call(
        functools.partial(score_kernel, owned),
        in_specs=[whole()] * (4 + len(blocks)),
        out_specs=[hbm, hbm, whole(), whole()],
        out_shape=[
            jax.ShapeDtypeStruct((cent, width), BF16),
            jax.ShapeDtypeStruct((owned, width), BF16),
            jax.ShapeDtypeStruct((cent, K2 // 2), F32),
            jax.ShapeDtypeStruct((cent, K2 // 2), BF16),
        ],
        scratch_shapes=[
            pltpu.VMEM((K2, width), F32),
            pltpu.VMEM((cent, width), BF16),
            pltpu.VMEM((owned, width), BF16),
            pltpu.SemaphoreType.DMA((2,)),
        ],
        compiler_params=small(),
    )(ids, mean, sums, tally, *blocks)


def summed_scores(devices, second_level, first_centroids):
    second_ids = jnp.arange(K2, dtype=jnp.int32)
    group_hot = (second_level == second_ids[None, :]).astype(BF16)
    group_totals = jnp.einsum("ck,cd->kd", group_hot, first_centroids, preferred_element_type=F32)
    group_counts = jnp.sum(group_hot.astype(F32), axis=0)
    total, total_counts = lax.psum((group_totals, group_counts), "dp")
    every = (total / total_counts[:, None]).astype(BF16)
    owned = K2 // devices
    second = lax.dynamic_slice_in_dim(every, lax.axis_index("dp") * owned, owned, 0)
    values = every.astype(F32)
    products = jnp.einsum("cd,kd->ck", first_centroids, every, preferred_element_type=F32)
    partial_value = products - 0.5 * jnp.sum(values * values, axis=1)[None, :]
    scores = lax.psum_scatter(
        partial_value.astype(BF16), "mp", scatter_dimension=1, tiled=True
    ).astype(F32)
    return second, scores


def shards(embeddings, first_level, second_level):
    devices = lax.axis_size("dp")
    cores = lax.axis_size("mp")
    cent = second_level.shape[0]
    everyone = [(d, c) for d in range(devices) for c in range(cores)]

    def partner(value, index):
        return exchanged(value, [(d * cores + c, (d ^ index) * cores + c) for d, c in everyone])

    def ahead(value, steps):
        return exchanged(
            value, [(d * cores + c, (d + steps) % devices * cores + c) for d, c in everyone]
        )

    own, own_meta, *sends = band_sums(devices, cent, first_level, embeddings, second_level)
    got = [None] * GROUP
    for index in ORDER[:-1]:
        got[index] = partner(sends[index - 1], index)
    got = got[1:]
    four = devices == GROUP * GROUP and cores == 2 and devices * cent <= K2
    base, base_meta, following, far = group_sums(cent, four, own, own_meta, got)
    if four:
        got = [partner(following, GROUP), partner(far, 2 * GROUP)]
    else:
        got = [ahead(following, GROUP), ahead(far, 2 * GROUP)]
    mean, send = means(cent, base, base_meta, got)
    if not four:
        return (mean, *summed_scores(devices, second_level, mean))

    def sideways(value, steps):
        return exchanged(
            value, [(d * cores + c, (d ^ steps[c]) * cores + c) for d, c in everyone]
        )

    def plane_rows(value):
        return [value, sideways(value, (1, 2)), sideways(value, (2, 1)), partner(value, 3)]

    def relayed_rows(value):
        first = sideways(value, (1, 2))
        return [value, first, sideways(joined(value, first), (2, 1))]

    near, ids = near_rows(cent, send, partner(send, GROUP))
    far = joined(partner(mean, 2 * GROUP), partner(mean, 3 * GROUP))
    sums, tally = gathered_sums(ids, plane_rows(near))
    mean, second, keep, send = second_level_scores(
        K2 // devices, ids, mean, sums, tally, plane_rows(far)
    )
    got = exchanged(send, [(d * cores + c, d * cores + (c ^ 1)) for d, c in everyone])
    return mean, second, keep + got.astype(F32)


def solution(mesh):
    placed = (P("dp", "mp"), P("dp"), P("dp", None))
    return jax.shard_map(
        shards,
        mesh=mesh,
        in_specs=placed,
        out_specs=(P("dp", "mp"), P("dp", "mp"), P("dp", "mp")),
        check_vma=False,
    )
```

```python
import functools

import jax
import jax.numpy as jnp
from jax import lax
from jax.experimental import pallas as pl
from jax.experimental.pallas import tpu as pltpu
from jax.sharding import PartitionSpec as P

BAND = 8
K2 = 1024
GROUP = 4
META = 8
BASE = 256
LANES = 128
BF16 = jnp.bfloat16
F32 = jnp.float32


def small():
    return pltpu.CompilerParams(vmem_limit_bytes=16 * 2**20)


def whole():
    return pl.BlockSpec(memory_space=pltpu.VMEM)


def exchanged(value, pairs):
    return lax.ppermute(value, ("dp", "mp"), pairs)


def iota(shape, dim):
    return lax.broadcasted_iota(jnp.int32, shape, dim)


def even_line():
    return lax.axis_index("dp") // GROUP % 2 == 0


def split_digits(row):
    high = jnp.floor(row * (1.0 / BASE))
    return high, row - high * BASE


def as_column(row, cent):
    hit = iota((cent, LANES), 0) == iota((cent, LANES), 1)
    return jnp.sum(jnp.where(hit, row, 0.0), axis=1, keepdims=True)


def as_row(column):
    rows = column.shape[0]
    hit = iota((rows, LANES), 0) == iota((rows, LANES), 1)
    return jnp.sum(jnp.where(hit, column, 0.0), axis=0, keepdims=True)


def one_hot_of(rows, label):
    hit = lax.broadcasted_iota(jnp.int16, (rows, label.shape[1]), 0) == label.astype(jnp.int16)
    return jnp.where(hit, jnp.ones((), BF16), jnp.zeros((), BF16))


ORDER = (3, 1, 2, 0)


def divided(value, by):
    if by & (by - 1):
        return value // by
    return lax.shift_right_logical(value, jnp.full_like(value, by.bit_length() - 1))


def labelled_sums(start, labels, chunks, label_ref, rows_ref, totals, copies=None):
    tallies = jnp.zeros((labels, LANES), BF16)
    for step, (low, high) in enumerate(chunks):
        one_hot = one_hot_of(labels, label_ref[:, low:high] - start)
        for at in range(0, high - low, LANES):
            tallies = tallies + one_hot[:, at : at + LANES]
        if copies:
            copies[step].wait()
        part = jnp.dot(one_hot, rows_ref[low:high], preferred_element_type=F32)
        if step == 0:
            totals[...] = part
        else:
            totals[...] += part
    counts = lax.dot_general(
        jnp.ones((8, LANES), BF16), tallies, (((1,), (1,)), ((), ())), preferred_element_type=F32
    )
    return counts[:1]


def fill_send(send, sums, counts, id_digits):
    pair = sums.shape[0]
    cent = id_digits.shape[1]
    high, low = split_digits(counts)
    meta = jnp.concatenate([high, low, jnp.zeros((META - 2, LANES), F32)], axis=0)
    send[:pair] = sums.astype(BF16)
    send[pair:, :LANES] = meta.astype(BF16)
    send[pair:, LANES:] = jnp.zeros((META, send.shape[1] - LANES), BF16)
    send[pair : pair + 2, LANES : LANES + cent] = id_digits.astype(BF16)


def first_kernel(devices, cent, chunks, ids_hbm, rows_hbm, group_hbm, *refs):
    sends, (rows_ref, label_ref, digits_ref, ids_ref, group_ref, totals, arrived) = refs[:2], refs[2:]
    steps = len(chunks)
    ids_copy = pltpu.make_async_copy(ids_hbm, ids_ref, arrived.at[steps])
    group_copy = pltpu.make_async_copy(group_hbm, group_ref, arrived.at[steps + 1])
    copies = [
        pltpu.make_async_copy(rows_hbm.at[low:high], rows_ref.at[low:high], arrived.at[step])
        for step, (low, high) in enumerate(chunks)
    ]
    ids_copy.start()
    for copy in copies:
        copy.start()
    group_copy.start()
    position = lax.axis_index("dp")
    mate = position % GROUP
    pair = 2 * cent
    ids_copy.wait()
    offset = ids_ref[...] - position * cent
    offset = jnp.where(offset < 0, offset + devices * cent, offset)
    ahead = divided(offset, cent) + mate
    partner = (ahead & (GROUP - 1)) ^ mate
    place = jnp.zeros_like(partner)
    for index, who in enumerate(ORDER):
        place = jnp.where(partner == who, index, place)
    slot = jnp.where(divided(ahead, GROUP) == 1, cent, 0)
    label_ref[...] = place * pair + slot + offset - divided(offset, cent) * cent
    counts = labelled_sums(0, 2 * pair, chunks, label_ref, rows_ref, totals, copies)
    group_copy.wait()
    digits = jnp.concatenate(split_digits(group_ref[...].astype(F32)), axis=0)
    digits_ref[...] = digits
    for index, send in enumerate(sends):
        at = index * pair
        fill_send(send, totals[at : at + pair], counts[:, at : at + pair], digits)


def second_kernel(cent, chunks, label_ref, rows_ref, digits_ref, send, own_ref, own_meta_ref, totals):
    pair = 2 * cent
    counts = labelled_sums(2 * pair, 2 * pair, chunks, label_ref, rows_ref, totals)
    digits = digits_ref[...]
    fill_send(send, totals[:pair], counts[:, :pair], digits)
    own_ref[...] = totals[pair:]
    high, low = split_digits(counts[:, pair:])
    meta = jnp.concatenate([high, low, jnp.zeros((META - 2, LANES), F32)], axis=0)
    own_meta_ref[:, :LANES] = meta
    own_meta_ref[:, LANES:] = jnp.zeros((META, LANES), F32)
    own_meta_ref[:2, LANES : LANES + cent] = digits


def band_sums(devices, cent, ids, rows, group):
    count, width = rows.shape
    pair = 2 * cent
    send = jax.ShapeDtypeStruct((pair + META, width), BF16)
    edges = [count * part // 12 for part in (0, 3, 6, 9, 12)]
    chunks = list(zip(edges[:-1], edges[1:]))
    half = count // 2
    hbm = pl.BlockSpec(memory_space=pltpu.HBM)
    one, two, rows, label, digits = pl.pallas_call(
        functools.partial(first_kernel, devices, cent, chunks),
        in_specs=[hbm] * 3,
        out_specs=[whole()] * 5,
        out_shape=[
            send,
            send,
            jax.ShapeDtypeStruct((count, width), BF16),
            jax.ShapeDtypeStruct((1, count), jnp.int32),
            jax.ShapeDtypeStruct((2, cent), F32),
        ],
        scratch_shapes=[
            pltpu.VMEM((1, count), jnp.int32),
            pltpu.VMEM((1, cent), jnp.int32),
            pltpu.VMEM((2 * pair, width), F32),
            pltpu.SemaphoreType.DMA((len(chunks) + 2,)),
        ],
        compiler_params=small(),
    )(
        pltpu.with_memory_space_constraint(ids.reshape(1, count), pltpu.HBM),
        pltpu.with_memory_space_constraint(rows, pltpu.HBM),
        pltpu.with_memory_space_constraint(group.reshape(1, cent), pltpu.HBM),
    )
    three, own, own_meta = pl.pallas_call(
        functools.partial(second_kernel, cent, [(0, half), (half, count)]),
        in_specs=[whole()] * 3,
        out_specs=[whole()] * 3,
        out_shape=[
            send,
            jax.ShapeDtypeStruct((pair, width), F32),
            jax.ShapeDtypeStruct((META, 2 * LANES), F32),
        ],
        cost_estimate=pl.CostEstimate(flops=100000000000, bytes_accessed=300000000, transcendentals=0),
        scratch_shapes=[pltpu.VMEM((2 * pair, width), F32)],
        compiler_params=small(),
    )(label, rows, digits)
    sends = [None] * GROUP
    for index, send in zip(ORDER, (one, two, three)):
        sends[index] = send
    return own, own_meta, *sends[1:]


def group_kernel(cent, four, three, one, two, own, own_meta, base_ref, base_meta_ref, next_ref, far_ref):
    mate = lax.axis_index("dp") % GROUP
    pair = 2 * cent
    lane = iota((1, LANES), 1)
    near = own[:cent]
    middle = own[cent:]
    far = jnp.zeros_like(near)
    counts = own_meta[0:1, :LANES] * BASE + own_meta[1:2, :LANES]
    far_counts = jnp.zeros_like(counts)
    id_digits = [own_meta[0:2, LANES:]]
    for index, got in ((1, one), (2, two), (3, three)):
        before = (mate ^ index) < mate
        first = got[:cent].astype(F32)
        near = near + jnp.where(before, first, 0.0)
        far = far + jnp.where(before, 0.0, first)
        middle = middle + got[cent:pair].astype(F32)
        meta = got[pair:, : 2 * LANES].astype(F32)
        row = meta[0:1, :LANES] * BASE + meta[1:2, :LANES]
        mask = (lane >= cent) | before
        counts = counts + jnp.where(mask, row, 0.0)
        far_counts = far_counts + jnp.where(mask, 0.0, row)
        id_digits.append(meta[0:2, LANES:])
    id_digits = jnp.concatenate(id_digits, axis=0)

    def meta_of(row):
        high, low = split_digits(row)
        digits = jnp.concatenate([high, low, jnp.zeros((META - 2, LANES), F32)], axis=0)
        return jnp.concatenate([digits, id_digits], axis=1)

    if four:
        even = even_line()
        near, far = jnp.where(even, far, near), jnp.where(even, near, far)
        counts, far_counts = (
            jnp.where(even & (lane < cent), far_counts, counts),
            jnp.where(even, counts, far_counts),
        )
    base_ref[...] = near
    base_meta_ref[...] = meta_of(counts)
    for send, sums, row in ((next_ref, middle, counts), (far_ref, far, far_counts)):
        send[:cent] = sums.astype(BF16)
        send[cent:, : 2 * LANES] = meta_of(row).astype(BF16)
        send[cent:, 2 * LANES :] = jnp.zeros((META, send.shape[1] - 2 * LANES), BF16)


def group_sums(cent, four, own, own_meta, got):
    width = own.shape[1]
    send = jax.ShapeDtypeStruct((cent + META, width), BF16)
    return pl.pallas_call(
        functools.partial(group_kernel, cent, four),
        in_specs=[whole()] * 5,
        out_specs=[whole()] * 4,
        out_shape=[
            jax.ShapeDtypeStruct((cent, width), F32),
            jax.ShapeDtypeStruct((META, 2 * LANES), F32),
            send,
            send,
        ],
        compiler_params=small(),
    )(got[2], got[0], got[1], own, own_meta)


def mean_kernel(cent, two, one, base, base_meta, mean_ref, send_ref):
    sums = base[...] + one[:cent].astype(F32) + two[:cent].astype(F32)
    metas = [meta[...].astype(F32) for meta in (base_meta, one.at[cent:], two.at[cent:])]
    rows = [meta[0:1, :LANES] * BASE + meta[1:2, :LANES] for meta in metas]
    row = rows[0] + pltpu.roll(rows[1], LANES - cent, 1) + rows[2]
    mean = (sums / as_column(row, cent)).astype(BF16)
    mean_ref[...] = mean
    send_ref[:cent] = mean
    for index, meta in enumerate(metas):
        ids = meta[:, LANES : 2 * LANES].astype(BF16)
        send_ref[cent:, index * LANES : (index + 1) * LANES] = ids
    known = len(metas) * LANES
    send_ref[cent:, known:] = jnp.zeros((META, mean.shape[1] - known), BF16)


def means(cent, base, base_meta, got):
    width = base.shape[1]
    mean = jax.ShapeDtypeStruct((cent, width), BF16)
    return pl.pallas_call(
        functools.partial(mean_kernel, cent),
        in_specs=[whole()] * 4,
        out_specs=[whole()] * 2,
        out_shape=[mean, jax.ShapeDtypeStruct((cent + META, width), BF16)],
        compiler_params=small(),
    )(got[1], got[0], base, base_meta)


def near_kernel(cent, own, got, near_ref, ids_ref):
    near_ref[:cent] = own[:cent]
    near_ref[cent:] = got[:cent]
    even = even_line()
    lane = iota((1, LANES), 1)

    def ids_of(block, steps, index):
        meta = block[cent:, steps * LANES : (steps + 1) * LANES].astype(F32)
        at = 2 * index
        return meta[at : at + 1] * BASE + meta[at + 1 : at + 2]

    near_rows, far_rows = [], []
    for index in range(GROUP):
        here, one, two = (ids_of(own, steps, index) for steps in range(3))
        three = ids_of(got, 2, index)
        near_rows.append((jnp.where(even, two, here), jnp.where(even, one, three)))
        far_rows.append((jnp.where(even, here, two), jnp.where(even, three, one)))
    rows = [
        jnp.where(lane < cent, left, pltpu.roll(right, cent, 1))
        for left, right in near_rows + far_rows
    ]
    ids_ref[...] = jnp.concatenate(rows, axis=0).astype(jnp.int32)


def near_rows(cent, own, got):
    width = own.shape[1]
    return pl.pallas_call(
        functools.partial(near_kernel, cent),
        in_specs=[whole()] * 2,
        out_specs=[whole()] * 2,
        out_shape=[
            jax.ShapeDtypeStruct((2 * cent, width), BF16),
            jax.ShapeDtypeStruct((2 * GROUP, LANES), jnp.int32),
        ],
        compiler_params=small(),
    )(own, got)


def join_kernel(second, first, out_ref):
    rows = first.shape[0]
    out_ref[:rows] = first[...]
    out_ref[rows:] = second[...]


def joined(first, second):
    rows, width = first.shape
    return pl.pallas_call(
        join_kernel,
        in_specs=[whole()] * 2,
        out_specs=whole(),
        out_shape=jax.ShapeDtypeStruct((2 * rows, width), BF16),
        cost_estimate=pl.CostEstimate(flops=100000000000, bytes_accessed=300000000, transcendentals=0),
        compiler_params=small(),
    )(second, first)


def ids_row(ids, base, order):
    low = lax.axis_index("mp") == 0
    first = ids[base + order : base + order + 1]
    if order in (0, GROUP - 1):
        return first
    other = ids[base + GROUP - 1 - order : base + GROUP - order]
    return jnp.where(low, first, other)


def picked_ids(ids, pick):
    return ids_row(ids, pick // GROUP * GROUP, pick % GROUP)


def gathered(ids, picks, blocks, start, count):
    one_hots = [one_hot_of(count, picked_ids(ids, pick) - start) for pick in picks]
    total = None
    for at in range(0, len(picks), 2):
        one_hot = jnp.concatenate(one_hots[at : at + 2], axis=1)
        rows = jnp.concatenate([block[...] for block in blocks[at : at + 2]], axis=0)
        part = jnp.dot(one_hot, rows, preferred_element_type=F32)
        total = part if total is None else total + part
    return total


def gather_kernel(picks, *refs):
    blocks, (ids, mean, far, sums_ref, tally_ref, first_ref) = refs[:-6], refs[-6:]
    first_ref[...] = jnp.where(even_line(), far[: mean.shape[0]], mean[...])
    sums_ref[...] = gathered(ids, picks, blocks, 0, K2)
    tally = one_hot_of(K2, picked_ids(ids, picks[0]))
    for pick in picks[1:]:
        tally = tally + one_hot_of(K2, picked_ids(ids, pick))
    tally_ref[...] = tally


def gathered_sums(ids, mean, far, picks, blocks):
    cent, width = mean.shape
    return pl.pallas_call(
        functools.partial(gather_kernel, picks),
        in_specs=[whole()] * (3 + len(picks)),
        out_specs=[whole()] * 3,
        out_shape=[
            jax.ShapeDtypeStruct((K2, width), F32),
            jax.ShapeDtypeStruct((K2, LANES), BF16),
            jax.ShapeDtypeStruct((cent, width), BF16),
        ],
        compiler_params=small(),
    )(*[blocks[pick] for pick in picks], ids, mean, far)


def half_centroids(ids, picks, blocks, sums, tally, start):
    half = K2 // 2
    rows = pl.ds(pl.multiple_of(start, half), half)
    total = sums[rows] + gathered(ids, picks, blocks, start, half)
    count = tally[rows]
    for pick in picks:
        count = count + one_hot_of(half, picked_ids(ids, pick) - start)
    count = jnp.sum(count.astype(F32), axis=1, keepdims=True)
    return (total * (1.0 / count)).astype(BF16)


def scores_of(first, second):
    values = second.astype(F32)
    norms = 0.5 * jnp.sum(values * values, axis=1, keepdims=True)
    row = jnp.concatenate(
        [as_row(norms[at : at + LANES]) for at in range(0, second.shape[0], LANES)], axis=1
    )
    products = lax.dot_general(
        first, second, (((1,), (1,)), ((), ())), preferred_element_type=F32
    )
    return products - row


def send_kernel(picks, *refs):
    blocks, refs = refs[:-8], refs[-8:]
    ids, first, sums, tally, first_hbm, other_ref, send_ref, sent = refs
    first_copy = pltpu.make_async_copy(first, first_hbm, sent.at[0])
    first_copy.start()
    start = (1 - lax.axis_index("mp")) * (K2 // 2)
    second = half_centroids(ids, picks, blocks, sums, tally, start)
    other_ref[...] = second
    send_ref[...] = scores_of(first[...], second).astype(BF16)
    first_copy.wait()


def sent_scores(ids, first, sums, tally, picks, blocks):
    cent, width = first.shape
    half = K2 // 2
    return pl.pallas_call(
        functools.partial(send_kernel, picks),
        in_specs=[whole()] * (4 + len(picks)),
        out_specs=[pl.BlockSpec(memory_space=pltpu.HBM), whole(), whole()],
        out_shape=[
            jax.ShapeDtypeStruct((cent, width), BF16),
            jax.ShapeDtypeStruct((half, width), BF16),
            jax.ShapeDtypeStruct((cent, half), BF16),
        ],
        scratch_shapes=[pltpu.SemaphoreType.DMA((1,))],
        compiler_params=small(),
    )(*[blocks[pick] for pick in picks], ids, first, sums, tally)


def keep_kernel(owned, picks, *refs):
    blocks, refs = refs[:-10], refs[-10:]
    ids, first, sums, tally, other, second_hbm, keep_ref, every, second_ref, sent = refs
    half = K2 // 2
    core = lax.axis_index("mp")
    second = half_centroids(ids, picks, blocks, sums, tally, core * half)
    every[...] = second
    at = lax.axis_index("dp") * owned
    rows = pl.ds(pl.multiple_of(at % half, owned), owned)
    second_ref[...] = jnp.where(at // half == core, every[rows], other[rows])
    second_copy = pltpu.make_async_copy(second_ref, second_hbm, sent.at[0])
    second_copy.start()
    keep_ref[...] = scores_of(first[...], second)
    second_copy.wait()


def kept_scores(owned, ids, first, sums, tally, other, picks, blocks):
    cent, width = first.shape
    half = K2 // 2
    return pl.pallas_call(
        functools.partial(keep_kernel, owned, picks),
        in_specs=[whole()] * (5 + len(picks)),
        out_specs=[pl.BlockSpec(memory_space=pltpu.HBM), whole()],
        out_shape=[
            jax.ShapeDtypeStruct((owned, width), BF16),
            jax.ShapeDtypeStruct((cent, half), F32),
        ],
        scratch_shapes=[
            pltpu.VMEM((half, width), BF16),
            pltpu.VMEM((owned, width), BF16),
            pltpu.SemaphoreType.DMA((1,)),
        ],
        compiler_params=small(),
    )(*[blocks[pick] for pick in picks], ids, first, sums, tally, other)


def summed_scores(devices, second_level, first_centroids):
    second_ids = jnp.arange(K2, dtype=jnp.int32)
    group_hot = (second_level == second_ids[None, :]).astype(BF16)
    group_totals = jnp.einsum("ck,cd->kd", group_hot, first_centroids, preferred_element_type=F32)
    group_counts = jnp.sum(group_hot.astype(F32), axis=0)
    total, total_counts = lax.psum((group_totals, group_counts), "dp")
    every = (total / total_counts[:, None]).astype(BF16)
    owned = K2 // devices
    second = lax.dynamic_slice_in_dim(every, lax.axis_index("dp") * owned, owned, 0)
    values = every.astype(F32)
    products = jnp.einsum("cd,kd->ck", first_centroids, every, preferred_element_type=F32)
    partial_value = products - 0.5 * jnp.sum(values * values, axis=1)[None, :]
    scores = lax.psum_scatter(
        partial_value.astype(BF16), "mp", scatter_dimension=1, tiled=True
    ).astype(F32)
    return second, scores


def shards(embeddings, first_level, second_level):
    devices = lax.axis_size("dp")
    cores = lax.axis_size("mp")
    cent = second_level.shape[0]
    everyone = [(d, c) for d in range(devices) for c in range(cores)]

    def partner(value, index):
        return exchanged(value, [(d * cores + c, (d ^ index) * cores + c) for d, c in everyone])

    def ahead(value, steps):
        return exchanged(
            value, [(d * cores + c, (d + steps) % devices * cores + c) for d, c in everyone]
        )

    own, own_meta, *sends = band_sums(devices, cent, first_level, embeddings, second_level)
    got = [None] * GROUP
    for index in ORDER[:-1]:
        got[index] = partner(sends[index - 1], index)
    got = got[1:]
    four = devices == GROUP * GROUP and cores == 2 and devices * cent <= K2
    base, base_meta, following, far = group_sums(cent, four, own, own_meta, got)
    if four:
        got = [partner(following, GROUP), partner(far, 2 * GROUP)]
    else:
        got = [ahead(following, GROUP), ahead(far, 2 * GROUP)]
    mean, send = means(cent, base, base_meta, got)
    if not four:
        return (mean, *summed_scores(devices, second_level, mean))

    def sideways(value, steps):
        return exchanged(
            value, [(d * cores + c, (d ^ steps[c]) * cores + c) for d, c in everyone]
        )

    def plane_rows(value):
        return [value, sideways(value, (1, 2)), sideways(value, (2, 1)), partner(value, 3)]

    def relayed_rows(value):
        first = sideways(value, (1, 2))
        return [value, first, sideways(joined(value, first), (2, 1))]

    near, ids = near_rows(cent, send, partner(send, GROUP))
    far = joined(partner(mean, 2 * GROUP), partner(mean, 3 * GROUP))
    blocks = plane_rows(near) + plane_rows(far)
    sums, tally, first = gathered_sums(ids, mean, far, (0, 1, 2, 3, 4), blocks)
    first_out, other, send = sent_scores(ids, first, sums, tally, (5, 6, 7), blocks)
    got = exchanged(send, [(d * cores + c, d * cores + (c ^ 1)) for d, c in everyone])
    second, keep = kept_scores(K2 // devices, ids, first, sums, tally, other, (5, 6, 7), blocks)
    return first_out, second, keep + got.astype(F32)


def solution(mesh):
    placed = (P("dp", "mp"), P("dp"), P("dp", None))
    return jax.shard_map(
        shards,
        mesh=mesh,
        in_specs=placed,
        out_specs=(P("dp", "mp"), P("dp", "mp"), P("dp", "mp")),
        check_vma=False,
    )
```

```python
import functools

import jax
import jax.numpy as jnp
from jax import lax
from jax.experimental import pallas as pl
from jax.experimental.pallas import tpu as pltpu
from jax.sharding import PartitionSpec as P

BAND = 8
K2 = 1024
GROUP = 4
META = 8
BASE = 256
LANES = 128
BF16 = jnp.bfloat16
F32 = jnp.float32


def small():
    return pltpu.CompilerParams(vmem_limit_bytes=16 * 2**20)


def whole():
    return pl.BlockSpec(memory_space=pltpu.VMEM)


def exchanged(value, pairs):
    return lax.ppermute(value, ("dp", "mp"), pairs)


def iota(shape, dim):
    return lax.broadcasted_iota(jnp.int32, shape, dim)


def even_line():
    return lax.axis_index("dp") // GROUP % 2 == 0


def split_digits(row):
    high = jnp.floor(row * (1.0 / BASE))
    return high, row - high * BASE


def as_column(row, cent):
    hit = iota((cent, LANES), 0) == iota((cent, LANES), 1)
    return jnp.sum(jnp.where(hit, row, 0.0), axis=1, keepdims=True)


def as_row(column):
    rows = column.shape[0]
    hit = iota((rows, LANES), 0) == iota((rows, LANES), 1)
    return jnp.sum(jnp.where(hit, column, 0.0), axis=0, keepdims=True)


def one_hot_of(rows, label):
    hit = lax.broadcasted_iota(jnp.int16, (rows, label.shape[1]), 0) == label.astype(jnp.int16)
    return jnp.where(hit, jnp.ones((), BF16), jnp.zeros((), BF16))


ORDER = (3, 1, 2, 0)


def divided(value, by):
    if by & (by - 1):
        return value // by
    return lax.shift_right_logical(value, jnp.full_like(value, by.bit_length() - 1))


def labelled_sums(start, labels, chunks, label_ref, rows_ref, totals, copies=None):
    tallies = jnp.zeros((labels, LANES), BF16)
    for step, (low, high) in enumerate(chunks):
        one_hot = one_hot_of(labels, label_ref[:, low:high] - start)
        for at in range(0, high - low, LANES):
            tallies = tallies + one_hot[:, at : at + LANES]
        if copies:
            copies[step].wait()
        part = jnp.dot(one_hot, rows_ref[low:high], preferred_element_type=F32)
        if step == 0:
            totals[...] = part
        else:
            totals[...] += part
    counts = lax.dot_general(
        jnp.ones((8, LANES), BF16), tallies, (((1,), (1,)), ((), ())), preferred_element_type=F32
    )
    return counts[:1]


def fill_send(send, sums, counts, id_digits):
    pair = sums.shape[0]
    cent = id_digits.shape[1]
    high, low = split_digits(counts)
    meta = jnp.concatenate([high, low, jnp.zeros((META - 2, LANES), F32)], axis=0)
    send[:pair] = sums.astype(BF16)
    send[pair:, :LANES] = meta.astype(BF16)
    send[pair:, LANES:] = jnp.zeros((META, send.shape[1] - LANES), BF16)
    send[pair : pair + 2, LANES : LANES + cent] = id_digits.astype(BF16)


def first_kernel(devices, cent, chunks, ids_hbm, rows_hbm, group_hbm, *refs):
    sends, (rows_ref, label_ref, digits_ref, ids_ref, group_ref, totals, arrived) = refs[:2], refs[2:]
    steps = len(chunks)
    ids_copy = pltpu.make_async_copy(ids_hbm, ids_ref, arrived.at[steps])
    group_copy = pltpu.make_async_copy(group_hbm, group_ref, arrived.at[steps + 1])
    copies = [
        pltpu.make_async_copy(rows_hbm.at[low:high], rows_ref.at[low:high], arrived.at[step])
        for step, (low, high) in enumerate(chunks)
    ]
    ids_copy.start()
    for copy in copies:
        copy.start()
    group_copy.start()
    position = lax.axis_index("dp")
    mate = position % GROUP
    pair = 2 * cent
    ids_copy.wait()
    offset = ids_ref[...] - position * cent
    offset = jnp.where(offset < 0, offset + devices * cent, offset)
    ahead = divided(offset, cent) + mate
    partner = (ahead & (GROUP - 1)) ^ mate
    swapped = (partner > 0) & (partner < 3) & (lax.axis_index("mp") % 2 == 1)
    partner = jnp.where(swapped, 3 - partner, partner)
    place = jnp.zeros_like(partner)
    for index, who in enumerate(ORDER):
        place = jnp.where(partner == who, index, place)
    slot = jnp.where(divided(ahead, GROUP) == 1, cent, 0)
    label_ref[...] = place * pair + slot + offset - divided(offset, cent) * cent
    counts = labelled_sums(0, 2 * pair, chunks, label_ref, rows_ref, totals, copies)
    group_copy.wait()
    digits = jnp.concatenate(split_digits(group_ref[...].astype(F32)), axis=0)
    digits_ref[...] = digits
    for index, send in enumerate(sends):
        at = index * pair
        fill_send(send, totals[at : at + pair], counts[:, at : at + pair], digits)


def second_kernel(cent, chunks, label_ref, rows_ref, digits_ref, send, own_ref, own_meta_ref, totals):
    pair = 2 * cent
    counts = labelled_sums(2 * pair, 2 * pair, chunks, label_ref, rows_ref, totals)
    digits = digits_ref[...]
    fill_send(send, totals[:pair], counts[:, :pair], digits)
    own_ref[...] = totals[pair:]
    high, low = split_digits(counts[:, pair:])
    meta = jnp.concatenate([high, low, jnp.zeros((META - 2, LANES), F32)], axis=0)
    own_meta_ref[:, :LANES] = meta
    own_meta_ref[:, LANES:] = jnp.zeros((META, LANES), F32)
    own_meta_ref[:2, LANES : LANES + cent] = digits


def band_sums(devices, cent, ids, rows, group):
    count, width = rows.shape
    pair = 2 * cent
    send = jax.ShapeDtypeStruct((pair + META, width), BF16)
    edges = [count * part // 12 for part in (0, 3, 6, 9, 12)]
    chunks = list(zip(edges[:-1], edges[1:]))
    half = count // 2
    hbm = pl.BlockSpec(memory_space=pltpu.HBM)
    one, two, rows, label, digits = pl.pallas_call(
        functools.partial(first_kernel, devices, cent, chunks),
        in_specs=[hbm] * 3,
        out_specs=[whole()] * 5,
        out_shape=[
            send,
            send,
            jax.ShapeDtypeStruct((count, width), BF16),
            jax.ShapeDtypeStruct((1, count), jnp.int32),
            jax.ShapeDtypeStruct((2, cent), F32),
        ],
        scratch_shapes=[
            pltpu.VMEM((1, count), jnp.int32),
            pltpu.VMEM((1, cent), jnp.int32),
            pltpu.VMEM((2 * pair, width), F32),
            pltpu.SemaphoreType.DMA((len(chunks) + 2,)),
        ],
        compiler_params=small(),
    )(
        pltpu.with_memory_space_constraint(ids.reshape(1, count), pltpu.HBM),
        pltpu.with_memory_space_constraint(rows, pltpu.HBM),
        pltpu.with_memory_space_constraint(group.reshape(1, cent), pltpu.HBM),
    )
    three, own, own_meta = pl.pallas_call(
        functools.partial(second_kernel, cent, [(0, half), (half, count)]),
        in_specs=[whole()] * 3,
        out_specs=[whole()] * 3,
        out_shape=[
            send,
            jax.ShapeDtypeStruct((pair, width), F32),
            jax.ShapeDtypeStruct((META, 2 * LANES), F32),
        ],
        cost_estimate=pl.CostEstimate(flops=100000000000, bytes_accessed=300000000, transcendentals=0),
        scratch_shapes=[pltpu.VMEM((2 * pair, width), F32)],
        compiler_params=small(),
    )(label, rows, digits)
    sends = [None] * GROUP
    for index, send in zip(ORDER, (one, two, three)):
        sends[index] = send
    return own, own_meta, *sends[1:]


def group_kernel(cent, four, three, one, two, own, own_meta, base_ref, base_meta_ref, next_ref, far_ref):
    mate = lax.axis_index("dp") % GROUP
    pair = 2 * cent
    lane = iota((1, LANES), 1)
    near = own[:cent]
    middle = own[cent:]
    far = jnp.zeros_like(near)
    counts = own_meta[0:1, :LANES] * BASE + own_meta[1:2, :LANES]
    far_counts = jnp.zeros_like(counts)
    id_digits = [own_meta[0:2, LANES:]]
    swapped = lax.axis_index("mp") % 2 == 1
    for index, got in ((1, one), (2, two), (3, three)):
        source = index if index == 3 else jnp.where(swapped, 3 - index, index)
        before = (mate ^ source) < mate
        first = got[:cent].astype(F32)
        near = near + jnp.where(before, first, 0.0)
        far = far + jnp.where(before, 0.0, first)
        middle = middle + got[cent:pair].astype(F32)
        meta = got[pair:, : 2 * LANES].astype(F32)
        row = meta[0:1, :LANES] * BASE + meta[1:2, :LANES]
        mask = (lane >= cent) | before
        counts = counts + jnp.where(mask, row, 0.0)
        far_counts = far_counts + jnp.where(mask, 0.0, row)
        id_digits.append(meta[0:2, LANES:])
    id_digits[1], id_digits[2] = (
        jnp.where(swapped, id_digits[2], id_digits[1]),
        jnp.where(swapped, id_digits[1], id_digits[2]),
    )
    id_digits = jnp.concatenate(id_digits, axis=0)

    def meta_of(row):
        high, low = split_digits(row)
        digits = jnp.concatenate([high, low, jnp.zeros((META - 2, LANES), F32)], axis=0)
        return jnp.concatenate([digits, id_digits], axis=1)

    if four:
        even = even_line()
        near, far = jnp.where(even, far, near), jnp.where(even, near, far)
        counts, far_counts = (
            jnp.where(even & (lane < cent), far_counts, counts),
            jnp.where(even, counts, far_counts),
        )
    base_ref[...] = near
    base_meta_ref[...] = meta_of(counts)
    for send, sums, row in ((next_ref, middle, counts), (far_ref, far, far_counts)):
        send[:cent] = sums.astype(BF16)
        send[cent:, : 2 * LANES] = meta_of(row).astype(BF16)
        send[cent:, 2 * LANES :] = jnp.zeros((META, send.shape[1] - 2 * LANES), BF16)


def group_sums(cent, four, own, own_meta, got):
    width = own.shape[1]
    send = jax.ShapeDtypeStruct((cent + META, width), BF16)
    return pl.pallas_call(
        functools.partial(group_kernel, cent, four),
        in_specs=[whole()] * 5,
        out_specs=[whole()] * 4,
        out_shape=[
            jax.ShapeDtypeStruct((cent, width), F32),
            jax.ShapeDtypeStruct((META, 2 * LANES), F32),
            send,
            send,
        ],
        compiler_params=small(),
    )(got[2], got[0], got[1], own, own_meta)


def mean_kernel(cent, two, one, base, base_meta, mean_ref, send_ref):
    sums = base[...] + one[:cent].astype(F32) + two[:cent].astype(F32)
    metas = [meta[...].astype(F32) for meta in (base_meta, one.at[cent:], two.at[cent:])]
    rows = [meta[0:1, :LANES] * BASE + meta[1:2, :LANES] for meta in metas]
    row = rows[0] + pltpu.roll(rows[1], LANES - cent, 1) + rows[2]
    mean = (sums / as_column(row, cent)).astype(BF16)
    mean_ref[...] = mean
    send_ref[:cent] = mean
    for index, meta in enumerate(metas):
        ids = meta[:, LANES : 2 * LANES].astype(BF16)
        send_ref[cent:, index * LANES : (index + 1) * LANES] = ids
    known = len(metas) * LANES
    send_ref[cent:, known:] = jnp.zeros((META, mean.shape[1] - known), BF16)


def means(cent, base, base_meta, got):
    width = base.shape[1]
    mean = jax.ShapeDtypeStruct((cent, width), BF16)
    return pl.pallas_call(
        functools.partial(mean_kernel, cent),
        in_specs=[whole()] * 4,
        out_specs=[whole()] * 2,
        out_shape=[mean, jax.ShapeDtypeStruct((cent + META, width), BF16)],
        compiler_params=small(),
    )(got[1], got[0], base, base_meta)


def near_kernel(cent, own, got, near_ref, ids_ref):
    near_ref[:cent] = own[:cent]
    near_ref[cent:] = got[:cent]
    even = even_line()
    lane = iota((1, LANES), 1)

    def ids_of(block, steps, index):
        meta = block[cent:, steps * LANES : (steps + 1) * LANES].astype(F32)
        at = 2 * index
        return meta[at : at + 1] * BASE + meta[at + 1 : at + 2]

    near_rows, far_rows = [], []
    for index in range(GROUP):
        here, one, two = (ids_of(own, steps, index) for steps in range(3))
        three = ids_of(got, 2, index)
        near_rows.append((jnp.where(even, two, here), jnp.where(even, one, three)))
        far_rows.append((jnp.where(even, here, two), jnp.where(even, three, one)))
    rows = [
        jnp.where(lane < cent, left, pltpu.roll(right, cent, 1))
        for left, right in near_rows + far_rows
    ]
    ids_ref[...] = jnp.concatenate(rows, axis=0).astype(jnp.int32)


def near_rows(cent, own, got):
    width = own.shape[1]
    return pl.pallas_call(
        functools.partial(near_kernel, cent),
        in_specs=[whole()] * 2,
        out_specs=[whole()] * 2,
        out_shape=[
            jax.ShapeDtypeStruct((2 * cent, width), BF16),
            jax.ShapeDtypeStruct((2 * GROUP, LANES), jnp.int32),
        ],
        compiler_params=small(),
    )(own, got)


def join_kernel(second, first, out_ref):
    rows = first.shape[0]
    out_ref[:rows] = first[...]
    out_ref[rows:] = second[...]


def joined(first, second):
    rows, width = first.shape
    return pl.pallas_call(
        join_kernel,
        in_specs=[whole()] * 2,
        out_specs=whole(),
        out_shape=jax.ShapeDtypeStruct((2 * rows, width), BF16),
        cost_estimate=pl.CostEstimate(flops=100000000000, bytes_accessed=300000000, transcendentals=0),
        compiler_params=small(),
    )(second, first)


def ids_row(ids, base, order):
    low = lax.axis_index("mp") == 0
    first = ids[base + order : base + order + 1]
    if order in (0, GROUP - 1):
        return first
    other = ids[base + GROUP - 1 - order : base + GROUP - order]
    return jnp.where(low, first, other)


def picked_ids(ids, pick):
    return ids_row(ids, pick // GROUP * GROUP, pick % GROUP)


def gathered(ids, picks, blocks, start, count):
    one_hots = [one_hot_of(count, picked_ids(ids, pick) - start) for pick in picks]
    total = None
    for at in range(0, len(picks), 2):
        one_hot = jnp.concatenate(one_hots[at : at + 2], axis=1)
        rows = jnp.concatenate([block[...] for block in blocks[at : at + 2]], axis=0)
        part = jnp.dot(one_hot, rows, preferred_element_type=F32)
        total = part if total is None else total + part
    return total


def gather_kernel(picks, *refs):
    blocks, refs = refs[:-8], refs[-8:]
    ids, mean, far, sums_ref, scale_ref, first_ref, first_hbm, sent = refs
    first_ref[...] = jnp.where(even_line(), far[: mean.shape[0]], mean[...])
    first_copy = pltpu.make_async_copy(first_ref, first_hbm, sent.at[0])
    first_copy.start()
    sums_ref[...] = gathered(ids, picks, blocks, 0, K2)
    tally = one_hot_of(K2, ids[0:1])
    for row in range(1, 2 * GROUP):
        tally = tally + one_hot_of(K2, ids[row : row + 1])
    count = jnp.sum(tally.astype(F32), axis=1, keepdims=True)
    scale_ref[...] = jnp.broadcast_to(1.0 / count, scale_ref.shape)
    first_copy.wait()


def gathered_sums(ids, mean, far, picks, blocks):
    cent, width = mean.shape
    return pl.pallas_call(
        functools.partial(gather_kernel, picks),
        in_specs=[whole()] * (3 + len(picks)),
        out_specs=[whole()] * 3 + [pl.BlockSpec(memory_space=pltpu.HBM)],
        out_shape=[
            jax.ShapeDtypeStruct((K2, width), F32),
            jax.ShapeDtypeStruct((K2, LANES), F32),
            jax.ShapeDtypeStruct((cent, width), BF16),
            jax.ShapeDtypeStruct((cent, width), BF16),
        ],
        scratch_shapes=[pltpu.SemaphoreType.DMA((1,))],
        compiler_params=small(),
    )(*[blocks[pick] for pick in picks], ids, mean, far)


def half_centroids(ids, picks, blocks, sums, scale, start):
    half = K2 // 2
    rows = pl.ds(pl.multiple_of(start, half), half)
    total = sums[rows] + gathered(ids, picks, blocks, start, half)
    factor = scale[rows]
    parts = [total[:, at : at + LANES] * factor for at in range(0, total.shape[1], LANES)]
    return jnp.concatenate(parts, axis=1).astype(BF16)


def scores_of(first, second):
    values = second.astype(F32)
    norms = 0.5 * jnp.sum(values * values, axis=1, keepdims=True)
    row = jnp.concatenate(
        [as_row(norms[at : at + LANES]) for at in range(0, second.shape[0], LANES)], axis=1
    )
    products = lax.dot_general(
        first, second, (((1,), (1,)), ((), ())), preferred_element_type=F32
    )
    return products - row


def send_kernel(picks, *refs):
    blocks, refs = refs[:-6], refs[-6:]
    ids, first, sums, scale, other_ref, send_ref = refs
    start = (1 - lax.axis_index("mp")) * (K2 // 2)
    second = half_centroids(ids, picks, blocks, sums, scale, start)
    other_ref[...] = second
    send_ref[...] = scores_of(first[...], second).astype(BF16)


def sent_scores(ids, first, sums, scale, picks, blocks):
    cent, width = first.shape
    half = K2 // 2
    return pl.pallas_call(
        functools.partial(send_kernel, picks),
        in_specs=[whole()] * (4 + len(picks)),
        out_specs=[whole()] * 2,
        out_shape=[
            jax.ShapeDtypeStruct((half, width), BF16),
            jax.ShapeDtypeStruct((cent, half), BF16),
        ],
        compiler_params=small(),
    )(*[blocks[pick] for pick in picks], ids, first, sums, scale)


def keep_kernel(owned, picks, *refs):
    blocks, refs = refs[:-10], refs[-10:]
    ids, first, sums, scale, other, second_hbm, keep_ref, every, second_ref, sent = refs
    half = K2 // 2
    core = lax.axis_index("mp")
    second = half_centroids(ids, picks, blocks, sums, scale, core * half)
    every[...] = second
    at = lax.axis_index("dp") * owned
    rows = pl.ds(pl.multiple_of(at % half, owned), owned)
    second_ref[...] = jnp.where(at // half == core, every[rows], other[rows])
    second_copy = pltpu.make_async_copy(second_ref, second_hbm, sent.at[0])
    second_copy.start()
    keep_ref[...] = scores_of(first[...], second)
    second_copy.wait()


def kept_scores(owned, ids, first, sums, scale, other, picks, blocks):
    cent, width = first.shape
    half = K2 // 2
    return pl.pallas_call(
        functools.partial(keep_kernel, owned, picks),
        in_specs=[whole()] * (5 + len(picks)),
        out_specs=[pl.BlockSpec(memory_space=pltpu.HBM), whole()],
        out_shape=[
            jax.ShapeDtypeStruct((owned, width), BF16),
            jax.ShapeDtypeStruct((cent, half), F32),
        ],
        scratch_shapes=[
            pltpu.VMEM((half, width), BF16),
            pltpu.VMEM((owned, width), BF16),
            pltpu.SemaphoreType.DMA((1,)),
        ],
        compiler_params=small(),
    )(*[blocks[pick] for pick in picks], ids, first, sums, scale, other)


def summed_scores(devices, second_level, first_centroids):
    second_ids = jnp.arange(K2, dtype=jnp.int32)
    group_hot = (second_level == second_ids[None, :]).astype(BF16)
    group_totals = jnp.einsum("ck,cd->kd", group_hot, first_centroids, preferred_element_type=F32)
    group_counts = jnp.sum(group_hot.astype(F32), axis=0)
    total, total_counts = lax.psum((group_totals, group_counts), "dp")
    every = (total / total_counts[:, None]).astype(BF16)
    owned = K2 // devices
    second = lax.dynamic_slice_in_dim(every, lax.axis_index("dp") * owned, owned, 0)
    values = every.astype(F32)
    products = jnp.einsum("cd,kd->ck", first_centroids, every, preferred_element_type=F32)
    partial_value = products - 0.5 * jnp.sum(values * values, axis=1)[None, :]
    scores = lax.psum_scatter(
        partial_value.astype(BF16), "mp", scatter_dimension=1, tiled=True
    ).astype(F32)
    return second, scores


def shards(embeddings, first_level, second_level):
    devices = lax.axis_size("dp")
    cores = lax.axis_size("mp")
    cent = second_level.shape[0]
    everyone = [(d, c) for d in range(devices) for c in range(cores)]

    def partner(value, index):
        return exchanged(value, [(d * cores + c, (d ^ index) * cores + c) for d, c in everyone])

    def sideways(value, steps):
        return exchanged(
            value, [(d * cores + c, (d ^ steps[c % 2]) * cores + c) for d, c in everyone]
        )

    def ahead(value, steps):
        return exchanged(
            value, [(d * cores + c, (d + steps) % devices * cores + c) for d, c in everyone]
        )

    own, own_meta, *sends = band_sums(devices, cent, first_level, embeddings, second_level)
    turns = ((1, 2), (2, 1), (3, 3))
    got = [None] * GROUP
    for index in ORDER[:-1]:
        got[index] = sideways(sends[index - 1], turns[index - 1])
    got = got[1:]
    four = devices == GROUP * GROUP and cores == 2 and devices * cent <= K2
    base, base_meta, following, far = group_sums(cent, four, own, own_meta, got)
    if four:
        got = [partner(following, GROUP), partner(far, 2 * GROUP)]
    else:
        got = [ahead(following, GROUP), ahead(far, 2 * GROUP)]
    mean, send = means(cent, base, base_meta, got)
    if not four:
        return (mean, *summed_scores(devices, second_level, mean))

    def plane_rows(value):
        return [value, sideways(value, (1, 2)), sideways(value, (2, 1)), partner(value, 3)]

    def relayed_rows(value):
        first = sideways(value, (1, 2))
        return [value, first, sideways(joined(value, first), (2, 1))]

    near, ids = near_rows(cent, send, partner(send, GROUP))
    far = joined(partner(mean, 2 * GROUP), partner(mean, 3 * GROUP))
    blocks = plane_rows(near) + plane_rows(far)
    sums, scale, first, first_out = gathered_sums(ids, mean, far, (0, 1, 2, 3, 4), blocks)
    other, send = sent_scores(ids, first, sums, scale, (5, 6, 7), blocks)
    got = exchanged(send, [(d * cores + c, d * cores + (c ^ 1)) for d, c in everyone])
    second, keep = kept_scores(K2 // devices, ids, first, sums, scale, other, (5, 6, 7), blocks)
    return first_out, second, keep + got.astype(F32)


def solution(mesh):
    placed = (P("dp", "mp"), P("dp"), P("dp", None))
    return jax.shard_map(
        shards,
        mesh=mesh,
        in_specs=placed,
        out_specs=(P("dp", "mp"), P("dp", "mp"), P("dp", "mp")),
        check_vma=False,
    )
```

```python
import functools

import jax
import jax.numpy as jnp
from jax import lax
from jax.experimental import pallas as pl
from jax.experimental.pallas import tpu as pltpu
from jax.sharding import PartitionSpec as P

BAND = 8
K2 = 1024
GROUP = 4
META = 16
BASE = 256
LANES = 128
BF16 = jnp.bfloat16
F32 = jnp.float32


def small():
    return pltpu.CompilerParams(vmem_limit_bytes=16 * 2**20)


def whole():
    return pl.BlockSpec(memory_space=pltpu.VMEM)


def exchanged(value, pairs):
    return lax.ppermute(value, ("dp", "mp"), pairs)


def iota(shape, dim):
    return lax.broadcasted_iota(jnp.int32, shape, dim)


def even_line():
    return lax.axis_index("dp") // GROUP % 2 == 0


def split_digits(row):
    high = jnp.floor(row * (1.0 / BASE))
    return high, row - high * BASE


def as_column(row, cent):
    hit = iota((cent, LANES), 0) == iota((cent, LANES), 1)
    return jnp.sum(jnp.where(hit, row, 0.0), axis=1, keepdims=True)


def as_row(column):
    rows = column.shape[0]
    hit = iota((rows, LANES), 0) == iota((rows, LANES), 1)
    return jnp.sum(jnp.where(hit, column, 0.0), axis=0, keepdims=True)


def one_hot_of(rows, label):
    hit = lax.broadcasted_iota(jnp.int16, (rows, label.shape[1]), 0) == label.astype(jnp.int16)
    return jnp.where(hit, jnp.ones((), BF16), jnp.zeros((), BF16))


ORDER = (3, 1, 2, 0)


def divided(value, by):
    if by & (by - 1):
        return value // by
    return lax.shift_right_logical(value, jnp.full_like(value, by.bit_length() - 1))


def labelled_sums(start, labels, chunks, label_ref, rows_ref, totals, copies=None):
    tallies = jnp.zeros((labels, LANES), BF16)
    for step, (low, high) in enumerate(chunks):
        one_hot = one_hot_of(labels, label_ref[:, low:high] - start)
        for at in range(0, high - low, LANES):
            tallies = tallies + one_hot[:, at : at + LANES]
        if copies:
            copies[step].wait()
        part = jnp.dot(one_hot, rows_ref[low:high], preferred_element_type=F32)
        if step == 0:
            totals[...] = part
        else:
            totals[...] += part
    counts = lax.dot_general(
        jnp.ones((8, LANES), BF16), tallies, (((1,), (1,)), ((), ())), preferred_element_type=F32
    )
    return counts[:1]


def fill_send(send, sums, counts, id_digits):
    pair = sums.shape[0]
    cent = id_digits.shape[1]
    high, low = split_digits(counts)
    meta = jnp.concatenate([high, low, jnp.zeros((META - 2, LANES), F32)], axis=0)
    send[:pair] = sums.astype(BF16)
    send[pair:, :LANES] = meta.astype(BF16)
    send[pair:, LANES:] = jnp.zeros((META, send.shape[1] - LANES), BF16)
    send[pair : pair + 2, LANES : LANES + cent] = id_digits.astype(BF16)


def first_kernel(devices, cent, chunks, ids_hbm, rows_hbm, group_hbm, *refs):
    sends, (rows_ref, label_ref, digits_ref, ids_ref, group_ref, totals, arrived) = refs[:2], refs[2:]
    steps = len(chunks)
    ids_copy = pltpu.make_async_copy(ids_hbm, ids_ref, arrived.at[steps])
    group_copy = pltpu.make_async_copy(group_hbm, group_ref, arrived.at[steps + 1])
    copies = [
        pltpu.make_async_copy(rows_hbm.at[low:high], rows_ref.at[low:high], arrived.at[step])
        for step, (low, high) in enumerate(chunks)
    ]
    ids_copy.start()
    for copy in copies:
        copy.start()
    group_copy.start()
    position = lax.axis_index("dp")
    mate = position % GROUP
    pair = 2 * cent
    ids_copy.wait()
    offset = ids_ref[...] - position * cent
    offset = jnp.where(offset < 0, offset + devices * cent, offset)
    ahead = divided(offset, cent) + mate
    partner = (ahead & (GROUP - 1)) ^ mate
    swapped = (partner > 0) & (partner < 3) & (lax.axis_index("mp") % 2 == 1)
    partner = jnp.where(swapped, 3 - partner, partner)
    place = jnp.zeros_like(partner)
    for index, who in enumerate(ORDER):
        place = jnp.where(partner == who, index, place)
    slot = jnp.where(divided(ahead, GROUP) == 1, cent, 0)
    label_ref[...] = place * pair + slot + offset - divided(offset, cent) * cent
    counts = labelled_sums(0, 2 * pair, chunks, label_ref, rows_ref, totals, copies)
    group_copy.wait()
    digits = jnp.concatenate(split_digits(group_ref[...].astype(F32)), axis=0)
    digits_ref[...] = digits
    for index, send in enumerate(sends):
        at = index * pair
        fill_send(send, totals[at : at + pair], counts[:, at : at + pair], digits)


def second_kernel(cent, chunks, label_ref, rows_ref, digits_ref, send, own_ref, own_meta_ref, totals):
    pair = 2 * cent
    counts = labelled_sums(2 * pair, 2 * pair, chunks, label_ref, rows_ref, totals)
    digits = digits_ref[...]
    fill_send(send, totals[:pair], counts[:, :pair], digits)
    own_ref[...] = totals[pair:]
    high, low = split_digits(counts[:, pair:])
    meta = jnp.concatenate([high, low, jnp.zeros((META - 2, LANES), F32)], axis=0)
    own_meta_ref[:, :LANES] = meta
    own_meta_ref[:, LANES:] = jnp.zeros((META, LANES), F32)
    own_meta_ref[:2, LANES : LANES + cent] = digits


def band_sums(devices, cent, ids, rows, group):
    count, width = rows.shape
    pair = 2 * cent
    send = jax.ShapeDtypeStruct((pair + META, width), BF16)
    edges = [count * part // 12 for part in (0, 3, 6, 9, 12)]
    chunks = list(zip(edges[:-1], edges[1:]))
    half = count // 2
    hbm = pl.BlockSpec(memory_space=pltpu.HBM)
    one, two, rows, label, digits = pl.pallas_call(
        functools.partial(first_kernel, devices, cent, chunks),
        in_specs=[hbm] * 3,
        out_specs=[whole()] * 5,
        out_shape=[
            send,
            send,
            jax.ShapeDtypeStruct((count, width), BF16),
            jax.ShapeDtypeStruct((1, count), jnp.int32),
            jax.ShapeDtypeStruct((2, cent), F32),
        ],
        scratch_shapes=[
            pltpu.VMEM((1, count), jnp.int32),
            pltpu.VMEM((1, cent), jnp.int32),
            pltpu.VMEM((2 * pair, width), F32),
            pltpu.SemaphoreType.DMA((len(chunks) + 2,)),
        ],
        compiler_params=small(),
    )(
        pltpu.with_memory_space_constraint(ids.reshape(1, count), pltpu.HBM),
        pltpu.with_memory_space_constraint(rows, pltpu.HBM),
        pltpu.with_memory_space_constraint(group.reshape(1, cent), pltpu.HBM),
    )
    three, own, own_meta = pl.pallas_call(
        functools.partial(second_kernel, cent, [(0, half), (half, count)]),
        in_specs=[whole()] * 3,
        out_specs=[whole()] * 3,
        out_shape=[
            send,
            jax.ShapeDtypeStruct((pair, width), F32),
            jax.ShapeDtypeStruct((META, 2 * LANES), F32),
        ],
        cost_estimate=pl.CostEstimate(flops=100000000000, bytes_accessed=300000000, transcendentals=0),
        scratch_shapes=[pltpu.VMEM((2 * pair, width), F32)],
        compiler_params=small(),
    )(label, rows, digits)
    sends = [None] * GROUP
    for index, send in zip(ORDER, (one, two, three)):
        sends[index] = send
    return own, own_meta, *sends[1:]


def group_kernel(cent, four, three, one, two, own, own_meta, base_ref, base_meta_ref, next_ref, far_ref):
    mate = lax.axis_index("dp") % GROUP
    pair = 2 * cent
    lane = iota((1, LANES), 1)
    near = own[:cent]
    middle = own[cent:]
    far = jnp.zeros_like(near)
    counts = own_meta[0:1, :LANES] * BASE + own_meta[1:2, :LANES]
    far_counts = jnp.zeros_like(counts)
    id_digits = [own_meta[0:2, LANES:]]
    swapped = lax.axis_index("mp") % 2 == 1
    for index, got in ((1, one), (2, two), (3, three)):
        source = index if index == 3 else jnp.where(swapped, 3 - index, index)
        before = (mate ^ source) < mate
        first = got[:cent].astype(F32)
        near = near + jnp.where(before, first, 0.0)
        far = far + jnp.where(before, 0.0, first)
        middle = middle + got[cent:pair].astype(F32)
        meta = got[pair:, : 2 * LANES].astype(F32)
        row = meta[0:1, :LANES] * BASE + meta[1:2, :LANES]
        mask = (lane >= cent) | before
        counts = counts + jnp.where(mask, row, 0.0)
        far_counts = far_counts + jnp.where(mask, 0.0, row)
        id_digits.append(meta[0:2, LANES:])
    id_digits[1], id_digits[2] = (
        jnp.where(swapped, id_digits[2], id_digits[1]),
        jnp.where(swapped, id_digits[1], id_digits[2]),
    )
    id_digits.append(jnp.zeros((META - 2 * GROUP, LANES), F32))
    id_digits = jnp.concatenate(id_digits, axis=0)

    def meta_of(row):
        high, low = split_digits(row)
        digits = jnp.concatenate([high, low, jnp.zeros((META - 2, LANES), F32)], axis=0)
        return jnp.concatenate([digits, id_digits], axis=1)

    if four:
        even = even_line()
        near, far = jnp.where(even, far, near), jnp.where(even, near, far)
        counts, far_counts = (
            jnp.where(even & (lane < cent), far_counts, counts),
            jnp.where(even, counts, far_counts),
        )
    base_ref[...] = near
    base_meta_ref[...] = meta_of(counts)
    for send, sums, row in ((next_ref, middle, counts), (far_ref, far, far_counts)):
        send[:cent] = sums.astype(BF16)
        send[cent:, : 2 * LANES] = meta_of(row).astype(BF16)
        send[cent:, 2 * LANES :] = jnp.zeros((META, send.shape[1] - 2 * LANES), BF16)


def group_sums(cent, four, own, own_meta, got):
    width = own.shape[1]
    send = jax.ShapeDtypeStruct((cent + META, width), BF16)
    return pl.pallas_call(
        functools.partial(group_kernel, cent, four),
        in_specs=[whole()] * 5,
        out_specs=[whole()] * 4,
        out_shape=[
            jax.ShapeDtypeStruct((cent, width), F32),
            jax.ShapeDtypeStruct((META, 2 * LANES), F32),
            send,
            send,
        ],
        compiler_params=small(),
    )(got[2], got[0], got[1], own, own_meta)


def mean_kernel(cent, two, one, base, base_meta, mean_ref, send_ref):
    sums = base[...] + one[:cent].astype(F32) + two[:cent].astype(F32)
    metas = [meta[...].astype(F32) for meta in (base_meta, one.at[cent:], two.at[cent:])]
    rows = [meta[0:1, :LANES] * BASE + meta[1:2, :LANES] for meta in metas]
    row = rows[0] + pltpu.roll(rows[1], LANES - cent, 1) + rows[2]
    mean = (sums / as_column(row, cent)).astype(BF16)
    mean_ref[...] = mean
    send_ref[:cent] = mean
    for index, meta in enumerate(metas):
        ids = meta[:, LANES : 2 * LANES].astype(BF16)
        send_ref[cent:, index * LANES : (index + 1) * LANES] = ids
    known = len(metas) * LANES
    send_ref[cent:, known:] = jnp.zeros((META, mean.shape[1] - known), BF16)


def means(cent, base, base_meta, got):
    width = base.shape[1]
    mean = jax.ShapeDtypeStruct((cent, width), BF16)
    return pl.pallas_call(
        functools.partial(mean_kernel, cent),
        in_specs=[whole()] * 4,
        out_specs=[whole()] * 2,
        out_shape=[mean, jax.ShapeDtypeStruct((cent + META, width), BF16)],
        compiler_params=small(),
    )(got[1], got[0], base, base_meta)


def near_kernel(cent, own, got, near_ref, ids_ref):
    near_ref[:cent] = own[:cent]
    near_ref[cent:] = got[:cent]
    even = even_line()
    lane = iota((1, LANES), 1)

    def ids_of(block, steps, index):
        meta = block[cent:, steps * LANES : (steps + 1) * LANES].astype(F32)
        at = 2 * index
        return meta[at : at + 1] * BASE + meta[at + 1 : at + 2]

    near_rows, far_rows = [], []
    for index in range(GROUP):
        here, one, two = (ids_of(own, steps, index) for steps in range(3))
        three = ids_of(got, 2, index)
        near_rows.append((jnp.where(even, two, here), jnp.where(even, one, three)))
        far_rows.append((jnp.where(even, here, two), jnp.where(even, three, one)))
    rows = [
        jnp.where(lane < cent, left, pltpu.roll(right, cent, 1))
        for left, right in near_rows + far_rows
    ]
    ids_ref[...] = jnp.concatenate(rows, axis=0).astype(jnp.int32)


def near_rows(cent, own, got):
    width = own.shape[1]
    return pl.pallas_call(
        functools.partial(near_kernel, cent),
        in_specs=[whole()] * 2,
        out_specs=[whole()] * 2,
        out_shape=[
            jax.ShapeDtypeStruct((2 * cent, width), BF16),
            jax.ShapeDtypeStruct((2 * GROUP, LANES), jnp.int32),
        ],
        compiler_params=small(),
    )(own, got)


def join_kernel(second, first, out_ref):
    rows = first.shape[0]
    out_ref[:rows] = first[...]
    out_ref[rows:] = second[...]


def joined(first, second):
    rows, width = first.shape
    return pl.pallas_call(
        join_kernel,
        in_specs=[whole()] * 2,
        out_specs=whole(),
        out_shape=jax.ShapeDtypeStruct((2 * rows, width), BF16),
        cost_estimate=pl.CostEstimate(flops=100000000000, bytes_accessed=300000000, transcendentals=0),
        compiler_params=small(),
    )(second, first)


def ids_row(ids, base, order):
    low = lax.axis_index("mp") == 0
    first = ids[base + order : base + order + 1]
    if order in (0, GROUP - 1):
        return first
    other = ids[base + GROUP - 1 - order : base + GROUP - order]
    return jnp.where(low, first, other)


def picked_ids(ids, pick):
    return ids_row(ids, pick // GROUP * GROUP, pick % GROUP)


def gathered(ids, picks, blocks, start, count):
    one_hots = [one_hot_of(count, picked_ids(ids, pick) - start) for pick in picks]
    total = None
    for at in range(0, len(picks), 2):
        one_hot = jnp.concatenate(one_hots[at : at + 2], axis=1)
        rows = jnp.concatenate([block[...] for block in blocks[at : at + 2]], axis=0)
        part = jnp.dot(one_hot, rows, preferred_element_type=F32)
        total = part if total is None else total + part
    return total


def gather_kernel(picks, *refs):
    blocks, refs = refs[:-8], refs[-8:]
    ids, mean, far, sums_ref, scale_ref, first_ref, first_hbm, sent = refs
    first_ref[...] = jnp.where(even_line(), far[: mean.shape[0]], mean[...])
    first_copy = pltpu.make_async_copy(first_ref, first_hbm, sent.at[0])
    first_copy.start()
    sums_ref[...] = gathered(ids, picks, blocks, 0, K2)
    tally = one_hot_of(K2, ids[0:1])
    for row in range(1, 2 * GROUP):
        tally = tally + one_hot_of(K2, ids[row : row + 1])
    count = jnp.sum(tally.astype(F32), axis=1, keepdims=True)
    scale_ref[...] = jnp.broadcast_to(1.0 / count, scale_ref.shape)
    first_copy.wait()


def gathered_sums(ids, mean, far, picks, blocks):
    cent, width = mean.shape
    return pl.pallas_call(
        functools.partial(gather_kernel, picks),
        in_specs=[whole()] * (3 + len(picks)),
        out_specs=[whole()] * 3 + [pl.BlockSpec(memory_space=pltpu.HBM)],
        out_shape=[
            jax.ShapeDtypeStruct((K2, width), F32),
            jax.ShapeDtypeStruct((K2, LANES), F32),
            jax.ShapeDtypeStruct((cent, width), BF16),
            jax.ShapeDtypeStruct((cent, width), BF16),
        ],
        scratch_shapes=[pltpu.SemaphoreType.DMA((1,))],
        compiler_params=small(),
    )(*[blocks[pick] for pick in picks], ids, mean, far)


def half_centroids(ids, picks, blocks, sums, scale, start):
    half = K2 // 2
    rows = pl.ds(pl.multiple_of(start, half), half)
    total = sums[rows] + gathered(ids, picks, blocks, start, half)
    factor = scale[rows]
    parts = [total[:, at : at + LANES] * factor for at in range(0, total.shape[1], LANES)]
    return jnp.concatenate(parts, axis=1).astype(BF16)


def scores_of(first, second):
    values = second.astype(F32)
    norms = 0.5 * jnp.sum(values * values, axis=1, keepdims=True)
    row = jnp.concatenate(
        [as_row(norms[at : at + LANES]) for at in range(0, second.shape[0], LANES)], axis=1
    )
    products = lax.dot_general(
        first, second, (((1,), (1,)), ((), ())), preferred_element_type=F32
    )
    return products - row


def send_kernel(picks, *refs):
    blocks, refs = refs[:-6], refs[-6:]
    ids, first, sums, scale, other_ref, send_ref = refs
    start = (1 - lax.axis_index("mp")) * (K2 // 2)
    second = half_centroids(ids, picks, blocks, sums, scale, start)
    other_ref[...] = second
    send_ref[...] = scores_of(first[...], second).astype(BF16)


def sent_scores(ids, first, sums, scale, picks, blocks):
    cent, width = first.shape
    half = K2 // 2
    return pl.pallas_call(
        functools.partial(send_kernel, picks),
        in_specs=[whole()] * (4 + len(picks)),
        out_specs=[whole()] * 2,
        out_shape=[
            jax.ShapeDtypeStruct((half, width), BF16),
            jax.ShapeDtypeStruct((cent, half), BF16),
        ],
        compiler_params=small(),
    )(*[blocks[pick] for pick in picks], ids, first, sums, scale)


def keep_kernel(owned, picks, *refs):
    blocks, refs = refs[:-10], refs[-10:]
    ids, first, sums, scale, other, second_hbm, keep_ref, every, second_ref, sent = refs
    half = K2 // 2
    core = lax.axis_index("mp")
    second = half_centroids(ids, picks, blocks, sums, scale, core * half)
    every[...] = second
    at = lax.axis_index("dp") * owned
    rows = pl.ds(pl.multiple_of(at % half, owned), owned)
    second_ref[...] = jnp.where(at // half == core, every[rows], other[rows])
    second_copy = pltpu.make_async_copy(second_ref, second_hbm, sent.at[0])
    second_copy.start()
    keep_ref[...] = scores_of(first[...], second)
    second_copy.wait()


def kept_scores(owned, ids, first, sums, scale, other, picks, blocks):
    cent, width = first.shape
    half = K2 // 2
    return pl.pallas_call(
        functools.partial(keep_kernel, owned, picks),
        in_specs=[whole()] * (5 + len(picks)),
        out_specs=[pl.BlockSpec(memory_space=pltpu.HBM), whole()],
        out_shape=[
            jax.ShapeDtypeStruct((owned, width), BF16),
            jax.ShapeDtypeStruct((cent, half), F32),
        ],
        scratch_shapes=[
            pltpu.VMEM((half, width), BF16),
            pltpu.VMEM((owned, width), BF16),
            pltpu.SemaphoreType.DMA((1,)),
        ],
        compiler_params=small(),
    )(*[blocks[pick] for pick in picks], ids, first, sums, scale, other)


def summed_scores(devices, second_level, first_centroids):
    second_ids = jnp.arange(K2, dtype=jnp.int32)
    group_hot = (second_level == second_ids[None, :]).astype(BF16)
    group_totals = jnp.einsum("ck,cd->kd", group_hot, first_centroids, preferred_element_type=F32)
    group_counts = jnp.sum(group_hot.astype(F32), axis=0)
    total, total_counts = lax.psum((group_totals, group_counts), "dp")
    every = (total / total_counts[:, None]).astype(BF16)
    owned = K2 // devices
    second = lax.dynamic_slice_in_dim(every, lax.axis_index("dp") * owned, owned, 0)
    values = every.astype(F32)
    products = jnp.einsum("cd,kd->ck", first_centroids, every, preferred_element_type=F32)
    partial_value = products - 0.5 * jnp.sum(values * values, axis=1)[None, :]
    scores = lax.psum_scatter(
        partial_value.astype(BF16), "mp", scatter_dimension=1, tiled=True
    ).astype(F32)
    return second, scores


def shards(embeddings, first_level, second_level):
    devices = lax.axis_size("dp")
    cores = lax.axis_size("mp")
    cent = second_level.shape[0]
    everyone = [(d, c) for d in range(devices) for c in range(cores)]

    def partner(value, index):
        return exchanged(value, [(d * cores + c, (d ^ index) * cores + c) for d, c in everyone])

    def sideways(value, steps):
        return exchanged(
            value, [(d * cores + c, (d ^ steps[c % 2]) * cores + c) for d, c in everyone]
        )

    def ahead(value, steps):
        return exchanged(
            value, [(d * cores + c, (d + steps) % devices * cores + c) for d, c in everyone]
        )

    own, own_meta, *sends = band_sums(devices, cent, first_level, embeddings, second_level)
    turns = ((1, 2), (2, 1), (3, 3))
    got = [None] * GROUP
    for index in ORDER[:-1]:
        got[index] = sideways(sends[index - 1], turns[index - 1])
    got = got[1:]
    four = devices == GROUP * GROUP and cores == 2 and devices * cent <= K2
    base, base_meta, following, far = group_sums(cent, four, own, own_meta, got)
    if four:
        got = [partner(following, GROUP), partner(far, 2 * GROUP)]
    else:
        got = [ahead(following, GROUP), ahead(far, 2 * GROUP)]
    mean, send = means(cent, base, base_meta, got)
    if not four:
        return (mean, *summed_scores(devices, second_level, mean))

    def plane_rows(value):
        return [value, sideways(value, (1, 2)), sideways(value, (2, 1)), partner(value, 3)]

    def relayed_rows(value):
        first = sideways(value, (1, 2))
        return [value, first, sideways(joined(value, first), (2, 1))]

    near, ids = near_rows(cent, send, partner(send, GROUP))
    far = joined(partner(mean, 2 * GROUP), partner(mean, 3 * GROUP))
    blocks = plane_rows(near) + plane_rows(far)
    sums, scale, first, first_out = gathered_sums(ids, mean, far, (0, 1, 2, 3, 4), blocks)
    other, send = sent_scores(ids, first, sums, scale, (5, 6, 7), blocks)
    got = exchanged(send, [(d * cores + c, d * cores + (c ^ 1)) for d, c in everyone])
    second, keep = kept_scores(K2 // devices, ids, first, sums, scale, other, (5, 6, 7), blocks)
    return first_out, second, keep + got.astype(F32)


def solution(mesh):
    placed = (P("dp", "mp"), P("dp"), P("dp", None))
    return jax.shard_map(
        shards,
        mesh=mesh,
        in_specs=placed,
        out_specs=(P("dp", "mp"), P("dp", "mp"), P("dp", "mp")),
        check_vma=False,
    )
```

```python
import functools

import jax
import jax.numpy as jnp
from jax import lax
from jax.experimental import pallas as pl
from jax.experimental.pallas import tpu as pltpu
from jax.sharding import PartitionSpec as P

BAND = 8
K2 = 1024
GROUP = 4
META = 8
BASE = 256
LANES = 128
BF16 = jnp.bfloat16
F32 = jnp.float32


def small():
    return pltpu.CompilerParams(vmem_limit_bytes=16 * 2**20)


def whole():
    return pl.BlockSpec(memory_space=pltpu.VMEM)


def exchanged(value, pairs):
    return lax.ppermute(value, ("dp", "mp"), pairs)


def iota(shape, dim):
    return lax.broadcasted_iota(jnp.int32, shape, dim)


def even_line():
    return lax.axis_index("dp") // GROUP % 2 == 0


def split_digits(row):
    high = jnp.floor(row * (1.0 / BASE))
    return high, row - high * BASE


def as_column(row, cent):
    hit = iota((cent, LANES), 0) == iota((cent, LANES), 1)
    return jnp.sum(jnp.where(hit, row, 0.0), axis=1, keepdims=True)


def as_row(column):
    rows = column.shape[0]
    hit = iota((rows, LANES), 0) == iota((rows, LANES), 1)
    return jnp.sum(jnp.where(hit, column, 0.0), axis=0, keepdims=True)


def one_hot_of(rows, label):
    hit = lax.broadcasted_iota(jnp.int16, (rows, label.shape[1]), 0) == label.astype(jnp.int16)
    return jnp.where(hit, jnp.ones((), BF16), jnp.zeros((), BF16))


ORDER = (3, 1, 2, 0)


def divided(value, by):
    if by & (by - 1):
        return value // by
    return lax.shift_right_logical(value, jnp.full_like(value, by.bit_length() - 1))


def labelled_sums(start, labels, chunks, label_ref, rows_ref, totals, copies=None):
    tallies = jnp.zeros((labels, LANES), BF16)
    for step, (low, high) in enumerate(chunks):
        one_hot = one_hot_of(labels, label_ref[:, low:high] - start)
        for at in range(0, high - low, LANES):
            tallies = tallies + one_hot[:, at : at + LANES]
        if copies:
            copies[step].wait()
        part = jnp.dot(one_hot, rows_ref[low:high], preferred_element_type=F32)
        if step == 0:
            totals[...] = part
        else:
            totals[...] += part
    counts = lax.dot_general(
        jnp.ones((8, LANES), BF16), tallies, (((1,), (1,)), ((), ())), preferred_element_type=F32
    )
    return counts[:1]


def fill_send(send, sums, counts, id_digits):
    pair = sums.shape[0]
    cent = id_digits.shape[1]
    high, low = split_digits(counts)
    meta = jnp.concatenate([high, low, jnp.zeros((META - 2, LANES), F32)], axis=0)
    send[:pair] = sums.astype(BF16)
    send[pair:, :LANES] = meta.astype(BF16)
    send[pair:, LANES:] = jnp.zeros((META, send.shape[1] - LANES), BF16)
    send[pair : pair + 2, LANES : LANES + cent] = id_digits.astype(BF16)


def first_kernel(devices, cent, chunks, ids_hbm, rows_hbm, group_hbm, *refs):
    sends, (rows_ref, label_ref, digits_ref, ids_ref, group_ref, totals, arrived) = refs[:2], refs[2:]
    steps = len(chunks)
    ids_copy = pltpu.make_async_copy(ids_hbm, ids_ref, arrived.at[steps])
    group_copy = pltpu.make_async_copy(group_hbm, group_ref, arrived.at[steps + 1])
    copies = [
        pltpu.make_async_copy(rows_hbm.at[low:high], rows_ref.at[low:high], arrived.at[step])
        for step, (low, high) in enumerate(chunks)
    ]
    ids_copy.start()
    for copy in copies:
        copy.start()
    group_copy.start()
    position = lax.axis_index("dp")
    mate = position % GROUP
    pair = 2 * cent
    ids_copy.wait()
    offset = ids_ref[...] - position * cent
    offset = jnp.where(offset < 0, offset + devices * cent, offset)
    ahead = divided(offset, cent) + mate
    partner = (ahead & (GROUP - 1)) ^ mate
    swapped = (partner > 0) & (partner < 3) & (lax.axis_index("mp") % 2 == 1)
    partner = jnp.where(swapped, 3 - partner, partner)
    place = jnp.zeros_like(partner)
    for index, who in enumerate(ORDER):
        place = jnp.where(partner == who, index, place)
    slot = jnp.where(divided(ahead, GROUP) == 1, cent, 0)
    label_ref[...] = place * pair + slot + offset - divided(offset, cent) * cent
    counts = labelled_sums(0, 2 * pair, chunks, label_ref, rows_ref, totals, copies)
    group_copy.wait()
    digits = jnp.concatenate(split_digits(group_ref[...].astype(F32)), axis=0)
    digits_ref[...] = digits
    for index, send in enumerate(sends):
        at = index * pair
        fill_send(send, totals[at : at + pair], counts[:, at : at + pair], digits)


def second_kernel(cent, chunks, label_ref, rows_ref, digits_ref, send, own_ref, own_meta_ref, totals):
    pair = 2 * cent
    counts = labelled_sums(2 * pair, 2 * pair, chunks, label_ref, rows_ref, totals)
    digits = digits_ref[...]
    fill_send(send, totals[:pair], counts[:, :pair], digits)
    own_ref[...] = totals[pair:]
    high, low = split_digits(counts[:, pair:])
    meta = jnp.concatenate([high, low, jnp.zeros((META - 2, LANES), F32)], axis=0)
    own_meta_ref[:, :LANES] = meta
    own_meta_ref[:, LANES:] = jnp.zeros((META, LANES), F32)
    own_meta_ref[:2, LANES : LANES + cent] = digits


def band_sums(devices, cent, ids, rows, group):
    count, width = rows.shape
    pair = 2 * cent
    send = jax.ShapeDtypeStruct((pair + META, width), BF16)
    edges = [count * part // 12 for part in (0, 3, 6, 9, 12)]
    chunks = list(zip(edges[:-1], edges[1:]))
    half = count // 2
    hbm = pl.BlockSpec(memory_space=pltpu.HBM)
    one, two, rows, label, digits = pl.pallas_call(
        functools.partial(first_kernel, devices, cent, chunks),
        in_specs=[hbm] * 3,
        out_specs=[whole()] * 5,
        out_shape=[
            send,
            send,
            jax.ShapeDtypeStruct((count, width), BF16),
            jax.ShapeDtypeStruct((1, count), jnp.int32),
            jax.ShapeDtypeStruct((2, cent), F32),
        ],
        scratch_shapes=[
            pltpu.VMEM((1, count), jnp.int32),
            pltpu.VMEM((1, cent), jnp.int32),
            pltpu.VMEM((2 * pair, width), F32),
            pltpu.SemaphoreType.DMA((len(chunks) + 2,)),
        ],
        compiler_params=small(),
    )(
        pltpu.with_memory_space_constraint(ids.reshape(1, count), pltpu.HBM),
        pltpu.with_memory_space_constraint(rows, pltpu.HBM),
        pltpu.with_memory_space_constraint(group.reshape(1, cent), pltpu.HBM),
    )
    three, own, own_meta = pl.pallas_call(
        functools.partial(second_kernel, cent, [(0, half), (half, count)]),
        in_specs=[whole()] * 3,
        out_specs=[whole()] * 3,
        out_shape=[
            send,
            jax.ShapeDtypeStruct((pair, width), F32),
            jax.ShapeDtypeStruct((META, 2 * LANES), F32),
        ],
        cost_estimate=pl.CostEstimate(flops=100000000000, bytes_accessed=300000000, transcendentals=0),
        scratch_shapes=[pltpu.VMEM((2 * pair, width), F32)],
        compiler_params=small(),
    )(label, rows, digits)
    sends = [None] * GROUP
    for index, send in zip(ORDER, (one, two, three)):
        sends[index] = send
    return own, own_meta, *sends[1:]


def group_kernel(cent, four, three, one, two, own, own_meta, base_ref, base_meta_ref, next_ref, far_ref):
    mate = lax.axis_index("dp") % GROUP
    pair = 2 * cent
    lane = iota((1, LANES), 1)
    near = own[:cent]
    middle = own[cent:]
    far = jnp.zeros_like(near)
    counts = own_meta[0:1, :LANES] * BASE + own_meta[1:2, :LANES]
    far_counts = jnp.zeros_like(counts)
    id_digits = [own_meta[0:2, LANES:]]
    swapped = lax.axis_index("mp") % 2 == 1
    for index, got in ((1, one), (2, two), (3, three)):
        source = index if index == 3 else jnp.where(swapped, 3 - index, index)
        before = (mate ^ source) < mate
        first = got[:cent].astype(F32)
        near = near + jnp.where(before, first, 0.0)
        far = far + jnp.where(before, 0.0, first)
        middle = middle + got[cent:pair].astype(F32)
        meta = got[pair:, : 2 * LANES].astype(F32)
        row = meta[0:1, :LANES] * BASE + meta[1:2, :LANES]
        mask = (lane >= cent) | before
        counts = counts + jnp.where(mask, row, 0.0)
        far_counts = far_counts + jnp.where(mask, 0.0, row)
        id_digits.append(meta[0:2, LANES:])
    id_digits[1], id_digits[2] = (
        jnp.where(swapped, id_digits[2], id_digits[1]),
        jnp.where(swapped, id_digits[1], id_digits[2]),
    )
    id_digits = jnp.concatenate(id_digits, axis=0)

    def meta_of(row):
        high, low = split_digits(row)
        digits = jnp.concatenate([high, low, jnp.zeros((META - 2, LANES), F32)], axis=0)
        return jnp.concatenate([digits, id_digits], axis=1)

    if four:
        even = even_line()
        near, far = jnp.where(even, far, near), jnp.where(even, near, far)
        counts, far_counts = (
            jnp.where(even & (lane < cent), far_counts, counts),
            jnp.where(even, counts, far_counts),
        )
    base_ref[...] = near
    base_meta_ref[...] = meta_of(counts)
    next_counts = counts
    if four:
        swapped = lax.axis_index("mp") % 2 == 0
        middle, far = jnp.where(swapped, far, middle), jnp.where(swapped, middle, far)
        next_counts, far_counts = (
            jnp.where(swapped, far_counts, counts),
            jnp.where(swapped, counts, far_counts),
        )
    for send, sums, row in ((next_ref, middle, next_counts), (far_ref, far, far_counts)):
        send[:cent] = sums.astype(BF16)
        send[cent:, : 2 * LANES] = meta_of(row).astype(BF16)
        send[cent:, 2 * LANES :] = jnp.zeros((META, send.shape[1] - 2 * LANES), BF16)


def group_sums(cent, four, own, own_meta, got):
    width = own.shape[1]
    send = jax.ShapeDtypeStruct((cent + META, width), BF16)
    return pl.pallas_call(
        functools.partial(group_kernel, cent, four),
        in_specs=[whole()] * 5,
        out_specs=[whole()] * 4,
        out_shape=[
            jax.ShapeDtypeStruct((cent, width), F32),
            jax.ShapeDtypeStruct((META, 2 * LANES), F32),
            send,
            send,
        ],
        compiler_params=small(),
    )(got[2], got[0], got[1], own, own_meta)


def mean_kernel(cent, four, two, one, base, base_meta, mean_ref, send_ref):
    sums = base[...] + one[:cent].astype(F32) + two[:cent].astype(F32)
    metas = [meta[...].astype(F32) for meta in (base_meta, one.at[cent:], two.at[cent:])]
    if four:
        swapped = lax.axis_index("mp") % 2 == 0
        metas[1:] = [
            jnp.where(swapped, metas[2], metas[1]),
            jnp.where(swapped, metas[1], metas[2]),
        ]
    rows = [meta[0:1, :LANES] * BASE + meta[1:2, :LANES] for meta in metas]
    row = rows[0] + pltpu.roll(rows[1], LANES - cent, 1) + rows[2]
    mean = (sums / as_column(row, cent)).astype(BF16)
    mean_ref[...] = mean
    send_ref[:cent] = mean
    for index, meta in enumerate(metas):
        ids = meta[:, LANES : 2 * LANES].astype(BF16)
        send_ref[cent:, index * LANES : (index + 1) * LANES] = ids
    known = len(metas) * LANES
    send_ref[cent:, known:] = jnp.zeros((META, mean.shape[1] - known), BF16)


def means(cent, four, base, base_meta, got):
    width = base.shape[1]
    mean = jax.ShapeDtypeStruct((cent, width), BF16)
    return pl.pallas_call(
        functools.partial(mean_kernel, cent, four),
        in_specs=[whole()] * 4,
        out_specs=[whole()] * 2,
        out_shape=[mean, jax.ShapeDtypeStruct((cent + META, width), BF16)],
        compiler_params=small(),
    )(got[1], got[0], base, base_meta)


def near_kernel(cent, own, got, near_ref, ids_ref):
    near_ref[:cent] = own[:cent]
    near_ref[cent:] = got[:cent]
    even = even_line()
    lane = iota((1, LANES), 1)

    def ids_of(block, steps, index):
        meta = block[cent:, steps * LANES : (steps + 1) * LANES].astype(F32)
        at = 2 * index
        return meta[at : at + 1] * BASE + meta[at + 1 : at + 2]

    near_rows, far_rows = [], []
    for index in range(GROUP):
        here, one, two = (ids_of(own, steps, index) for steps in range(3))
        three = ids_of(got, 2, index)
        near_rows.append((jnp.where(even, two, here), jnp.where(even, one, three)))
        far_rows.append((jnp.where(even, here, two), jnp.where(even, three, one)))
    rows = [
        jnp.where(lane < cent, left, pltpu.roll(right, cent, 1))
        for left, right in near_rows + far_rows
    ]
    ids_ref[...] = jnp.concatenate(rows, axis=0).astype(jnp.int32)


def near_rows(cent, own, got):
    width = own.shape[1]
    return pl.pallas_call(
        functools.partial(near_kernel, cent),
        in_specs=[whole()] * 2,
        out_specs=[whole()] * 2,
        out_shape=[
            jax.ShapeDtypeStruct((2 * cent, width), BF16),
            jax.ShapeDtypeStruct((2 * GROUP, LANES), jnp.int32),
        ],
        compiler_params=small(),
    )(own, got)


def join_kernel(second, first, out_ref):
    rows = first.shape[0]
    out_ref[:rows] = first[...]
    out_ref[rows:] = second[...]


def joined(first, second):
    rows, width = first.shape
    return pl.pallas_call(
        join_kernel,
        in_specs=[whole()] * 2,
        out_specs=whole(),
        out_shape=jax.ShapeDtypeStruct((2 * rows, width), BF16),
        cost_estimate=pl.CostEstimate(flops=100000000000, bytes_accessed=300000000, transcendentals=0),
        compiler_params=small(),
    )(second, first)


def ids_row(ids, base, order):
    low = lax.axis_index("mp") == 0
    first = ids[base + order : base + order + 1]
    if order in (0, GROUP - 1):
        return first
    other = ids[base + GROUP - 1 - order : base + GROUP - order]
    return jnp.where(low, first, other)


def picked_ids(ids, pick):
    return ids_row(ids, pick // GROUP * GROUP, pick % GROUP)


def gathered(ids, picks, blocks, start, count):
    one_hots = [one_hot_of(count, picked_ids(ids, pick) - start) for pick in picks]
    total = None
    for at in range(0, len(picks), 2):
        one_hot = jnp.concatenate(one_hots[at : at + 2], axis=1)
        rows = jnp.concatenate([block[...] for block in blocks[at : at + 2]], axis=0)
        part = jnp.dot(one_hot, rows, preferred_element_type=F32)
        total = part if total is None else total + part
    return total


def gather_kernel(picks, *refs):
    blocks, refs = refs[:-8], refs[-8:]
    ids, mean, far, sums_ref, scale_ref, first_ref, first_hbm, sent = refs
    first_ref[...] = jnp.where(even_line(), far[: mean.shape[0]], mean[...])
    first_copy = pltpu.make_async_copy(first_ref, first_hbm, sent.at[0])
    first_copy.start()
    sums_ref[...] = gathered(ids, picks, blocks, 0, K2)
    tally = one_hot_of(K2, ids[0:1])
    for row in range(1, 2 * GROUP):
        tally = tally + one_hot_of(K2, ids[row : row + 1])
    count = jnp.sum(tally.astype(F32), axis=1, keepdims=True)
    scale_ref[...] = jnp.broadcast_to(1.0 / count, scale_ref.shape)
    first_copy.wait()


def gathered_sums(ids, mean, far, picks, blocks):
    cent, width = mean.shape
    return pl.pallas_call(
        functools.partial(gather_kernel, picks),
        in_specs=[whole()] * (3 + len(picks)),
        out_specs=[whole()] * 3 + [pl.BlockSpec(memory_space=pltpu.HBM)],
        out_shape=[
            jax.ShapeDtypeStruct((K2, width), F32),
            jax.ShapeDtypeStruct((K2, LANES), F32),
            jax.ShapeDtypeStruct((cent, width), BF16),
            jax.ShapeDtypeStruct((cent, width), BF16),
        ],
        scratch_shapes=[pltpu.SemaphoreType.DMA((1,))],
        compiler_params=small(),
    )(*[blocks[pick] for pick in picks], ids, mean, far)


def half_centroids(ids, picks, blocks, sums, scale, start):
    half = K2 // 2
    rows = pl.ds(pl.multiple_of(start, half), half)
    total = sums[rows] + gathered(ids, picks, blocks, start, half)
    factor = scale[rows]
    parts = [total[:, at : at + LANES] * factor for at in range(0, total.shape[1], LANES)]
    return jnp.concatenate(parts, axis=1).astype(BF16)


def scores_of(first, second):
    values = second.astype(F32)
    norms = 0.5 * jnp.sum(values * values, axis=1, keepdims=True)
    row = jnp.concatenate(
        [as_row(norms[at : at + LANES]) for at in range(0, second.shape[0], LANES)], axis=1
    )
    products = lax.dot_general(
        first, second, (((1,), (1,)), ((), ())), preferred_element_type=F32
    )
    return products - row


def send_kernel(picks, *refs):
    blocks, refs = refs[:-6], refs[-6:]
    ids, first, sums, scale, other_ref, send_ref = refs
    start = (1 - lax.axis_index("mp")) * (K2 // 2)
    second = half_centroids(ids, picks, blocks, sums, scale, start)
    other_ref[...] = second
    send_ref[...] = scores_of(first[...], second).astype(BF16)


def sent_scores(ids, first, sums, scale, picks, blocks):
    cent, width = first.shape
    half = K2 // 2
    return pl.pallas_call(
        functools.partial(send_kernel, picks),
        in_specs=[whole()] * (4 + len(picks)),
        out_specs=[whole()] * 2,
        out_shape=[
            jax.ShapeDtypeStruct((half, width), BF16),
            jax.ShapeDtypeStruct((cent, half), BF16),
        ],
        compiler_params=small(),
    )(*[blocks[pick] for pick in picks], ids, first, sums, scale)


def keep_kernel(owned, picks, *refs):
    blocks, refs = refs[:-10], refs[-10:]
    ids, first, sums, scale, other, second_hbm, keep_ref, every, second_ref, sent = refs
    half = K2 // 2
    core = lax.axis_index("mp")
    second = half_centroids(ids, picks, blocks, sums, scale, core * half)
    every[...] = second
    at = lax.axis_index("dp") * owned
    rows = pl.ds(pl.multiple_of(at % half, owned), owned)
    second_ref[...] = jnp.where(at // half == core, every[rows], other[rows])
    second_copy = pltpu.make_async_copy(second_ref, second_hbm, sent.at[0])
    second_copy.start()
    keep_ref[...] = scores_of(first[...], second)
    second_copy.wait()


def kept_scores(owned, ids, first, sums, scale, other, picks, blocks):
    cent, width = first.shape
    half = K2 // 2
    return pl.pallas_call(
        functools.partial(keep_kernel, owned, picks),
        in_specs=[whole()] * (5 + len(picks)),
        out_specs=[pl.BlockSpec(memory_space=pltpu.HBM), whole()],
        out_shape=[
            jax.ShapeDtypeStruct((owned, width), BF16),
            jax.ShapeDtypeStruct((cent, half), F32),
        ],
        scratch_shapes=[
            pltpu.VMEM((half, width), BF16),
            pltpu.VMEM((owned, width), BF16),
            pltpu.SemaphoreType.DMA((1,)),
        ],
        compiler_params=small(),
    )(*[blocks[pick] for pick in picks], ids, first, sums, scale, other)


def summed_scores(devices, second_level, first_centroids):
    second_ids = jnp.arange(K2, dtype=jnp.int32)
    group_hot = (second_level == second_ids[None, :]).astype(BF16)
    group_totals = jnp.einsum("ck,cd->kd", group_hot, first_centroids, preferred_element_type=F32)
    group_counts = jnp.sum(group_hot.astype(F32), axis=0)
    total, total_counts = lax.psum((group_totals, group_counts), "dp")
    every = (total / total_counts[:, None]).astype(BF16)
    owned = K2 // devices
    second = lax.dynamic_slice_in_dim(every, lax.axis_index("dp") * owned, owned, 0)
    values = every.astype(F32)
    products = jnp.einsum("cd,kd->ck", first_centroids, every, preferred_element_type=F32)
    partial_value = products - 0.5 * jnp.sum(values * values, axis=1)[None, :]
    scores = lax.psum_scatter(
        partial_value.astype(BF16), "mp", scatter_dimension=1, tiled=True
    ).astype(F32)
    return second, scores


def shards(embeddings, first_level, second_level):
    devices = lax.axis_size("dp")
    cores = lax.axis_size("mp")
    cent = second_level.shape[0]
    everyone = [(d, c) for d in range(devices) for c in range(cores)]

    def partner(value, index):
        return exchanged(value, [(d * cores + c, (d ^ index) * cores + c) for d, c in everyone])

    def sideways(value, steps):
        return exchanged(
            value, [(d * cores + c, (d ^ steps[c % 2]) * cores + c) for d, c in everyone]
        )

    def ahead(value, steps):
        return exchanged(
            value, [(d * cores + c, (d + steps) % devices * cores + c) for d, c in everyone]
        )

    own, own_meta, *sends = band_sums(devices, cent, first_level, embeddings, second_level)
    turns = ((1, 2), (2, 1), (3, 3))
    got = [None] * GROUP
    for index in ORDER[:-1]:
        got[index] = sideways(sends[index - 1], turns[index - 1])
    got = got[1:]
    four = devices == GROUP * GROUP and cores == 2 and devices * cent <= K2
    base, base_meta, following, far = group_sums(cent, four, own, own_meta, got)
    if four:
        turns = ((2 * GROUP, GROUP), (GROUP, 2 * GROUP))
        got = [sideways(following, turns[0]), sideways(far, turns[1])]
    else:
        got = [ahead(following, GROUP), ahead(far, 2 * GROUP)]
    mean, send = means(cent, four, base, base_meta, got)
    if not four:
        return (mean, *summed_scores(devices, second_level, mean))

    def plane_rows(value):
        return [value, sideways(value, (1, 2)), sideways(value, (2, 1)), partner(value, 3)]

    def relayed_rows(value):
        first = sideways(value, (1, 2))
        return [value, first, sideways(joined(value, first), (2, 1))]

    near, ids = near_rows(cent, send, partner(send, GROUP))
    far = joined(partner(mean, 2 * GROUP), partner(mean, 3 * GROUP))
    blocks = plane_rows(near) + plane_rows(far)
    sums, scale, first, first_out = gathered_sums(ids, mean, far, (0, 1, 2, 3, 4), blocks)
    other, send = sent_scores(ids, first, sums, scale, (5, 6, 7), blocks)
    got = exchanged(send, [(d * cores + c, d * cores + (c ^ 1)) for d, c in everyone])
    second, keep = kept_scores(K2 // devices, ids, first, sums, scale, other, (5, 6, 7), blocks)
    return first_out, second, keep + got.astype(F32)


def solution(mesh):
    placed = (P("dp", "mp"), P("dp"), P("dp", None))
    return jax.shard_map(
        shards,
        mesh=mesh,
        in_specs=placed,
        out_specs=(P("dp", "mp"), P("dp", "mp"), P("dp", "mp")),
        check_vma=False,
    )
```

```python
import functools

import jax
import jax.numpy as jnp
from jax import lax
from jax.experimental import pallas as pl
from jax.experimental.pallas import tpu as pltpu
from jax.sharding import PartitionSpec as P

BAND = 8
K2 = 1024
GROUP = 4
META = 8
BASE = 256
LANES = 128
BF16 = jnp.bfloat16
F32 = jnp.float32


def small():
    return pltpu.CompilerParams(vmem_limit_bytes=16 * 2**20)


def whole():
    return pl.BlockSpec(memory_space=pltpu.VMEM)


def exchanged(value, pairs):
    return lax.ppermute(value, ("dp", "mp"), pairs)


def iota(shape, dim):
    return lax.broadcasted_iota(jnp.int32, shape, dim)


def even_line():
    return lax.axis_index("dp") // GROUP % 2 == 0


def split_digits(row):
    high = jnp.floor(row * (1.0 / BASE))
    return high, row - high * BASE


def as_column(row, cent):
    hit = iota((cent, LANES), 0) == iota((cent, LANES), 1)
    return jnp.sum(jnp.where(hit, row, 0.0), axis=1, keepdims=True)


def as_row(column):
    rows = column.shape[0]
    hit = iota((rows, LANES), 0) == iota((rows, LANES), 1)
    return jnp.sum(jnp.where(hit, column, 0.0), axis=0, keepdims=True)


def one_hot_of(rows, label):
    hit = lax.broadcasted_iota(jnp.int16, (rows, label.shape[1]), 0) == label.astype(jnp.int16)
    return jnp.where(hit, jnp.ones((), BF16), jnp.zeros((), BF16))


ORDER = (3, 1, 2, 0)


def divided(value, by):
    if by & (by - 1):
        return value // by
    return lax.shift_right_logical(value, jnp.full_like(value, by.bit_length() - 1))


def labelled_sums(start, labels, chunks, label_ref, rows_ref, totals, copies=None):
    tallies = jnp.zeros((labels, LANES), BF16)
    for step, (low, high) in enumerate(chunks):
        one_hot = one_hot_of(labels, label_ref[:, low:high] - start)
        for at in range(0, high - low, LANES):
            tallies = tallies + one_hot[:, at : at + LANES]
        if copies:
            copies[step].wait()
        part = jnp.dot(one_hot, rows_ref[low:high], preferred_element_type=F32)
        if step == 0:
            totals[...] = part
        else:
            totals[...] += part
    counts = lax.dot_general(
        jnp.ones((8, LANES), BF16), tallies, (((1,), (1,)), ((), ())), preferred_element_type=F32
    )
    return counts[:1]


def fill_send(send, sums, counts, id_digits):
    pair = sums.shape[0]
    cent = id_digits.shape[1]
    high, low = split_digits(counts)
    meta = jnp.concatenate([high, low, jnp.zeros((META - 2, LANES), F32)], axis=0)
    send[:pair] = sums.astype(BF16)
    send[pair:, :LANES] = meta.astype(BF16)
    send[pair:, LANES:] = jnp.zeros((META, send.shape[1] - LANES), BF16)
    send[pair : pair + 2, LANES : LANES + cent] = id_digits.astype(BF16)


def first_kernel(devices, cent, chunks, ids_hbm, rows_hbm, group_hbm, *refs):
    sends, (rows_ref, label_ref, digits_ref, ids_ref, group_ref, totals, arrived) = refs[:2], refs[2:]
    steps = len(chunks)
    ids_copy = pltpu.make_async_copy(ids_hbm, ids_ref, arrived.at[steps])
    group_copy = pltpu.make_async_copy(group_hbm, group_ref, arrived.at[steps + 1])
    copies = [
        pltpu.make_async_copy(rows_hbm.at[low:high], rows_ref.at[low:high], arrived.at[step])
        for step, (low, high) in enumerate(chunks)
    ]
    ids_copy.start()
    for copy in copies:
        copy.start()
    group_copy.start()
    position = lax.axis_index("dp")
    mate = position % GROUP
    pair = 2 * cent
    ids_copy.wait()
    offset = ids_ref[...] - position * cent
    offset = jnp.where(offset < 0, offset + devices * cent, offset)
    ahead = divided(offset, cent) + mate
    partner = (ahead & (GROUP - 1)) ^ mate
    swapped = (partner > 0) & (partner < 3) & (lax.axis_index("mp") % 2 == 1)
    partner = jnp.where(swapped, 3 - partner, partner)
    place = jnp.zeros_like(partner)
    for index, who in enumerate(ORDER):
        place = jnp.where(partner == who, index, place)
    slot = jnp.where(divided(ahead, GROUP) == 1, cent, 0)
    label_ref[...] = place * pair + slot + offset - divided(offset, cent) * cent
    counts = labelled_sums(0, 2 * pair, chunks, label_ref, rows_ref, totals, copies)
    group_copy.wait()
    digits = jnp.concatenate(split_digits(group_ref[...].astype(F32)), axis=0)
    digits_ref[...] = digits
    for index, send in enumerate(sends):
        at = index * pair
        fill_send(send, totals[at : at + pair], counts[:, at : at + pair], digits)


def second_kernel(cent, chunks, label_ref, rows_ref, digits_ref, send, own_ref, own_meta_ref, totals):
    pair = 2 * cent
    counts = labelled_sums(2 * pair, 2 * pair, chunks, label_ref, rows_ref, totals)
    digits = digits_ref[...]
    fill_send(send, totals[:pair], counts[:, :pair], digits)
    own_ref[...] = totals[pair:]
    high, low = split_digits(counts[:, pair:])
    meta = jnp.concatenate([high, low, jnp.zeros((META - 2, LANES), F32)], axis=0)
    own_meta_ref[:, :LANES] = meta
    own_meta_ref[:, LANES:] = jnp.zeros((META, LANES), F32)
    own_meta_ref[:2, LANES : LANES + cent] = digits


def band_sums(devices, cent, ids, rows, group):
    count, width = rows.shape
    pair = 2 * cent
    send = jax.ShapeDtypeStruct((pair + META, width), BF16)
    edges = [count * part // 12 for part in (0, 2, 4, 6, 8, 10, 12)]
    chunks = list(zip(edges[:-1], edges[1:]))
    half = count // 2
    hbm = pl.BlockSpec(memory_space=pltpu.HBM)
    one, two, rows, label, digits = pl.pallas_call(
        functools.partial(first_kernel, devices, cent, chunks),
        in_specs=[hbm] * 3,
        out_specs=[whole()] * 5,
        out_shape=[
            send,
            send,
            jax.ShapeDtypeStruct((count, width), BF16),
            jax.ShapeDtypeStruct((1, count), jnp.int32),
            jax.ShapeDtypeStruct((2, cent), F32),
        ],
        scratch_shapes=[
            pltpu.VMEM((1, count), jnp.int32),
            pltpu.VMEM((1, cent), jnp.int32),
            pltpu.VMEM((2 * pair, width), F32),
            pltpu.SemaphoreType.DMA((len(chunks) + 2,)),
        ],
        compiler_params=small(),
    )(
        pltpu.with_memory_space_constraint(ids.reshape(1, count), pltpu.HBM),
        pltpu.with_memory_space_constraint(rows, pltpu.HBM),
        pltpu.with_memory_space_constraint(group.reshape(1, cent), pltpu.HBM),
    )
    three, own, own_meta = pl.pallas_call(
        functools.partial(second_kernel, cent, [(0, half), (half, count)]),
        in_specs=[whole()] * 3,
        out_specs=[whole()] * 3,
        out_shape=[
            send,
            jax.ShapeDtypeStruct((pair, width), F32),
            jax.ShapeDtypeStruct((META, 2 * LANES), F32),
        ],
        cost_estimate=pl.CostEstimate(flops=100000000000, bytes_accessed=300000000, transcendentals=0),
        scratch_shapes=[pltpu.VMEM((2 * pair, width), F32)],
        compiler_params=small(),
    )(label, rows, digits)
    sends = [None] * GROUP
    for index, send in zip(ORDER, (one, two, three)):
        sends[index] = send
    return own, own_meta, *sends[1:]


def group_kernel(cent, four, three, one, two, own, own_meta, base_ref, base_meta_ref, next_ref, far_ref):
    mate = lax.axis_index("dp") % GROUP
    pair = 2 * cent
    lane = iota((1, LANES), 1)
    near = own[:cent]
    middle = own[cent:]
    far = jnp.zeros_like(near)
    counts = own_meta[0:1, :LANES] * BASE + own_meta[1:2, :LANES]
    far_counts = jnp.zeros_like(counts)
    id_digits = [own_meta[0:2, LANES:]]
    swapped = lax.axis_index("mp") % 2 == 1
    for index, got in ((1, one), (2, two), (3, three)):
        source = index if index == 3 else jnp.where(swapped, 3 - index, index)
        before = (mate ^ source) < mate
        first = got[:cent].astype(F32)
        near = near + jnp.where(before, first, 0.0)
        far = far + jnp.where(before, 0.0, first)
        middle = middle + got[cent:pair].astype(F32)
        meta = got[pair:, : 2 * LANES].astype(F32)
        row = meta[0:1, :LANES] * BASE + meta[1:2, :LANES]
        mask = (lane >= cent) | before
        counts = counts + jnp.where(mask, row, 0.0)
        far_counts = far_counts + jnp.where(mask, 0.0, row)
        id_digits.append(meta[0:2, LANES:])
    id_digits[1], id_digits[2] = (
        jnp.where(swapped, id_digits[2], id_digits[1]),
        jnp.where(swapped, id_digits[1], id_digits[2]),
    )
    id_digits = jnp.concatenate(id_digits, axis=0)

    def meta_of(row):
        high, low = split_digits(row)
        digits = jnp.concatenate([high, low, jnp.zeros((META - 2, LANES), F32)], axis=0)
        return jnp.concatenate([digits, id_digits], axis=1)

    if four:
        even = even_line()
        near, far = jnp.where(even, far, near), jnp.where(even, near, far)
        counts, far_counts = (
            jnp.where(even & (lane < cent), far_counts, counts),
            jnp.where(even, counts, far_counts),
        )
    base_ref[...] = near
    base_meta_ref[...] = meta_of(counts)
    for send, sums, row in ((next_ref, middle, counts), (far_ref, far, far_counts)):
        send[:cent] = sums.astype(BF16)
        send[cent:, : 2 * LANES] = meta_of(row).astype(BF16)
        send[cent:, 2 * LANES :] = jnp.zeros((META, send.shape[1] - 2 * LANES), BF16)


def group_sums(cent, four, own, own_meta, got):
    width = own.shape[1]
    send = jax.ShapeDtypeStruct((cent + META, width), BF16)
    return pl.pallas_call(
        functools.partial(group_kernel, cent, four),
        in_specs=[whole()] * 5,
        out_specs=[whole()] * 4,
        out_shape=[
            jax.ShapeDtypeStruct((cent, width), F32),
            jax.ShapeDtypeStruct((META, 2 * LANES), F32),
            send,
            send,
        ],
        compiler_params=small(),
    )(got[2], got[0], got[1], own, own_meta)


def mean_kernel(cent, two, one, base, base_meta, mean_ref, send_ref):
    sums = base[...] + one[:cent].astype(F32) + two[:cent].astype(F32)
    metas = [meta[...].astype(F32) for meta in (base_meta, one.at[cent:], two.at[cent:])]
    rows = [meta[0:1, :LANES] * BASE + meta[1:2, :LANES] for meta in metas]
    row = rows[0] + pltpu.roll(rows[1], LANES - cent, 1) + rows[2]
    mean = (sums / as_column(row, cent)).astype(BF16)
    mean_ref[...] = mean
    send_ref[:cent] = mean
    for index, meta in enumerate(metas):
        ids = meta[:, LANES : 2 * LANES].astype(BF16)
        send_ref[cent:, index * LANES : (index + 1) * LANES] = ids
    known = len(metas) * LANES
    send_ref[cent:, known:] = jnp.zeros((META, mean.shape[1] - known), BF16)


def means(cent, base, base_meta, got):
    width = base.shape[1]
    mean = jax.ShapeDtypeStruct((cent, width), BF16)
    return pl.pallas_call(
        functools.partial(mean_kernel, cent),
        in_specs=[whole()] * 4,
        out_specs=[whole()] * 2,
        out_shape=[mean, jax.ShapeDtypeStruct((cent + META, width), BF16)],
        compiler_params=small(),
    )(got[1], got[0], base, base_meta)


def near_kernel(cent, own, got, near_ref, ids_ref):
    near_ref[:cent] = own[:cent]
    near_ref[cent:] = got[:cent]
    even = even_line()
    lane = iota((1, LANES), 1)

    def ids_of(block, steps, index):
        meta = block[cent:, steps * LANES : (steps + 1) * LANES].astype(F32)
        at = 2 * index
        return meta[at : at + 1] * BASE + meta[at + 1 : at + 2]

    near_rows, far_rows = [], []
    for index in range(GROUP):
        here, one, two = (ids_of(own, steps, index) for steps in range(3))
        three = ids_of(got, 2, index)
        near_rows.append((jnp.where(even, two, here), jnp.where(even, one, three)))
        far_rows.append((jnp.where(even, here, two), jnp.where(even, three, one)))
    rows = [
        jnp.where(lane < cent, left, pltpu.roll(right, cent, 1))
        for left, right in near_rows + far_rows
    ]
    ids_ref[...] = jnp.concatenate(rows, axis=0).astype(jnp.int32)


def near_rows(cent, own, got):
    width = own.shape[1]
    return pl.pallas_call(
        functools.partial(near_kernel, cent),
        in_specs=[whole()] * 2,
        out_specs=[whole()] * 2,
        out_shape=[
            jax.ShapeDtypeStruct((2 * cent, width), BF16),
            jax.ShapeDtypeStruct((2 * GROUP, LANES), jnp.int32),
        ],
        compiler_params=small(),
    )(own, got)


def join_kernel(second, first, out_ref):
    rows = first.shape[0]
    out_ref[:rows] = first[...]
    out_ref[rows:] = second[...]


def joined(first, second):
    rows, width = first.shape
    return pl.pallas_call(
        join_kernel,
        in_specs=[whole()] * 2,
        out_specs=whole(),
        out_shape=jax.ShapeDtypeStruct((2 * rows, width), BF16),
        cost_estimate=pl.CostEstimate(flops=100000000000, bytes_accessed=300000000, transcendentals=0),
        compiler_params=small(),
    )(second, first)


def ids_row(ids, base, order):
    low = lax.axis_index("mp") == 0
    first = ids[base + order : base + order + 1]
    if order in (0, GROUP - 1):
        return first
    other = ids[base + GROUP - 1 - order : base + GROUP - order]
    return jnp.where(low, first, other)


def picked_ids(ids, pick):
    return ids_row(ids, pick // GROUP * GROUP, pick % GROUP)


def gathered(ids, picks, blocks, start, count):
    one_hots = [one_hot_of(count, picked_ids(ids, pick) - start) for pick in picks]
    total = None
    for at in range(0, len(picks), 2):
        one_hot = jnp.concatenate(one_hots[at : at + 2], axis=1)
        rows = jnp.concatenate([block[...] for block in blocks[at : at + 2]], axis=0)
        part = jnp.dot(one_hot, rows, preferred_element_type=F32)
        total = part if total is None else total + part
    return total


def gather_kernel(picks, *refs):
    blocks, refs = refs[:-8], refs[-8:]
    ids, mean, far, sums_ref, scale_ref, first_ref, first_hbm, sent = refs
    first_ref[...] = jnp.where(even_line(), far[: mean.shape[0]], mean[...])
    first_copy = pltpu.make_async_copy(first_ref, first_hbm, sent.at[0])
    first_copy.start()
    sums_ref[...] = gathered(ids, picks, blocks, 0, K2)
    tally = one_hot_of(K2, ids[0:1])
    for row in range(1, 2 * GROUP):
        tally = tally + one_hot_of(K2, ids[row : row + 1])
    count = jnp.sum(tally.astype(F32), axis=1, keepdims=True)
    scale_ref[...] = jnp.broadcast_to(1.0 / count, scale_ref.shape)
    first_copy.wait()


def gathered_sums(ids, mean, far, picks, blocks):
    cent, width = mean.shape
    return pl.pallas_call(
        functools.partial(gather_kernel, picks),
        in_specs=[whole()] * (3 + len(picks)),
        out_specs=[whole()] * 3 + [pl.BlockSpec(memory_space=pltpu.HBM)],
        out_shape=[
            jax.ShapeDtypeStruct((K2, width), F32),
            jax.ShapeDtypeStruct((K2, LANES), F32),
            jax.ShapeDtypeStruct((cent, width), BF16),
            jax.ShapeDtypeStruct((cent, width), BF16),
        ],
        scratch_shapes=[pltpu.SemaphoreType.DMA((1,))],
        compiler_params=small(),
    )(*[blocks[pick] for pick in picks], ids, mean, far)


def half_centroids(ids, picks, blocks, sums, scale, start):
    half = K2 // 2
    rows = pl.ds(pl.multiple_of(start, half), half)
    total = sums[rows] + gathered(ids, picks, blocks, start, half)
    factor = scale[rows]
    parts = [total[:, at : at + LANES] * factor for at in range(0, total.shape[1], LANES)]
    return jnp.concatenate(parts, axis=1).astype(BF16)


def scores_of(first, second):
    values = second.astype(F32)
    norms = 0.5 * jnp.sum(values * values, axis=1, keepdims=True)
    row = jnp.concatenate(
        [as_row(norms[at : at + LANES]) for at in range(0, second.shape[0], LANES)], axis=1
    )
    products = lax.dot_general(
        first, second, (((1,), (1,)), ((), ())), preferred_element_type=F32
    )
    return products - row


def send_kernel(picks, *refs):
    blocks, refs = refs[:-6], refs[-6:]
    ids, first, sums, scale, other_ref, send_ref = refs
    start = (1 - lax.axis_index("mp")) * (K2 // 2)
    second = half_centroids(ids, picks, blocks, sums, scale, start)
    other_ref[...] = second
    send_ref[...] = scores_of(first[...], second).astype(BF16)


def sent_scores(ids, first, sums, scale, picks, blocks):
    cent, width = first.shape
    half = K2 // 2
    return pl.pallas_call(
        functools.partial(send_kernel, picks),
        in_specs=[whole()] * (4 + len(picks)),
        out_specs=[whole()] * 2,
        out_shape=[
            jax.ShapeDtypeStruct((half, width), BF16),
            jax.ShapeDtypeStruct((cent, half), BF16),
        ],
        compiler_params=small(),
    )(*[blocks[pick] for pick in picks], ids, first, sums, scale)


def keep_kernel(owned, picks, *refs):
    blocks, refs = refs[:-10], refs[-10:]
    ids, first, sums, scale, other, second_hbm, keep_ref, every, second_ref, sent = refs
    half = K2 // 2
    core = lax.axis_index("mp")
    second = half_centroids(ids, picks, blocks, sums, scale, core * half)
    every[...] = second
    at = lax.axis_index("dp") * owned
    rows = pl.ds(pl.multiple_of(at % half, owned), owned)
    second_ref[...] = jnp.where(at // half == core, every[rows], other[rows])
    second_copy = pltpu.make_async_copy(second_ref, second_hbm, sent.at[0])
    second_copy.start()
    keep_ref[...] = scores_of(first[...], second)
    second_copy.wait()


def kept_scores(owned, ids, first, sums, scale, other, picks, blocks):
    cent, width = first.shape
    half = K2 // 2
    return pl.pallas_call(
        functools.partial(keep_kernel, owned, picks),
        in_specs=[whole()] * (5 + len(picks)),
        out_specs=[pl.BlockSpec(memory_space=pltpu.HBM), whole()],
        out_shape=[
            jax.ShapeDtypeStruct((owned, width), BF16),
            jax.ShapeDtypeStruct((cent, half), F32),
        ],
        scratch_shapes=[
            pltpu.VMEM((half, width), BF16),
            pltpu.VMEM((owned, width), BF16),
            pltpu.SemaphoreType.DMA((1,)),
        ],
        compiler_params=small(),
    )(*[blocks[pick] for pick in picks], ids, first, sums, scale, other)


def summed_scores(devices, second_level, first_centroids):
    second_ids = jnp.arange(K2, dtype=jnp.int32)
    group_hot = (second_level == second_ids[None, :]).astype(BF16)
    group_totals = jnp.einsum("ck,cd->kd", group_hot, first_centroids, preferred_element_type=F32)
    group_counts = jnp.sum(group_hot.astype(F32), axis=0)
    total, total_counts = lax.psum((group_totals, group_counts), "dp")
    every = (total / total_counts[:, None]).astype(BF16)
    owned = K2 // devices
    second = lax.dynamic_slice_in_dim(every, lax.axis_index("dp") * owned, owned, 0)
    values = every.astype(F32)
    products = jnp.einsum("cd,kd->ck", first_centroids, every, preferred_element_type=F32)
    partial_value = products - 0.5 * jnp.sum(values * values, axis=1)[None, :]
    scores = lax.psum_scatter(
        partial_value.astype(BF16), "mp", scatter_dimension=1, tiled=True
    ).astype(F32)
    return second, scores


def shards(embeddings, first_level, second_level):
    devices = lax.axis_size("dp")
    cores = lax.axis_size("mp")
    cent = second_level.shape[0]
    everyone = [(d, c) for d in range(devices) for c in range(cores)]

    def partner(value, index):
        return exchanged(value, [(d * cores + c, (d ^ index) * cores + c) for d, c in everyone])

    def sideways(value, steps):
        return exchanged(
            value, [(d * cores + c, (d ^ steps[c % 2]) * cores + c) for d, c in everyone]
        )

    def ahead(value, steps):
        return exchanged(
            value, [(d * cores + c, (d + steps) % devices * cores + c) for d, c in everyone]
        )

    own, own_meta, *sends = band_sums(devices, cent, first_level, embeddings, second_level)
    turns = ((1, 2), (2, 1), (3, 3))
    got = [None] * GROUP
    for index in ORDER[:-1]:
        got[index] = sideways(sends[index - 1], turns[index - 1])
    got = got[1:]
    four = devices == GROUP * GROUP and cores == 2 and devices * cent <= K2
    base, base_meta, following, far = group_sums(cent, four, own, own_meta, got)
    if four:
        got = [partner(following, GROUP), partner(far, 2 * GROUP)]
    else:
        got = [ahead(following, GROUP), ahead(far, 2 * GROUP)]
    mean, send = means(cent, base, base_meta, got)
    if not four:
        return (mean, *summed_scores(devices, second_level, mean))

    def plane_rows(value):
        return [value, sideways(value, (1, 2)), sideways(value, (2, 1)), partner(value, 3)]

    def relayed_rows(value):
        first = sideways(value, (1, 2))
        return [value, first, sideways(joined(value, first), (2, 1))]

    near, ids = near_rows(cent, send, partner(send, GROUP))
    far = joined(partner(mean, 2 * GROUP), partner(mean, 3 * GROUP))
    blocks = plane_rows(near) + plane_rows(far)
    sums, scale, first, first_out = gathered_sums(ids, mean, far, (0, 1, 2, 3, 4), blocks)
    other, send = sent_scores(ids, first, sums, scale, (5, 6, 7), blocks)
    got = exchanged(send, [(d * cores + c, d * cores + (c ^ 1)) for d, c in everyone])
    second, keep = kept_scores(K2 // devices, ids, first, sums, scale, other, (5, 6, 7), blocks)
    return first_out, second, keep + got.astype(F32)


def solution(mesh):
    placed = (P("dp", "mp"), P("dp"), P("dp", None))
    return jax.shard_map(
        shards,
        mesh=mesh,
        in_specs=placed,
        out_specs=(P("dp", "mp"), P("dp", "mp"), P("dp", "mp")),
        check_vma=False,
    )
```
